32 devices in a mesh: lat: 8 (over z, core), lon: 4 (over y, x).
Axes of the slice: x: 2, y: 2, z: 4, core: 2. Of those that a mesh axis runs over, the one named last changes fastest.
Arguments:
- spectra: float32 [64, 2, 360, 721], P('lat', None, 'lon'), may hold values from -0.03 to 0.03
- field_slot: int32 [64], replicated, may hold values from 0 to 63, each once
- field_weight: float32 [64], replicated, may hold values from 0.3 to 3
- latents: bfloat16 [64, 1440, 512], P('lat', 'lon'), may hold values from -6 to 6
- w_hidden: bfloat16 [512, 512], replicated, may hold values from -0.25 to 0.25
- b_hidden: float32 [512], replicated, may hold values from -3 to 3
- w_out: bfloat16 [512, 64], replicated, may hold values from -0.75 to 0.75
Outputs:
- latent_grad: bfloat16 [64, 1440, 512], P('lat', 'lon')
- hidden_grad: float32 [512, 512], replicated
- bias_grad: float32 [512], replicated
- out_grad: float32 [512, 64], replicated
The draws below stay inside these ranges and needn't reach their ends.
Inputs may be any that keep to these rules, and one draw needn't show every extreme that they name: Slot f of the spectra holds field field_slot[f]; every field stands in exactly one slot.
All inputs are finite; a program needn't handle non-finite values.
Results may differ from the reference program's by a relative error of at most 0.007.
Values sent between devices are 32-bit elements; how exact they have to be, the bound alone decides.
No kernel may reach another device: no remote copies, remote signals or barrier semaphores. Data moves between devices by JAX's collectives and lax.ppermute only.
A program may use at most 256 MiB of HBM per device.

```python
import math
import jax
import jax.numpy as jnp
from jax import lax

NM = 720
NLON = 1440
WIDTH = 512
F = 64
LAT_DEV = 8
NLATW = 64
NPAIR = 360
N_LAT = 8


def block_scale(stream_key, extent, shards, smallest, high):
    factor_of, own = 1.0, jax.random.fold_in(stream_key, 6)
    for position, shards_of in shards:
        heights = jnp.exp(jax.random.uniform(jax.random.fold_in(own, position), (shards_of,), jnp.float32, smallest / len(shards), high / len(shards)))
        factor_of = factor_of * jnp.repeat(heights, extent[position] // shards_of).reshape([-1 if axis == position else 1 for axis in range(len(extent))])
    return factor_of


def noise(key, extent, scale, limit, cuts=(), held_as=jnp.bfloat16):
    array = jax.random.normal(key, extent, jnp.float32) * scale
    if len(cuts) > 0:
        array = block_scale(key, extent, cuts, -0.22, 0.18) * array
    return jnp.clip(array, min=-limit, max=limit).astype(held_as)


def setup_inputs(seed: int = 0) -> dict:
    key_list = jax.random.split(jax.random.key(seed), 8)
    spectra = noise(key_list[0], (F, 2, NPAIR, NM + 1), 0.005, 0.03, ((0, 8), (2, 4)), jnp.float32)
    field_slot = jax.random.permutation(key_list[1], F).astype(jnp.int32)
    field_weight = jnp.clip(jnp.exp(jax.random.uniform(key_list[2], (F,), jnp.float32, math.log(0.3), math.log(3.0))), 0.3, 3.0)
    latents = noise(key_list[3], (NLATW, NLON, WIDTH), 1.0, 6.0, ((0, 8), (1, 4)))
    w_hidden = noise(key_list[4], (WIDTH, WIDTH), WIDTH ** -0.5, 0.25)
    b_hidden = noise(key_list[5], (WIDTH,), 0.5, 3.0, (), jnp.float32)
    w_out = noise(key_list[6], (WIDTH, F), F ** -0.5, 0.75)
    return {"spectra": spectra, "field_slot": field_slot, "field_weight": field_weight, "latents": latents, "w_hidden": w_hidden, "b_hidden": b_hidden, "w_out": w_out}


def band_angles(row_ids, rows_all):
    return jnp.pi * (NM // 2 - rows_all // 2 + row_ids.astype(jnp.float32)) / NM

def pair_layout(pair_ids):
    step_ids = jnp.arange(NM + 1, dtype=jnp.int32)[:, None]
    switch = (NM - pair_ids)[None, :]
    in_first = step_ids < switch
    order_ids = jnp.where(in_first, pair_ids[None, :], NM - 1 - pair_ids[None, :])
    degree_ids = jnp.where(in_first, pair_ids[None, :] + step_ids, step_ids - 1)
    restart = (step_ids == 0) | (step_ids == switch)
    return (in_first, order_ids, degree_ids, restart)

def legendre_table(pair_ids, colatitude):
    in_first, order_ids, degree_ids, restart = pair_layout(pair_ids)
    order_real = order_ids.astype(jnp.float32)
    degree_real = degree_ids.astype(jnp.float32)
    grow_coef = jnp.sqrt((4.0 * degree_real * degree_real - 1.0) / jnp.maximum(degree_real * degree_real - order_real * order_real, 1.0))
    lower_deg = degree_real - 1.0
    shrink_coef = jnp.sqrt(jnp.maximum(lower_deg * lower_deg - order_real * order_real, 0.0) / jnp.maximum(4.0 * lower_deg * lower_deg - 1.0, 1.0))
    term_ids = jnp.arange(1, NM, dtype=jnp.float32)
    log_terms = jnp.log((2.0 * term_ids + 1.0) / (2.0 * term_ids))
    log_sine = jnp.log(jnp.sin(colatitude))

    def seed_for(order_set):
        order_set_real = order_set.astype(jnp.float32)
        included = term_ids[None, :] <= order_set_real[:, None]
        log_total = lax.optimization_barrier(jnp.sum(jnp.where(included, log_terms[None, :], 0.0), axis=1))
        return jnp.exp(0.5 * log_total[:, None] - 0.5 * jnp.log(4.0 * jnp.pi) + order_set_real[:, None] * log_sine[None, :])
    seed_first = seed_for(pair_ids)
    seed_second = seed_for(NM - 1 - pair_ids)
    cosine = jnp.cos(colatitude)[None, :]

    def advance(state, step_inputs):
        previous, before_prev = state
        grow_step, shrink_step, restart_step, first_step = step_inputs
        seed_value = jnp.where(first_step[:, None], seed_first, seed_second)
        new_value = jnp.where(restart_step[:, None], seed_value, grow_step[:, None] * (cosine * previous - shrink_step[:, None] * before_prev))
        return ((new_value, previous), new_value)
    zero_state = jnp.zeros((pair_ids.shape[0], colatitude.shape[0]), jnp.float32)
    unused_state, legendre = lax.scan(advance, (zero_state, zero_state), (grow_coef, shrink_coef, restart, in_first))
    return legendre

def spectral_coefficients(spectra, pair_ids, colatitude):
    legendre = legendre_table(pair_ids, colatitude)
    lower_half = jnp.transpose(pair_layout(pair_ids)[0]).astype(jnp.float32)
    halves = []
    for selector in (lower_half, 1.0 - lower_half):
        halves.append(jnp.einsum('fcpk,kpi->fcpi', spectra * selector, legendre, precision=lax.Precision.HIGHEST))
    return jnp.stack(halves, axis=3).astype(jnp.bfloat16)

def trig_table(pair_ids):
    order_ids = jnp.stack([pair_ids, NM - 1 - pair_ids], axis=1)
    column_ids = jnp.arange(NLON, dtype=jnp.int32)
    phase_ids = order_ids[:, :, None] * column_ids[None, None, :] % NLON
    phase = phase_ids.astype(jnp.float32) * (2.0 * jnp.pi / NLON)
    return jnp.stack([jnp.cos(phase), jnp.sin(phase)], axis=0).astype(jnp.bfloat16)

def reference(spectra, field_slot, field_weight, latents, w_hidden, b_hidden, w_out):
    rows_all = LAT_DEV * N_LAT
    colatitude = band_angles(jnp.arange(rows_all, dtype=jnp.int32), rows_all)
    pair_ids = jnp.arange(NM // 2, dtype=jnp.int32)
    coeffs = spectral_coefficients(spectra, pair_ids, colatitude)
    trig = trig_table(pair_ids)
    grid_field = jnp.einsum('fcphi,cphj->fij', coeffs.astype(jnp.float32), trig.astype(jnp.float32), precision=lax.Precision.HIGHEST)
    slot_weight = field_weight[field_slot]
    scaled = (grid_field * jnp.sin(colatitude)[None, :, None] * slot_weight[:, None, None]).astype(jnp.bfloat16)
    ordered = jnp.zeros_like(scaled).at[field_slot].set(scaled)
    field_cells = jnp.transpose(ordered, (1, 2, 0)).reshape(N_LAT, LAT_DEV * NLON, F)
    latent_blocks = latents.reshape(N_LAT, LAT_DEV * NLON, WIDTH)

    def decode_block(running, block):
        latent_rows, field_grad = block
        preact = jnp.dot(latent_rows, w_hidden, preferred_element_type=jnp.float32) + b_hidden
        hidden = jax.nn.gelu(preact).astype(jnp.bfloat16)
        out_part = jnp.dot(hidden.T, field_grad, preferred_element_type=jnp.float32)
        hidden_back = jnp.dot(field_grad, w_out.T, preferred_element_type=jnp.float32)
        unused_out, pullback = jax.vjp(jax.nn.gelu, preact)
        preact_back = pullback(hidden_back)[0].astype(jnp.bfloat16)
        hidden_part = jnp.dot(latent_rows.T, preact_back, preferred_element_type=jnp.float32)
        bias_part = lax.optimization_barrier(jnp.sum(preact_back.astype(jnp.float32), axis=0))
        latent_part = jnp.dot(preact_back, w_hidden.T, preferred_element_type=jnp.float32).astype(jnp.bfloat16)
        return ((running[0] + hidden_part, running[1] + bias_part, running[2] + out_part), latent_part)
    start_sums = (jnp.zeros((WIDTH, WIDTH), jnp.float32), jnp.zeros((WIDTH,), jnp.float32), jnp.zeros((WIDTH, F), jnp.float32))
    sums, latent_parts = lax.scan(decode_block, start_sums, (latent_blocks, field_cells))
    norm_factor = math.sqrt(rows_all * NLON)
    latent_grad = latent_parts.reshape(rows_all, NLON, WIDTH)
    return (latent_grad, sums[0] / norm_factor, sums[1] / norm_factor, sums[2] / norm_factor)
```

```python
import functools
import math

import jax
import jax.numpy as jnp
from jax import lax
from jax.experimental import pallas as pl
from jax.experimental.pallas import tpu as pltpu
from jax.sharding import PartitionSpec as P

NM = 720
NLON = 1440
F = 64
LANES = 128
SUBS = 8
STEPS = NM + 1
TABLE_ROWS = 728
VMEM_LIMIT = 56 * 1024 * 1024


def band_angles(row_ids, rows_all):
    return jnp.pi * (NM // 2 - rows_all // 2 + row_ids.astype(jnp.float32)) / NM


def pad_to(value, multiple):
    return (value + multiple - 1) // multiple * multiple


def coeff_kernel(
    first_ref, spectra_hbm, out_ref, spectra_ref, grow_ref, shrink_ref, table_ref, stage_ref,
    copy_sem, *, pair_count, rows_all, lat_rows, slot_count,
):
    per_block = LANES // rows_all
    vregs = pad_to(pair_count, SUBS * per_block) // (SUBS * per_block)
    step_tile = rows_all
    tile_total = pad_to(STEPS, step_tile) // step_tile
    pair_pad = pad_to(pair_count, SUBS)
    lat_count = rows_all // lat_rows
    first_pair = first_ref[0]

    fetch = pltpu.make_async_copy(spectra_hbm, spectra_ref, copy_sem)
    fetch.start()

    lane = lax.broadcasted_iota(jnp.int32, (SUBS, LANES), 1)
    sub = lax.broadcasted_iota(jnp.int32, (SUBS, LANES), 0)
    inner = lane & (rows_all - 1)
    which = lane // rows_all
    colatitude = band_angles(inner, rows_all)
    cosine = jnp.cos(colatitude)
    log_sine = jnp.log(jnp.sin(colatitude))

    def log_total(order_column):
        total = jnp.zeros((SUBS, LANES), jnp.float32)
        for tile in range(pad_to(NM, LANES) // LANES):
            term = (lane + tile * LANES).astype(jnp.float32)
            safe = jnp.maximum(term, 1.0)
            value = jnp.log((2.0 * safe + 1.0) / (2.0 * safe))
            total = total + jnp.where((term >= 1.0) & (term <= order_column), value, 0.0)
        return jnp.sum(total, axis=1, keepdims=True)

    def seed(order_of):
        total = jnp.zeros((SUBS, LANES), jnp.float32)
        for part in range(per_block):
            column = order_of(part).astype(jnp.float32)
            total = jnp.where(which == part, log_total(column), total)
        order = order_of(which).astype(jnp.float32)
        return jnp.exp(0.5 * total - 0.5 * math.log(4.0 * math.pi) + order * log_sine)

    firsts, seconds, switches = [], [], []
    for v in range(vregs):
        base = first_pair + (sub + v * SUBS) * per_block

        def order_first(part, base=base):
            return base + part

        def order_second(part, base=base):
            return NM - 1 - (base + part)

        firsts.append(seed(order_first))
        seconds.append(seed(order_second))
        pair = base + which
        switch = NM - pair
        switches.append(switch)
        for tile in range(tile_total):
            step = inner + tile * step_tile
            in_first = step < switch
            order = jnp.where(in_first, pair, NM - 1 - pair).astype(jnp.float32)
            degree = jnp.where(in_first, pair + step, step - 1).astype(jnp.float32)
            lower = degree - 1.0
            grow = jnp.sqrt(
                (4.0 * degree * degree - 1.0) / jnp.maximum(degree * degree - order * order, 1.0)
            )
            shrink = jnp.sqrt(
                jnp.maximum(lower * lower - order * order, 0.0)
                / jnp.maximum(4.0 * lower * lower - 1.0, 1.0)
            )
            start = step == 0
            grow_ref[tile, pl.ds(v * SUBS, SUBS), :] = jnp.where(start, 1.0, grow)
            shrink_ref[tile, pl.ds(v * SUBS, SUBS), :] = jnp.where(start, -1.0, shrink)

    def advance(tile, offset, state, grows, shrinks):
        previous, before = state
        index = which * rows_all + offset
        step = tile * step_tile + offset
        produced = []
        for v in range(vregs):
            grow = jnp.take_along_axis(grows[v], index, axis=1)
            shrink = jnp.take_along_axis(shrinks[v], index, axis=1)
            value = grow * (cosine * previous[v] - shrink * before[v])
            value = jnp.where(switches[v] == step, seconds[v], value)
            table_ref[pl.ds(v * SUBS * TABLE_ROWS + step, SUBS, stride=TABLE_ROWS), :] = value
            produced.append(value)
        return (tuple(produced), previous)

    def run_tile(tile, state, count, unroll):
        grows = [grow_ref[tile, pl.ds(v * SUBS, SUBS), :] for v in range(vregs)]
        shrinks = [shrink_ref[tile, pl.ds(v * SUBS, SUBS), :] for v in range(vregs)]

        def body(offset, carry):
            return advance(tile, offset, carry, grows, shrinks)

        return lax.fori_loop(0, count, body, state, unroll=unroll)

    zeros = tuple(jnp.zeros((SUBS, LANES), jnp.float32) for _ in range(vregs))
    state = (zeros, tuple(firsts))
    whole_tiles = STEPS // step_tile
    state = lax.fori_loop(
        0, whole_tiles, lambda tile, carry: run_tile(tile, carry, step_tile, 8), state
    )
    if STEPS % step_tile:
        run_tile(whole_tiles, state, STEPS % step_tile, STEPS % step_tile % 16)

    for row in range(slot_count):
        for part in range(4):
            stage_ref[row, pl.ds(part * pair_pad + pair_pad - SUBS, SUBS), :] = jnp.zeros(
                (SUBS, LANES), jnp.float32
            )
    fetch.wait()

    split = 256
    rows_half = 2 * slot_count * SUBS

    def split_parts(values):
        high = values.astype(jnp.bfloat16)
        low = (values - high.astype(jnp.float32)).astype(jnp.bfloat16)
        return high, low

    def product(left, right):
        left_high, left_low = left
        right_high, right_low = right
        dot = functools.partial(jnp.dot, preferred_element_type=jnp.float32)
        return (
            dot(left_high, right_high) + dot(left_low, right_high) + dot(left_high, right_low)
        )

    def group(start):
        values = spectra_ref[:, pl.ds(start, SUBS), :]
        step = lax.broadcasted_iota(jnp.int32, (1, SUBS, STEPS), 2)
        pair = first_pair + start + lax.broadcasted_iota(jnp.int32, (1, SUBS, STEPS), 1)
        in_first = step < NM - pair
        early = values[:, :, :split].reshape(rows_half, split)
        late = jnp.concatenate(
            [jnp.where(in_first, values, 0.0), jnp.where(in_first, 0.0, values)], axis=0
        )[:, :, split:].reshape(2 * rows_half, STEPS - split)
        early, late = split_parts(early), split_parts(late)
        total = jnp.zeros((2 * rows_half, LANES), jnp.float32)
        row_pair = lax.broadcasted_iota(jnp.int32, (2 * rows_half, LANES), 0) & (SUBS - 1)
        lane_part = lax.broadcasted_iota(jnp.int32, (2 * rows_half, LANES), 1) // rows_all
        first_block = start // per_block
        for block in range(0, SUBS // per_block, 2):
            tables = [
                table_ref[pl.ds((first_block + block + n) * TABLE_ROWS, STEPS), :]
                for n in range(2)
            ]
            table = jnp.concatenate(tables, axis=1)
            top = product(early, split_parts(table[:split]))
            bottom = product(late, split_parts(table[split:]))
            both = jnp.concatenate([bottom[:rows_half] + top, bottom[rows_half:]], axis=0)
            for n in range(2):
                keep = row_pair == (block + n) * per_block + lane_part
                total = total + jnp.where(keep, both[:, n * LANES : (n + 1) * LANES], 0.0)
        for part in range(1, per_block):
            total = total + pltpu.roll(total, LANES - part * rows_all, 1) if part == 1 else total
        total = total.astype(jnp.bfloat16).astype(jnp.float32)
        for half in range(2):
            for row in range(slot_count):
                for trig in range(2):
                    source = ((half * slot_count + row) * 2 + trig) * SUBS
                    target = (half * 2 + trig) * pair_pad + start
                    stage_ref[row, pl.ds(target, SUBS), :] = total[source : source + SUBS]

    def group_body(index, carry):
        group(pl.multiple_of(index * SUBS, SUBS))
        return carry

    lax.fori_loop(0, pair_count // SUBS, group_body, 0)
    if pair_count % SUBS:
        group(pair_count - SUBS)

    for row in range(slot_count):
        flipped = stage_ref[row].T
        out_ref[:, pl.ds(row * lat_rows, lat_rows), :] = flipped[:rows_all].reshape(
            lat_count, lat_rows, 4 * pair_pad
        )


def coefficients(spectra, first_pair, rows_all, lat_rows):
    slot_count, _, pair_count, steps = spectra.shape
    per_block = LANES // rows_all
    vregs = pad_to(pair_count, SUBS * per_block) // (SUBS * per_block)
    tile_total = pad_to(STEPS, rows_all) // rows_all
    pair_pad = pad_to(pair_count, SUBS)
    lat_count = rows_all // lat_rows
    kernel = functools.partial(
        coeff_kernel, pair_count=pair_count, rows_all=rows_all, lat_rows=lat_rows,
        slot_count=slot_count,
    )
    return pl.pallas_call(
        kernel,
        out_shape=jax.ShapeDtypeStruct(
            (lat_count, slot_count * lat_rows, 4 * pair_pad), jnp.float32
        ),
        in_specs=[
            pl.BlockSpec(memory_space=pltpu.SMEM),
            pl.BlockSpec(memory_space=pl.ANY),
        ],
        out_specs=pl.BlockSpec(memory_space=pltpu.VMEM),
        scratch_shapes=[
            pltpu.VMEM((2 * slot_count, pair_count, steps), jnp.float32),
            pltpu.VMEM((tile_total, vregs * SUBS, LANES), jnp.float32),
            pltpu.VMEM((tile_total, vregs * SUBS, LANES), jnp.float32),
            pltpu.VMEM((vregs * SUBS * TABLE_ROWS, LANES), jnp.float32),
            pltpu.VMEM((slot_count, 4 * pair_pad, LANES), jnp.float32),
            pltpu.SemaphoreType.DMA,
        ],
        compiler_params=pltpu.CompilerParams(vmem_limit_bytes=VMEM_LIMIT),
        name="coefficients",
    )(first_pair, spectra.reshape(2 * slot_count, pair_count, steps))


def grid_kernel(trig_ref, coeff_ref, out_ref, *, lon_count):
    rows = coeff_ref.shape[0] // lon_count * coeff_ref.shape[1]
    width = coeff_ref.shape[2]
    values = coeff_ref[...].reshape(rows // coeff_ref.shape[1], lon_count, coeff_ref.shape[1], width)
    total = None
    for block in range(lon_count):
        right = values[:, block].reshape(rows, width).astype(jnp.bfloat16)
        part = lax.dot_general(
            trig_ref[block], right, (((1,), (1,)), ((), ())), preferred_element_type=jnp.float32
        )
        total = part if total is None else total + part
    out_ref[...] = total


def grid_field(trig, coeffs, lon_count, lon_cols):
    lat_count = coeffs.shape[0] // lon_count
    rows = lat_count * coeffs.shape[1]
    width = trig.shape[3]
    return pl.pallas_call(
        functools.partial(grid_kernel, lon_count=lon_count),
        grid=(lon_count,),
        out_shape=jax.ShapeDtypeStruct((lon_count, lon_cols, rows), jnp.float32),
        in_specs=[
            pl.BlockSpec((None, lon_count, lon_cols, width), lambda j: (j, 0, 0, 0)),
            pl.BlockSpec(coeffs.shape, lambda j: (0, 0, 0)),
        ],
        out_specs=pl.BlockSpec((None, lon_cols, rows), lambda j: (j, 0, 0)),
        compiler_params=pltpu.CompilerParams(vmem_limit_bytes=VMEM_LIMIT),
        cost_estimate=pl.CostEstimate(
            flops=2 * NLON * lon_count * width * rows,
            bytes_accessed=trig.size * 2 + 2 * coeffs.size * 4,
            transcendentals=0,
        ),
        name="grid_field",
    )(trig, coeffs)


def trig_table(pair_count, lon_count, lon_cols):
    pair_pad = pad_to(pair_count, SUBS)
    block_ids = jnp.arange(lon_count, dtype=jnp.int32)[:, None, None, None]
    half_ids = jnp.arange(2, dtype=jnp.int32)[None, :, None, None]
    part_ids = jnp.arange(2, dtype=jnp.int32)[None, None, :, None]
    pair_ids = block_ids * pair_count + jnp.arange(pair_pad, dtype=jnp.int32)
    order = jnp.where(half_ids == 0, pair_ids, NM - 1 - pair_ids) + 0 * part_ids
    order = order.reshape(lon_count, 4 * pair_pad)
    is_sine = jnp.broadcast_to(part_ids, (lon_count, 2, 2, pair_pad)).reshape(lon_count, -1) == 1

    def angles(column_ids):
        phase_ids = order[:, None, :] * column_ids[None, :, None] % NLON
        phase = phase_ids.astype(jnp.float32) * (2.0 * jnp.pi / NLON)
        return jnp.cos(phase), jnp.sin(phase)

    fine_total = 20
    fine_cos, fine_sin = angles(jnp.arange(fine_total, dtype=jnp.int32))
    coarse_cos, coarse_sin = angles(jnp.arange(0, NLON, fine_total, dtype=jnp.int32))
    left = jnp.where(is_sine[:, None, :], coarse_sin, coarse_cos)
    right = jnp.where(is_sine[:, None, :], coarse_cos, -coarse_sin)
    table = left[:, :, None, :] * fine_cos[:, None] + right[:, :, None, :] * fine_sin[:, None]
    table = table.astype(jnp.bfloat16)
    table = table.reshape(lon_count, lon_count, lon_cols, 4 * pair_pad)
    return jnp.transpose(table, (1, 0, 2, 3))


def gelu_parts(preact):
    scale = math.sqrt(2.0 / math.pi)
    square = preact * preact
    bend = jnp.tanh(scale * (preact + 0.044715 * (square * preact)))
    half = 0.5 * (1.0 + bend)
    slope = half + (0.5 * preact) * (1.0 - bend * bend) * (
        scale * (1.0 + (3.0 * 0.044715) * square)
    )
    return preact * half, slope


def forward_kernel(latents_ref, w_ref, b_ref, slope_ref, hidden_t_ref, latents_t_ref):
    latents = latents_ref[...]
    preact = jnp.dot(latents, w_ref[...], preferred_element_type=jnp.float32) + b_ref[...]
    hidden, slope = gelu_parts(preact)
    slope_ref[...] = slope
    hidden_t_ref[...] = hidden.T.astype(jnp.bfloat16)
    latents_t_ref[...] = latents.T


def forward(latents, w_hidden, b_hidden):
    rows, cols, width = latents.shape
    cells = rows * cols
    return pl.pallas_call(
        forward_kernel,
        grid=(rows,),
        out_shape=(
            jax.ShapeDtypeStruct((rows, cols, width), jnp.float32),
            jax.ShapeDtypeStruct((rows, width, cols), jnp.bfloat16),
            jax.ShapeDtypeStruct((rows, width, cols), jnp.bfloat16),
        ),
        in_specs=[
            pl.BlockSpec((None, cols, width), lambda i: (i, 0, 0)),
            pl.BlockSpec((width, width), lambda i: (0, 0)),
            pl.BlockSpec((1, width), lambda i: (0, 0)),
        ],
        out_specs=(
            pl.BlockSpec((None, cols, width), lambda i: (i, 0, 0)),
            pl.BlockSpec((None, width, cols), lambda i: (i, 0, 0)),
            pl.BlockSpec((None, width, cols), lambda i: (i, 0, 0)),
        ),
        compiler_params=pltpu.CompilerParams(vmem_limit_bytes=VMEM_LIMIT),
        cost_estimate=pl.CostEstimate(
            flops=2 * cells * width * width,
            bytes_accessed=cells * width * 10,
            transcendentals=cells * width,
        ),
        name="forward",
    )(latents, w_hidden, b_hidden.reshape(1, width))


def backward_kernel(
    grid_ref, scale_ref, place_ref, w_out_ref, slope_ref, hidden_t_ref, latents_t_ref,
    preact_ref, sums_ref, field_ref, hidden_acc, out_acc, bias_acc, *, sum_rows,
):
    index = pl.program_id(0)
    total = pl.num_programs(0)
    blocks = grid_ref.shape[0]
    rows = field_ref.shape[0]
    width = hidden_acc.shape[0]

    @pl.when(index == 0)
    def _():
        field = None
        for block in range(blocks):
            scaled = (grid_ref[block] * scale_ref[block]).astype(jnp.bfloat16)
            part = jnp.dot(scaled, place_ref[block], preferred_element_type=jnp.float32)
            field = part if field is None else field + part
        field = field.astype(jnp.bfloat16)
        for row in range(rows):
            field_ref[row] = field[:, row * LANES : (row + 1) * LANES]
        hidden_acc[...] = jnp.zeros_like(hidden_acc)
        out_acc[...] = jnp.zeros_like(out_acc)
        bias_acc[...] = jnp.zeros_like(bias_acc)

    field = field_ref[index]
    back = jnp.dot(field, w_out_ref[...], preferred_element_type=jnp.float32)
    preact_back = (back * slope_ref[...]).astype(jnp.bfloat16)
    preact_ref[...] = preact_back
    hidden_acc[...] += jnp.dot(
        latents_t_ref[...], preact_back, preferred_element_type=jnp.float32
    )
    out_acc[...] += jnp.dot(hidden_t_ref[...], field, preferred_element_type=jnp.float32)
    bias_acc[...] += jnp.sum(preact_back.astype(jnp.float32), axis=0, keepdims=True)

    @pl.when(index == total - 1)
    def _():
        tiles = width // LANES
        for row_tile in range(width // SUBS):
            for tile in range(tiles):
                sums_ref[pl.ds((row_tile * tiles + tile) * SUBS, SUBS), :] = hidden_acc[
                    pl.ds(row_tile * SUBS, SUBS), pl.ds(tile * LANES, LANES)
                ]
        base = width * tiles
        flipped = out_acc[...].T
        for tile in range(tiles):
            sums_ref[pl.ds(base + tile * F, F), :] = flipped[:F, tile * LANES : (tile + 1) * LANES]
        base = base + tiles * F
        sums_ref[pl.ds(base, sum_rows - base), :] = jnp.zeros((sum_rows - base, LANES), jnp.float32)
        for tile in range(tiles):
            sums_ref[pl.ds(base + tile, 1), :] = bias_acc[:, tile * LANES : (tile + 1) * LANES]


def backward(grid, scale, place, w_out_t, slope, hidden_t, latents_t, sum_rows):
    rows, cols, width = slope.shape
    blocks, _, lanes = grid.shape
    cells = rows * cols
    return pl.pallas_call(
        functools.partial(backward_kernel, sum_rows=sum_rows),
        grid=(rows,),
        out_shape=(
            jax.ShapeDtypeStruct((rows, cols, width), jnp.bfloat16),
            jax.ShapeDtypeStruct((sum_rows, LANES), jnp.float32),
        ),
        in_specs=[
            pl.BlockSpec(grid.shape, lambda i: (0, 0, 0)),
            pl.BlockSpec(scale.shape, lambda i: (0, 0, 0)),
            pl.BlockSpec(place.shape, lambda i: (0, 0, 0)),
            pl.BlockSpec(w_out_t.shape, lambda i: (0, 0)),
            pl.BlockSpec((None, cols, width), lambda i: (i, 0, 0)),
            pl.BlockSpec((None, width, cols), lambda i: (i, 0, 0)),
            pl.BlockSpec((None, width, cols), lambda i: (i, 0, 0)),
        ],
        out_specs=(
            pl.BlockSpec((None, cols, width), lambda i: (i, 0, 0)),
            pl.BlockSpec((sum_rows, LANES), lambda i: (0, 0)),
        ),
        scratch_shapes=[
            pltpu.VMEM((rows, cols, LANES), jnp.bfloat16),
            pltpu.VMEM((width, width), jnp.float32),
            pltpu.VMEM((width, LANES), jnp.float32),
            pltpu.VMEM((1, width), jnp.float32),
        ],
        compiler_params=pltpu.CompilerParams(vmem_limit_bytes=VMEM_LIMIT),
        cost_estimate=pl.CostEstimate(
            flops=2 * cells * width * (width + 2 * LANES),
            bytes_accessed=cells * width * 10,
            transcendentals=0,
        ),
        name="backward",
    )(grid, scale, place, w_out_t, slope, hidden_t, latents_t)


def local(spectra, field_slot, field_weight, latents, w_hidden, b_hidden, w_out):
    slot_count, _, pair_count, _ = spectra.shape
    lat_rows, lon_cols, width = latents.shape
    lat_count = lax.axis_size("lat")
    lon_count = lax.axis_size("lon")
    rows_all = lat_rows * lat_count
    lat_index = lax.axis_index("lat")
    lon_index = lax.axis_index("lon")
    pair_pad = pad_to(pair_count, SUBS)

    first_pair = (lon_index * pair_count).astype(jnp.int32).reshape(1)
    coeffs = coefficients(spectra, first_pair, rows_all, lat_rows)
    share = slot_count * lat_rows // lon_count
    coeffs = coeffs.reshape(lat_count * lon_count, share, 4 * pair_pad)
    coeffs = lax.all_to_all(coeffs, ("lat", "lon"), split_axis=0, concat_axis=0, tiled=True)

    slope, hidden_t, latents_t = forward(latents, w_hidden, b_hidden)
    trig = trig_table(pair_count, lon_count, lon_cols)

    lanes = lat_count * share
    lane_ids = jnp.arange(lanes, dtype=jnp.int32)[None, :]
    block_ids = jnp.arange(lon_count, dtype=jnp.int32)[:, None]
    line = block_ids * share + lane_ids % share
    slot_ids = (lane_ids // share) * slot_count + line // lat_rows
    row_ids = line % lat_rows
    field_ids = field_slot[slot_ids]
    sine = jnp.sin(band_angles(lat_index * lat_rows + row_ids, rows_all))
    scale = (sine * field_weight[field_ids])[:, None, :]
    target = row_ids * LANES + field_ids
    place = (
        target[:, :, None] == jnp.arange(lat_rows * LANES, dtype=jnp.int32)[None, None, :]
    ).astype(jnp.bfloat16)
    w_out_t = jnp.concatenate([w_out.T, jnp.zeros((LANES - F, width), w_out.dtype)], axis=0)

    grid = grid_field(trig, coeffs, lon_count, lon_cols)
    grid = lax.all_to_all(grid, "lon", split_axis=0, concat_axis=0, tiled=True)

    device_count = lat_count * lon_count
    used_rows = width * width // LANES + F * width // LANES + width // LANES
    chunk = pad_to(pad_to(used_rows, device_count) // device_count, SUBS)
    sum_rows = chunk * device_count
    preact_back, sums = backward(
        grid, scale, place, w_out_t, slope, hidden_t, latents_t, sum_rows
    )
    latent_grad = lax.dot_general(
        preact_back, w_hidden, (((2,), (1,)), ((), ())), preferred_element_type=jnp.float32
    ).astype(jnp.bfloat16)

    sums = sums.reshape(lon_count, lat_count * chunk, LANES)
    sums = lax.all_to_all(sums, "lon", split_axis=0, concat_axis=0, tiled=True)
    sums = jnp.sum(sums, axis=0).reshape(lat_count, chunk, LANES)
    sums = lax.all_to_all(sums, "lat", split_axis=0, concat_axis=0, tiled=True)
    sums = jnp.sum(sums, axis=0) / math.sqrt(rows_all * NLON)
    sums = jnp.broadcast_to(sums[None], (lat_count, chunk, LANES))
    sums = lax.all_to_all(sums, "lat", split_axis=0, concat_axis=0, tiled=True)
    sums = jnp.broadcast_to(sums.reshape(1, lat_count * chunk, LANES), (lon_count, lat_count * chunk, LANES))
    sums = lax.all_to_all(sums, "lon", split_axis=0, concat_axis=0, tiled=True)
    sums = sums.reshape(sum_rows, LANES)

    tiles = width // LANES
    hidden_rows = width * tiles
    out_rows = F * tiles
    hidden_grad = (
        sums[:hidden_rows]
        .reshape(width // SUBS, tiles, SUBS, LANES)
        .transpose(0, 2, 1, 3)
        .reshape(width, width)
    )
    out_grad = (
        sums[hidden_rows : hidden_rows + out_rows]
        .reshape(tiles, F, LANES)
        .transpose(0, 2, 1)
        .reshape(width, F)
    )
    bias_grad = sums[hidden_rows + out_rows : hidden_rows + out_rows + tiles].reshape(width)
    return (latent_grad, hidden_grad, bias_grad, out_grad)


def solution(mesh):
    in_specs = (P("lat", None, "lon", None), P(), P(), P("lat", "lon", None), P(), P(), P())
    out_specs = (P("lat", "lon", None), P(), P(), P())
    return jax.shard_map(local, mesh=mesh, in_specs=in_specs, out_specs=out_specs, check_vma=False)
```

```python
import functools
import math

import jax
import jax.numpy as jnp
from jax import lax
from jax.experimental import pallas as pl
from jax.experimental.pallas import tpu as pltpu
from jax.sharding import PartitionSpec as P

NM = 720
NLON = 1440
F = 64
LANES = 128
SUBS = 8
STEPS = NM + 1
PAIRS = 4
TABLE_ROWS = 728
VMEM_LIMIT = 56 * 1024 * 1024


def band_angles(row_ids, rows_all):
    return jnp.pi * (NM // 2 - rows_all // 2 + row_ids.astype(jnp.float32)) / NM


def pad_to(value, multiple):
    return (value + multiple - 1) // multiple * multiple


def coeff_kernel(
    first_ref, spectra_hbm, out_ref, spectra_ref, grow_ref, shrink_ref, table_ref, stage_ref,
    copy_sem, *, pair_count, rows_all, lat_rows, slot_count,
):
    per_block = LANES // rows_all
    vregs = pad_to(pair_count, SUBS * per_block) // (SUBS * per_block)
    step_tile = rows_all
    tile_total = pad_to(STEPS, step_tile) // step_tile
    pair_pad = pad_to(pair_count, SUBS)
    lat_count = rows_all // lat_rows
    first_pair = first_ref[0]

    fetch = pltpu.make_async_copy(spectra_hbm, spectra_ref, copy_sem)
    fetch.start()

    lane = lax.broadcasted_iota(jnp.int32, (SUBS, LANES), 1)
    sub = lax.broadcasted_iota(jnp.int32, (SUBS, LANES), 0)
    inner = lane & (rows_all - 1)
    which = lane // rows_all
    colatitude = band_angles(inner, rows_all)
    cosine = jnp.cos(colatitude)
    log_sine = jnp.log(jnp.sin(colatitude))

    def log_total(order_column):
        total = jnp.zeros((SUBS, LANES), jnp.float32)
        for tile in range(pad_to(NM, LANES) // LANES):
            term = (lane + tile * LANES).astype(jnp.float32)
            safe = jnp.maximum(term, 1.0)
            value = jnp.log((2.0 * safe + 1.0) / (2.0 * safe))
            total = total + jnp.where((term >= 1.0) & (term <= order_column), value, 0.0)
        return jnp.sum(total, axis=1, keepdims=True)

    def seed(order_of):
        total = jnp.zeros((SUBS, LANES), jnp.float32)
        for part in range(per_block):
            column = order_of(part).astype(jnp.float32)
            total = jnp.where(which == part, log_total(column), total)
        order = order_of(which).astype(jnp.float32)
        return jnp.exp(0.5 * total - 0.5 * math.log(4.0 * math.pi) + order * log_sine)

    firsts, seconds, switches = [], [], []
    for v in range(vregs):
        base = first_pair + (sub + v * SUBS) * per_block

        def order_first(part, base=base):
            return base + part

        def order_second(part, base=base):
            return NM - 1 - (base + part)

        firsts.append(seed(order_first))
        seconds.append(seed(order_second))
        pair = base + which
        switch = NM - pair
        switches.append(switch)
        for tile in range(tile_total):
            step = inner + tile * step_tile
            in_first = step < switch
            order = jnp.where(in_first, pair, NM - 1 - pair).astype(jnp.float32)
            degree = jnp.where(in_first, pair + step, step - 1).astype(jnp.float32)
            lower = degree - 1.0
            grow = jnp.sqrt(
                (4.0 * degree * degree - 1.0) / jnp.maximum(degree * degree - order * order, 1.0)
            )
            shrink = jnp.sqrt(
                jnp.maximum(lower * lower - order * order, 0.0)
                / jnp.maximum(4.0 * lower * lower - 1.0, 1.0)
            )
            start = step == 0
            grow_ref[tile, pl.ds(v * SUBS, SUBS), :] = jnp.where(start, 1.0, grow)
            shrink_ref[tile, pl.ds(v * SUBS, SUBS), :] = jnp.where(start, -1.0, shrink)

    def advance(tile, offset, state, grows, shrinks):
        previous, before = state
        index = which * rows_all + offset
        step = tile * step_tile + offset
        produced = []
        for v in range(vregs):
            grow = jnp.take_along_axis(grows[v], index, axis=1)
            shrink = jnp.take_along_axis(shrinks[v], index, axis=1)
            value = grow * (cosine * previous[v] - shrink * before[v])
            value = jnp.where(switches[v] == step, seconds[v], value)
            table_ref[pl.ds(v * SUBS * TABLE_ROWS + step, SUBS, stride=TABLE_ROWS), :] = value
            produced.append(value)
        return (tuple(produced), previous)

    def run_tile(tile, state, count, unroll):
        grows = [grow_ref[tile, pl.ds(v * SUBS, SUBS), :] for v in range(vregs)]
        shrinks = [shrink_ref[tile, pl.ds(v * SUBS, SUBS), :] for v in range(vregs)]

        def body(offset, carry):
            return advance(tile, offset, carry, grows, shrinks)

        return lax.fori_loop(0, count, body, state, unroll=unroll)

    zeros = tuple(jnp.zeros((SUBS, LANES), jnp.float32) for _ in range(vregs))
    state = (zeros, tuple(firsts))
    whole_tiles = STEPS // step_tile
    state = lax.fori_loop(
        0, whole_tiles, lambda tile, carry: run_tile(tile, carry, step_tile, 8), state
    )
    if STEPS % step_tile:
        run_tile(whole_tiles, state, STEPS % step_tile, STEPS % step_tile % 16)

    for row in range(slot_count):
        for half in range(2):
            stage_ref[row, pl.ds((half + 1) * 2 * pair_pad - 2 * SUBS, 2 * SUBS), :] = jnp.zeros(
                (2 * SUBS, LANES), jnp.float32
            )
    fetch.wait()

    rows_half = slot_count * SUBS
    edges = (0, 256, 512, STEPS)
    dot = functools.partial(jnp.dot, preferred_element_type=jnp.float32)

    def split_parts(values):
        high = values.astype(jnp.bfloat16)
        low = (values - high.astype(jnp.float32)).astype(jnp.bfloat16)
        return high, low

    def product(left, right):
        left_high, left_low = split_parts(left)
        right_high, right_low = split_parts(right)
        if left.shape[1] % LANES:
            return (
                dot(left_high, right_high) + dot(left_low, right_high) + dot(left_high, right_low)
            )
        return dot(
            jnp.concatenate([left_high, left_low, left_high], axis=1),
            jnp.concatenate([right_high, right_high, right_low], axis=0),
        )

    def group(start):
        values = spectra_ref[:, pl.ds(start, PAIRS), :, :].reshape(slot_count, SUBS, STEPS)
        step = lax.broadcasted_iota(jnp.int32, (1, SUBS, STEPS), 2)
        row_pair = lax.broadcasted_iota(jnp.int32, (1, SUBS, STEPS), 1) // 2
        in_first = step < NM - (first_pair + start + row_pair)
        lower = jnp.where(in_first, values, 0.0)
        upper = jnp.where(in_first, 0.0, values)
        first_block = start // per_block
        blocks = PAIRS // per_block
        table = jnp.concatenate(
            [table_ref[pl.ds((first_block + n) * TABLE_ROWS, STEPS), :] for n in range(blocks)],
            axis=1,
        )
        begin, end = edges[0], edges[1]
        base = product(
            values[:, :, begin:end].reshape(rows_half, end - begin), table[begin:end]
        )
        rest = None
        for begin, end in zip(edges[1:-1], edges[2:]):
            left = jnp.concatenate([lower[:, :, begin:end], upper[:, :, begin:end]], axis=0)
            part = product(left.reshape(2 * rows_half, end - begin), table[begin:end])
            rest = part if rest is None else rest + part
        both = jnp.concatenate([rest[:rows_half] + base, rest[rows_half:]], axis=0)
        row_id = lax.broadcasted_iota(jnp.int32, (2 * rows_half, LANES), 0) % SUBS // 2
        lane_part = lax.broadcasted_iota(jnp.int32, (2 * rows_half, LANES), 1) // rows_all
        total = jnp.zeros((2 * rows_half, LANES), jnp.float32)
        for block in range(blocks):
            keep = row_id == block * per_block + lane_part
            total = total + jnp.where(keep, both[:, block * LANES : (block + 1) * LANES], 0.0)
        if per_block == 2:
            total = total + pltpu.roll(total, rows_all, 1)
        total = total.astype(jnp.bfloat16).astype(jnp.float32)
        for half in range(2):
            for row in range(slot_count):
                source = (half * slot_count + row) * SUBS
                stage_ref[row, pl.ds(half * 2 * pair_pad + 2 * start, SUBS), :] = total[
                    source : source + SUBS
                ]

    def group_body(index, carry):
        group(index * PAIRS)
        return carry

    lax.fori_loop(0, pair_count // PAIRS, group_body, 0)
    if pair_count % PAIRS:
        group(pair_count - PAIRS)

    for row in range(slot_count):
        flipped = stage_ref[row].T
        out_ref[:, pl.ds(row * lat_rows, lat_rows), :] = flipped[:rows_all].reshape(
            lat_count, lat_rows, 4 * pair_pad
        )


def coefficients(spectra, first_pair, rows_all, lat_rows):
    slot_count, _, pair_count, steps = spectra.shape
    per_block = LANES // rows_all
    vregs = pad_to(pair_count, SUBS * per_block) // (SUBS * per_block)
    tile_total = pad_to(STEPS, rows_all) // rows_all
    pair_pad = pad_to(pair_count, SUBS)
    lat_count = rows_all // lat_rows
    kernel = functools.partial(
        coeff_kernel, pair_count=pair_count, rows_all=rows_all, lat_rows=lat_rows,
        slot_count=slot_count,
    )
    return pl.pallas_call(
        kernel,
        out_shape=jax.ShapeDtypeStruct(
            (lat_count, slot_count * lat_rows, 4 * pair_pad), jnp.float32
        ),
        in_specs=[
            pl.BlockSpec(memory_space=pltpu.SMEM),
            pl.BlockSpec(memory_space=pl.ANY),
        ],
        out_specs=pl.BlockSpec(memory_space=pltpu.VMEM),
        scratch_shapes=[
            pltpu.VMEM((slot_count, pair_count, 2, steps), jnp.float32),
            pltpu.VMEM((tile_total, vregs * SUBS, LANES), jnp.float32),
            pltpu.VMEM((tile_total, vregs * SUBS, LANES), jnp.float32),
            pltpu.VMEM((vregs * SUBS * TABLE_ROWS, LANES), jnp.float32),
            pltpu.VMEM((slot_count, 4 * pair_pad, LANES), jnp.float32),
            pltpu.SemaphoreType.DMA,
        ],
        compiler_params=pltpu.CompilerParams(vmem_limit_bytes=VMEM_LIMIT),
        name="coefficients",
    )(first_pair, jnp.transpose(spectra, (0, 2, 1, 3)))


def trig_kernel(out_ref, *, pair_count, pair_pad, quarter, fine_total):
    block = pl.program_id(0)
    width = 4 * pair_pad
    coarse_total = pad_to(quarter // fine_total, SUBS)

    def orders(rows):
        lane = lax.broadcasted_iota(jnp.int32, (rows, width), 1)
        upper = lane >= 2 * pair_pad
        pair = jnp.where(upper, lane - 2 * pair_pad, lane)
        is_sine = (pair & 1) == 1
        pair = block * pair_count + (pair >> 1)
        return jnp.where(upper, NM - 1 - pair, pair), is_sine

    def angles(rows, spacing):
        order, _ = orders(rows)
        column = lax.broadcasted_iota(jnp.int32, (rows, width), 0) * spacing
        phase = (order * column % NLON).astype(jnp.float32) * (2.0 * math.pi / NLON)
        return jnp.cos(phase), jnp.sin(phase)

    fine_cos, fine_sin = angles(fine_total, 1)
    coarse_cos, coarse_sin = angles(coarse_total, fine_total)
    order, is_sine = orders(1)
    weights = []
    for turn in range(4):
        side = (order * turn) & 3
        even = jnp.where(side == 0, 1.0, jnp.where(side == 2, -1.0, 0.0))
        odd = jnp.where(side == 1, 1.0, jnp.where(side == 3, -1.0, 0.0))
        weights.append((jnp.where(is_sine, odd, even), jnp.where(is_sine, even, -odd)))
    for tile in range(quarter // fine_total):
        left, right = coarse_cos[tile : tile + 1], coarse_sin[tile : tile + 1]
        cosine = left * fine_cos - right * fine_sin
        sine = right * fine_cos + left * fine_sin
        for turn in range(4):
            on_cos, on_sin = weights[turn]
            out_ref[pl.ds(turn * quarter + tile * fine_total, fine_total), :] = (
                on_cos * cosine + on_sin * sine
            ).astype(jnp.bfloat16)


def trig_table(pair_count, lon_count):
    pair_pad = pad_to(pair_count, SUBS)
    quarter = NLON // 4
    fine_total = 40
    return pl.pallas_call(
        functools.partial(
            trig_kernel, pair_count=pair_count, pair_pad=pair_pad, quarter=quarter,
            fine_total=fine_total,
        ),
        grid=(lon_count,),
        out_shape=jax.ShapeDtypeStruct((lon_count, NLON, 4 * pair_pad), jnp.bfloat16),
        out_specs=pl.BlockSpec((None, NLON, 4 * pair_pad), lambda b: (b, 0, 0)),
        compiler_params=pltpu.CompilerParams(vmem_limit_bytes=VMEM_LIMIT),
        cost_estimate=pl.CostEstimate(
            flops=20 * lon_count * NLON * pair_pad,
            bytes_accessed=lon_count * NLON * 8 * pair_pad,
            transcendentals=0,
        ),
        name="trig_table",
    )()


def grid_kernel(trig_ref, coeff_ref, out_ref, right_ref, *, lon_count):
    share = coeff_ref.shape[1]
    width = coeff_ref.shape[2]
    rows = coeff_ref.shape[0] // lon_count * share

    @pl.when(pl.program_id(0) == 0)
    def _():
        values = coeff_ref[...].reshape(rows // share, lon_count, share, width)
        for block in range(lon_count):
            right_ref[block] = values[:, block].reshape(rows, width).T.astype(jnp.bfloat16)

    total = None
    for block in range(lon_count):
        part = jnp.dot(trig_ref[block], right_ref[block], preferred_element_type=jnp.float32)
        total = part if total is None else total + part
    out_ref[...] = total


def grid_field(trig, coeffs, lon_count):
    share = coeffs.shape[1]
    rows = coeffs.shape[0] // lon_count * share
    width = trig.shape[2]
    pieces = 4
    cols = NLON // pieces
    return pl.pallas_call(
        functools.partial(grid_kernel, lon_count=lon_count),
        grid=(pieces,),
        out_shape=jax.ShapeDtypeStruct((NLON, rows), jnp.float32),
        in_specs=[
            pl.BlockSpec((lon_count, cols, width), lambda j: (0, j, 0)),
            pl.BlockSpec(coeffs.shape, lambda j: (0, 0, 0)),
        ],
        out_specs=pl.BlockSpec((cols, rows), lambda j: (j, 0)),
        scratch_shapes=[pltpu.VMEM((lon_count, width, rows), jnp.bfloat16)],
        compiler_params=pltpu.CompilerParams(vmem_limit_bytes=VMEM_LIMIT),
        cost_estimate=pl.CostEstimate(
            flops=2 * NLON * lon_count * width * rows,
            bytes_accessed=trig.size * 2 + 2 * coeffs.size * 4,
            transcendentals=0,
        ),
        name="grid_field",
    )(trig, coeffs)


def gelu_parts(preact):
    scale = math.sqrt(2.0 / math.pi)
    square = preact * preact
    bend = jnp.tanh(scale * (preact + 0.044715 * (square * preact)))
    half = 0.5 * (1.0 + bend)
    slope = half + (0.5 * preact) * (1.0 - bend * bend) * (
        scale * (1.0 + (3.0 * 0.044715) * square)
    )
    return preact * half, slope


def forward_kernel(latents_ref, w_ref, b_ref, slope_ref, hidden_t_ref, latents_t_ref):
    latents = latents_ref[...]
    preact = jnp.dot(latents, w_ref[...], preferred_element_type=jnp.float32) + b_ref[...]
    hidden, slope = gelu_parts(preact)
    slope_ref[...] = slope
    hidden_t_ref[...] = hidden.T.astype(jnp.bfloat16)
    latents_t_ref[...] = latents.T


def forward(latents, w_hidden, b_hidden, parts):
    cells, width = latents.shape
    cols = cells // parts
    return pl.pallas_call(
        forward_kernel,
        grid=(parts,),
        out_shape=(
            jax.ShapeDtypeStruct((cells, width), jnp.float32),
            jax.ShapeDtypeStruct((parts, width, cols), jnp.bfloat16),
            jax.ShapeDtypeStruct((parts, width, cols), jnp.bfloat16),
        ),
        in_specs=[
            pl.BlockSpec((cols, width), lambda i: (i, 0)),
            pl.BlockSpec((width, width), lambda i: (0, 0)),
            pl.BlockSpec((1, width), lambda i: (0, 0)),
        ],
        out_specs=(
            pl.BlockSpec((cols, width), lambda i: (i, 0)),
            pl.BlockSpec((None, width, cols), lambda i: (i, 0, 0)),
            pl.BlockSpec((None, width, cols), lambda i: (i, 0, 0)),
        ),
        compiler_params=pltpu.CompilerParams(vmem_limit_bytes=VMEM_LIMIT),
        cost_estimate=pl.CostEstimate(
            flops=2 * cells * width * width,
            bytes_accessed=cells * width * 10,
            transcendentals=cells * width,
        ),
        name="forward",
    )(latents, w_hidden, b_hidden.reshape(1, width))


def backward_kernel(
    core_ref, grid_ref, scale_ref, place_ref, w_out_ref, slope_ref, hidden_t_ref, latents_t_ref,
    preact_ref, keep_ref, send_ref, field_ref, hidden_acc, out_acc, bias_acc, sums_ref,
):
    index = pl.program_id(0)
    total = pl.num_programs(0)
    blocks = grid_ref.shape[0]
    lon_cols = grid_ref.shape[1]
    width = hidden_acc.shape[0]
    cols = slope_ref.shape[0]
    sum_rows = sums_ref.shape[0]

    @pl.when(index == 0)
    def _():
        field = None
        for block in range(blocks):
            scaled = (grid_ref[block] * scale_ref[block]).astype(jnp.bfloat16)
            part = jnp.dot(scaled, place_ref[block], preferred_element_type=jnp.float32)
            field = part if field is None else field + part
        for row in range(field.shape[1] // LANES):
            field_ref[pl.ds(row * lon_cols, lon_cols), :] = field[
                :, row * LANES : (row + 1) * LANES
            ]
        hidden_acc[...] = jnp.zeros_like(hidden_acc)
        out_acc[...] = jnp.zeros_like(out_acc)
        bias_acc[...] = jnp.zeros_like(bias_acc)

    field = field_ref[pl.ds(pl.multiple_of(index * cols, SUBS), cols), :].astype(jnp.bfloat16)
    back = jnp.dot(field, w_out_ref[...], preferred_element_type=jnp.float32)
    preact_back = (back * slope_ref[...]).astype(jnp.bfloat16)
    preact_ref[...] = preact_back
    hidden_acc[...] += jnp.dot(
        latents_t_ref[...], preact_back, preferred_element_type=jnp.float32
    )
    out_acc[...] += jnp.dot(hidden_t_ref[...], field, preferred_element_type=jnp.float32)
    bias_acc[...] += jnp.sum(preact_back.astype(jnp.float32), axis=0, keepdims=True)

    @pl.when(index == total - 1)
    def _():
        tiles = width // LANES
        for row_tile in range(width // SUBS):
            for tile in range(tiles):
                sums_ref[pl.ds((row_tile * tiles + tile) * SUBS, SUBS), :] = hidden_acc[
                    pl.ds(row_tile * SUBS, SUBS), pl.ds(tile * LANES, LANES)
                ]
        base = width * tiles
        flipped = out_acc[...].T
        for tile in range(tiles):
            sums_ref[pl.ds(base + tile * F, F), :] = flipped[:F, tile * LANES : (tile + 1) * LANES]
        base = base + tiles * F
        sums_ref[pl.ds(base, sum_rows - base), :] = jnp.zeros((sum_rows - base, LANES), jnp.float32)
        for tile in range(tiles):
            sums_ref[pl.ds(base + tile, 1), :] = bias_acc[:, tile * LANES : (tile + 1) * LANES]
        half = sum_rows // 2
        mine = core_ref[0]
        keep_ref[...] = sums_ref[pl.ds(pl.multiple_of(mine * half, SUBS), half), :]
        send_ref[...] = sums_ref[pl.ds(pl.multiple_of((1 - mine) * half, SUBS), half), :]


def backward(core, grid, scale, place, w_out_t, slope, hidden_t, latents_t, sum_rows):
    cells, width = slope.shape
    parts, _, cols = hidden_t.shape
    half = (sum_rows // 2, LANES)
    whole3 = lambda i: (0, 0, 0)
    whole2 = lambda i: (0, 0)
    return pl.pallas_call(
        backward_kernel,
        grid=(parts,),
        out_shape=(
            jax.ShapeDtypeStruct((cells, width), jnp.bfloat16),
            jax.ShapeDtypeStruct(half, jnp.float32),
            jax.ShapeDtypeStruct(half, jnp.float32),
        ),
        in_specs=[
            pl.BlockSpec(memory_space=pltpu.SMEM),
            pl.BlockSpec(grid.shape, whole3),
            pl.BlockSpec(scale.shape, whole3),
            pl.BlockSpec(place.shape, whole3),
            pl.BlockSpec(w_out_t.shape, whole2),
            pl.BlockSpec((cols, width), lambda i: (i, 0)),
            pl.BlockSpec((None, width, cols), lambda i: (i, 0, 0)),
            pl.BlockSpec((None, width, cols), lambda i: (i, 0, 0)),
        ],
        out_specs=(
            pl.BlockSpec((cols, width), lambda i: (i, 0)),
            pl.BlockSpec(half, whole2),
            pl.BlockSpec(half, whole2),
        ),
        scratch_shapes=[
            pltpu.VMEM((cells, LANES), jnp.float32),
            pltpu.VMEM((width, width), jnp.float32),
            pltpu.VMEM((width, LANES), jnp.float32),
            pltpu.VMEM((1, width), jnp.float32),
            pltpu.VMEM((sum_rows, LANES), jnp.float32),
        ],
        compiler_params=pltpu.CompilerParams(vmem_limit_bytes=VMEM_LIMIT),
        cost_estimate=pl.CostEstimate(
            flops=2 * cells * width * (width + 2 * LANES),
            bytes_accessed=cells * width * 10,
            transcendentals=0,
        ),
        name="backward",
    )(core, grid, scale, place, w_out_t, slope, hidden_t, latents_t)


def add_kernel(index_ref, *refs, inputs, outputs, factor):
    size = refs[0].shape[0] // outputs
    for part in range(outputs):
        start = 0 if outputs == 1 else pl.multiple_of((index_ref[0] ^ part) * size, SUBS)
        total = refs[0][pl.ds(start, size), :]
        for piece in refs[1:inputs]:
            total = total + piece[pl.ds(start, size), :]
        if factor is not None:
            total = total * factor
        refs[inputs + part][...] = total


def add_pieces(index, pieces, outputs, factor=None):
    rows = pieces[0].shape[0]
    size = rows // outputs
    return pl.pallas_call(
        functools.partial(add_kernel, inputs=len(pieces), outputs=outputs, factor=factor),
        out_shape=[jax.ShapeDtypeStruct((size, LANES), jnp.float32)] * outputs,
        in_specs=[pl.BlockSpec(memory_space=pltpu.SMEM)]
        + [pl.BlockSpec(memory_space=pltpu.VMEM)] * len(pieces),
        out_specs=[pl.BlockSpec(memory_space=pltpu.VMEM)] * outputs,
        cost_estimate=pl.CostEstimate(
            flops=len(pieces) * rows * LANES,
            bytes_accessed=4 * (len(pieces) + 1) * rows * LANES,
            transcendentals=0,
        ),
        name="add_pieces",
    )(index, *pieces)


def finish_kernel(
    place_ref, own_ref, other_ref, hidden_ref, bias_ref, out_ref, flat_ref, *, lon_count, depth
):
    core, lon, deep = place_ref[0], place_ref[1], place_ref[2]
    size = own_ref.shape[0] // (lon_count * depth)
    for half, source in enumerate((own_ref, other_ref)):
        for part in range(lon_count):
            for piece in range(depth):
                start = (((core ^ half) * lon_count + (lon ^ part)) * depth + (deep ^ piece)) * size
                flat_ref[pl.ds(pl.multiple_of(start, SUBS), size), :] = source[
                    pl.ds((part * depth + piece) * size, size), :
                ]
    width = hidden_ref.shape[0]
    tiles = width // LANES
    for row_tile in range(width // SUBS):
        for tile in range(tiles):
            hidden_ref[pl.ds(row_tile * SUBS, SUBS), pl.ds(tile * LANES, LANES)] = flat_ref[
                pl.ds((row_tile * tiles + tile) * SUBS, SUBS), :
            ]
    base = width * tiles
    for tile in range(tiles):
        out_ref[:, pl.ds(tile * LANES, LANES)] = flat_ref[pl.ds(base + tile * F, F), :]
        bias_ref[:, pl.ds(tile * LANES, LANES)] = flat_ref[pl.ds(base + tiles * F + tile, 1), :]


def finish(place, own, other, width, lon_count, depth):
    return pl.pallas_call(
        functools.partial(finish_kernel, lon_count=lon_count, depth=depth),
        out_shape=(
            jax.ShapeDtypeStruct((width, width), jnp.float32),
            jax.ShapeDtypeStruct((1, width), jnp.float32),
            jax.ShapeDtypeStruct((F, width), jnp.float32),
        ),
        in_specs=[pl.BlockSpec(memory_space=pltpu.SMEM)]
        + [pl.BlockSpec(memory_space=pltpu.VMEM)] * 2,
        out_specs=(pl.BlockSpec(memory_space=pltpu.VMEM),) * 3,
        scratch_shapes=[pltpu.VMEM((2 * own.shape[0], LANES), jnp.float32)],
        name="finish",
    )(place, own, other)


def swap(value, axis, bits):
    count = lax.axis_size(axis)
    return lax.ppermute(value, axis, [(i, i ^ bits) for i in range(count)])


def local(spectra, field_slot, field_weight, latents, w_hidden, b_hidden, w_out):
    slot_count, _, pair_count, _ = spectra.shape
    lat_rows, lon_cols, width = latents.shape
    lat_count = lax.axis_size("lat")
    lon_count = lax.axis_size("lon")
    rows_all = lat_rows * lat_count
    lat_index = lax.axis_index("lat").astype(jnp.int32)
    lon_index = lax.axis_index("lon").astype(jnp.int32)
    pair_pad = pad_to(pair_count, SUBS)
    cells = lat_rows * lon_cols
    parts = 4

    coeffs = coefficients(spectra, (lon_index * pair_count).reshape(1), rows_all, lat_rows)
    share = slot_count * lat_rows // lon_count
    coeffs = coeffs.reshape(lat_count * lon_count, share, 4 * pair_pad)
    coeffs = lax.all_to_all(coeffs, ("lat", "lon"), split_axis=0, concat_axis=0, tiled=True)

    slope, hidden_t, latents_t = forward(
        latents.reshape(cells, width), w_hidden, b_hidden, parts
    )
    trig = trig_table(pair_count, lon_count)

    lanes = lat_count * share

    def spread(values):
        values = jnp.broadcast_to(values, (lat_count, slot_count, lat_rows))
        values = values.reshape(lat_count, lon_count, share)
        return jnp.transpose(values, (1, 0, 2)).reshape(lon_count, lanes)

    field_ids = spread(field_slot.reshape(lat_count, slot_count, 1))
    row_ids = spread(jnp.arange(lat_rows, dtype=jnp.int32).reshape(1, 1, lat_rows))
    chosen = field_ids[:, :, None] == jnp.arange(F, dtype=jnp.int32)
    weight = jnp.sum(jnp.where(chosen, field_weight, 0.0), axis=2)
    sine = jnp.sin(band_angles(lat_index * lat_rows + row_ids, rows_all))
    scale = (sine * weight)[:, None, :]
    target = row_ids * LANES + field_ids
    place = (
        target[:, :, None] == jnp.arange(lat_rows * LANES, dtype=jnp.int32)[None, None, :]
    ).astype(jnp.bfloat16)
    w_out_t = jnp.concatenate([w_out.T, jnp.zeros((LANES - F, width), w_out.dtype)], axis=0)

    coeffs, slope, hidden_t, latents_t, trig, scale, place, w_out_t = lax.optimization_barrier(
        (coeffs, slope, hidden_t, latents_t, trig, scale, place, w_out_t)
    )
    grid = grid_field(trig, coeffs, lon_count).reshape(lon_count, lon_cols, lanes)
    grid = lax.all_to_all(grid, "lon", split_axis=0, concat_axis=0, tiled=True)

    device_count = lat_count * lon_count
    used_rows = (width + F + 1) * width // LANES
    chunk = pad_to(pad_to(used_rows, device_count) // device_count, SUBS)
    core_index, deep_index = lat_index & 1, lat_index >> 1
    depth = lat_count // 2
    preact_back, keep, send = backward(
        core_index.reshape(1), grid, scale, place, w_out_t, slope, hidden_t, latents_t,
        chunk * device_count,
    )
    latent_grad = lax.dot_general(
        preact_back, w_hidden, (((1,), (1,)), ((), ())), preferred_element_type=jnp.float32
    ).astype(jnp.bfloat16)

    pieces = add_pieces(
        lon_index.reshape(1), [keep, swap(send, "lat", 1)], lon_count
    )
    arrived = [swap(pieces[part], "lon", part) for part in range(1, lon_count)]
    pieces = add_pieces(deep_index.reshape(1), [pieces[0]] + arrived, depth)
    arrived = [swap(pieces[part], "lat", 2 * part) for part in range(1, depth)]
    norm = 1.0 / math.sqrt(rows_all * NLON)
    total = add_pieces(deep_index.reshape(1), [pieces[0]] + arrived, 1, norm)[0]
    total = jnp.concatenate([total] + [swap(total, "lat", 2 * part) for part in range(1, depth)])
    total = jnp.concatenate([total] + [swap(total, "lon", part) for part in range(1, lon_count)])
    other = swap(total, "lat", 1)
    hidden_grad, bias_grad, out_grad = finish(
        jnp.stack([core_index, lon_index, deep_index]), total, other, width, lon_count, depth
    )
    return (
        latent_grad.reshape(lat_rows, lon_cols, width),
        hidden_grad,
        bias_grad.reshape(width),
        out_grad.T,
    )


def solution(mesh):
    in_specs = (P("lat", None, "lon", None), P(), P(), P("lat", "lon", None), P(), P(), P())
    out_specs = (P("lat", "lon", None), P(), P(), P())
    return jax.shard_map(local, mesh=mesh, in_specs=in_specs, out_specs=out_specs, check_vma=False)
```

```python
import functools
import math

import jax
import jax.numpy as jnp
from jax import lax
from jax.experimental import pallas as pl
from jax.experimental.pallas import tpu as pltpu
from jax.sharding import PartitionSpec as P

NM = 720
NLON = 1440
F = 64
LANES = 128
SUBS = 8
STEPS = NM + 1
PAIRS = 4
TABLE_ROWS = 729
VMEM_LIMIT = 56 * 1024 * 1024


def band_angles(row_ids, rows_all):
    return jnp.pi * (NM // 2 - rows_all // 2 + row_ids.astype(jnp.float32)) / NM


def pad_to(value, multiple):
    return (value + multiple - 1) // multiple * multiple


def coeff_kernel(
    first_ref, spectra_hbm, out_ref, spectra_ref, grow_ref, shrink_ref, table_ref, stage_ref,
    copy_sem, *, pair_count, rows_all, lat_rows, slot_count,
):
    per_block = LANES // rows_all
    vregs = pad_to(pair_count, SUBS * per_block) // (SUBS * per_block)
    step_tile = rows_all
    tile_total = pad_to(STEPS, step_tile) // step_tile
    pair_pad = pad_to(pair_count, SUBS)
    lat_count = rows_all // lat_rows
    first_pair = first_ref[0]

    fetch = pltpu.make_async_copy(spectra_hbm, spectra_ref, copy_sem)
    fetch.start()

    lane = lax.broadcasted_iota(jnp.int32, (SUBS, LANES), 1)
    sub = lax.broadcasted_iota(jnp.int32, (SUBS, LANES), 0)
    inner = lane & (rows_all - 1)
    which = lane // rows_all
    colatitude = band_angles(inner, rows_all)
    cosine = jnp.cos(colatitude)
    log_sine = jnp.log(jnp.sin(colatitude))

    def log_total(order_column):
        total = jnp.zeros((SUBS, LANES), jnp.float32)
        for tile in range(pad_to(NM, LANES) // LANES):
            term = (lane + tile * LANES).astype(jnp.float32)
            safe = jnp.maximum(term, 1.0)
            value = jnp.log((2.0 * safe + 1.0) / (2.0 * safe))
            total = total + jnp.where((term >= 1.0) & (term <= order_column), value, 0.0)
        return jnp.sum(total, axis=1, keepdims=True)

    def seed(order_of):
        total = jnp.zeros((SUBS, LANES), jnp.float32)
        for part in range(per_block):
            column = order_of(part).astype(jnp.float32)
            total = jnp.where(which == part, log_total(column), total)
        order = order_of(which).astype(jnp.float32)
        return jnp.exp(0.5 * total - 0.5 * math.log(4.0 * math.pi) + order * log_sine)

    firsts, seconds, switches = [], [], []
    for v in range(vregs):
        base = first_pair + (sub + v * SUBS) * per_block

        def order_first(part, base=base):
            return base + part

        def order_second(part, base=base):
            return NM - 1 - (base + part)

        firsts.append(seed(order_first))
        seconds.append(seed(order_second))
        pair = base + which
        switch = NM - pair
        switches.append(switch)
        for tile in range(tile_total):
            step = inner + tile * step_tile
            in_first = step < switch
            order = jnp.where(in_first, pair, NM - 1 - pair).astype(jnp.float32)
            degree = jnp.where(in_first, pair + step, step - 1).astype(jnp.float32)
            lower = degree - 1.0
            grow = jnp.sqrt(
                (4.0 * degree * degree - 1.0) / jnp.maximum(degree * degree - order * order, 1.0)
            )
            shrink = jnp.sqrt(
                jnp.maximum(lower * lower - order * order, 0.0)
                / jnp.maximum(4.0 * lower * lower - 1.0, 1.0)
            )
            start = step == 0
            grow_ref[tile, pl.ds(v * SUBS, SUBS), :] = jnp.where(start, 1.0, grow)
            shrink_ref[tile, pl.ds(v * SUBS, SUBS), :] = jnp.where(start, -1.0, shrink)

    def advance(tile, offset, state, grows, shrinks):
        previous, before = state
        index = which * rows_all + offset
        step = tile * step_tile + offset
        produced = []
        for v in range(vregs):
            grow = jnp.take_along_axis(grows[v], index, axis=1)
            shrink = jnp.take_along_axis(shrinks[v], index, axis=1)
            value = grow * (cosine * previous[v] - shrink * before[v])
            value = jnp.where(switches[v] == step, seconds[v], value)
            table_ref[pl.ds(v * SUBS * TABLE_ROWS + step, SUBS, stride=TABLE_ROWS), :] = value
            produced.append(value)
        return (tuple(produced), previous)

    def run_tile(tile, state, count, unroll):
        grows = [grow_ref[tile, pl.ds(v * SUBS, SUBS), :] for v in range(vregs)]
        shrinks = [shrink_ref[tile, pl.ds(v * SUBS, SUBS), :] for v in range(vregs)]

        def body(offset, carry):
            return advance(tile, offset, carry, grows, shrinks)

        return lax.fori_loop(0, count, body, state, unroll=unroll)

    zeros = tuple(jnp.zeros((SUBS, LANES), jnp.float32) for _ in range(vregs))
    state = (zeros, tuple(firsts))
    whole_tiles = STEPS // step_tile
    state = lax.fori_loop(
        0, whole_tiles, lambda tile, carry: run_tile(tile, carry, step_tile, 8), state
    )
    if STEPS % step_tile:
        run_tile(whole_tiles, state, STEPS % step_tile, STEPS % step_tile % 16)

    for row in range(slot_count):
        for half in range(2):
            stage_ref[row, pl.ds((half + 1) * 2 * pair_pad - 2 * SUBS, 2 * SUBS), :] = jnp.zeros(
                (2 * SUBS, LANES), jnp.float32
            )
    fetch.wait()

    rows_half = slot_count * SUBS
    edges = (0, 256, 512, STEPS)
    dot = functools.partial(jnp.dot, preferred_element_type=jnp.float32)

    def split_parts(values):
        high = values.astype(jnp.bfloat16)
        low = (values - high.astype(jnp.float32)).astype(jnp.bfloat16)
        return high, low

    def product(left, right):
        left_high, left_low = split_parts(left)
        right_high, right_low = split_parts(right)
        if left.shape[1] % LANES:
            return (
                dot(left_high, right_high) + dot(left_low, right_high) + dot(left_high, right_low)
            )
        return dot(
            jnp.concatenate([left_high, left_low, left_high], axis=1),
            jnp.concatenate([right_high, right_high, right_low], axis=0),
        )

    def group(start):
        values = spectra_ref[:, pl.ds(start, PAIRS), :, :].reshape(slot_count, SUBS, STEPS)
        step = lax.broadcasted_iota(jnp.int32, (1, SUBS, STEPS), 2)
        row_pair = lax.broadcasted_iota(jnp.int32, (1, SUBS, STEPS), 1) // 2
        in_first = step < NM - (first_pair + start + row_pair)
        lower = jnp.where(in_first, values, 0.0)
        upper = jnp.where(in_first, 0.0, values)
        first_block = start // per_block
        blocks = PAIRS // per_block
        table = jnp.concatenate(
            [table_ref[pl.ds((first_block + n) * TABLE_ROWS, STEPS), :] for n in range(blocks)],
            axis=1,
        )
        begin, end = edges[0], edges[1]
        base = product(
            values[:, :, begin:end].reshape(rows_half, end - begin), table[begin:end]
        )
        rest = None
        for begin, end in zip(edges[1:-1], edges[2:]):
            left = jnp.concatenate([lower[:, :, begin:end], upper[:, :, begin:end]], axis=0)
            part = product(left.reshape(2 * rows_half, end - begin), table[begin:end])
            rest = part if rest is None else rest + part
        both = jnp.concatenate([rest[:rows_half] + base, rest[rows_half:]], axis=0)
        row_id = lax.broadcasted_iota(jnp.int32, (2 * rows_half, LANES), 0) % SUBS // 2
        lane_part = lax.broadcasted_iota(jnp.int32, (2 * rows_half, LANES), 1) // rows_all
        total = jnp.zeros((2 * rows_half, LANES), jnp.float32)
        for block in range(blocks):
            keep = row_id == block * per_block + lane_part
            total = total + jnp.where(keep, both[:, block * LANES : (block + 1) * LANES], 0.0)
        if per_block == 2:
            total = total + pltpu.roll(total, rows_all, 1)
        total = total.astype(jnp.bfloat16).astype(jnp.float32)
        for half in range(2):
            for row in range(slot_count):
                source = (half * slot_count + row) * SUBS
                stage_ref[row, pl.ds(half * 2 * pair_pad + 2 * start, SUBS), :] = total[
                    source : source + SUBS
                ]

    def group_body(index, carry):
        group(index * PAIRS)
        return carry

    lax.fori_loop(0, pair_count // PAIRS, group_body, 0)
    if pair_count % PAIRS:
        group(pair_count - PAIRS)

    for row in range(slot_count):
        flipped = stage_ref[row].T
        out_ref[:, pl.ds(row * lat_rows, lat_rows), :] = flipped[:rows_all].reshape(
            lat_count, lat_rows, 4 * pair_pad
        )


def coefficients(spectra, first_pair, rows_all, lat_rows):
    slot_count, _, pair_count, steps = spectra.shape
    per_block = LANES // rows_all
    vregs = pad_to(pair_count, SUBS * per_block) // (SUBS * per_block)
    tile_total = pad_to(STEPS, rows_all) // rows_all
    pair_pad = pad_to(pair_count, SUBS)
    lat_count = rows_all // lat_rows
    kernel = functools.partial(
        coeff_kernel, pair_count=pair_count, rows_all=rows_all, lat_rows=lat_rows,
        slot_count=slot_count,
    )
    return pl.pallas_call(
        kernel,
        out_shape=jax.ShapeDtypeStruct(
            (lat_count, slot_count * lat_rows, 4 * pair_pad), jnp.float32
        ),
        in_specs=[
            pl.BlockSpec(memory_space=pltpu.SMEM),
            pl.BlockSpec(memory_space=pl.ANY),
        ],
        out_specs=pl.BlockSpec(memory_space=pltpu.VMEM),
        scratch_shapes=[
            pltpu.VMEM((slot_count, pair_count, 2, steps), jnp.float32),
            pltpu.VMEM((tile_total, vregs * SUBS, LANES), jnp.float32),
            pltpu.VMEM((tile_total, vregs * SUBS, LANES), jnp.float32),
            pltpu.VMEM((vregs * SUBS * TABLE_ROWS, LANES), jnp.float32),
            pltpu.VMEM((slot_count, 4 * pair_pad, LANES), jnp.float32),
            pltpu.SemaphoreType.DMA,
        ],
        compiler_params=pltpu.CompilerParams(vmem_limit_bytes=VMEM_LIMIT),
        name="coefficients",
    )(first_pair, jnp.transpose(spectra, (0, 2, 1, 3)))


def trig_kernel(out_ref, *, pair_count, pair_pad, quarter, fine_total):
    block = pl.program_id(0)
    width = 4 * pair_pad
    coarse_total = pad_to(quarter // fine_total, SUBS)

    def orders(rows):
        lane = lax.broadcasted_iota(jnp.int32, (rows, width), 1)
        upper = lane >= 2 * pair_pad
        pair = jnp.where(upper, lane - 2 * pair_pad, lane)
        is_sine = (pair & 1) == 1
        pair = block * pair_count + (pair >> 1)
        return jnp.where(upper, NM - 1 - pair, pair), is_sine

    def angles(rows, spacing):
        order, _ = orders(rows)
        column = lax.broadcasted_iota(jnp.int32, (rows, width), 0) * spacing
        phase = (order * column % NLON).astype(jnp.float32) * (2.0 * math.pi / NLON)
        return jnp.cos(phase), jnp.sin(phase)

    fine_cos, fine_sin = angles(fine_total, 1)
    coarse_cos, coarse_sin = angles(coarse_total, fine_total)
    _, is_sine = orders(fine_total)
    for tile in range(quarter // fine_total):
        left, right = coarse_cos[tile : tile + 1], coarse_sin[tile : tile + 1]
        cosine = left * fine_cos - right * fine_sin
        sine = right * fine_cos + left * fine_sin
        out_ref[pl.ds(tile * fine_total, fine_total), :] = jnp.where(
            is_sine, sine, cosine
        ).astype(jnp.bfloat16)


def trig_table(pair_count, lon_count):
    pair_pad = pad_to(pair_count, SUBS)
    quarter = NLON // 4
    fine_total = 40
    return pl.pallas_call(
        functools.partial(
            trig_kernel, pair_count=pair_count, pair_pad=pair_pad, quarter=quarter,
            fine_total=fine_total,
        ),
        grid=(lon_count,),
        out_shape=jax.ShapeDtypeStruct((lon_count, quarter, 4 * pair_pad), jnp.bfloat16),
        out_specs=pl.BlockSpec((None, quarter, 4 * pair_pad), lambda b: (b, 0, 0)),
        compiler_params=pltpu.CompilerParams(vmem_limit_bytes=VMEM_LIMIT),
        cost_estimate=pl.CostEstimate(
            flops=24 * lon_count * quarter * pair_pad,
            bytes_accessed=lon_count * quarter * 8 * pair_pad,
            transcendentals=0,
        ),
        name="trig_table",
    )()


def grid_kernel(trig_ref, coeff_ref, out_ref, right_ref, *, lon_count, pair_count):
    share = coeff_ref.shape[1]
    width = coeff_ref.shape[2]
    rows = coeff_ref.shape[0] // lon_count * share
    values = coeff_ref[...].reshape(rows // share, lon_count, share, width)
    line = lax.broadcasted_iota(jnp.int32, (width, rows), 0)
    upper = line >= width // 2
    pair = jnp.where(upper, line - width // 2, line)
    is_sine = (pair & 1) == 1
    for block in range(lon_count):
        flat = values[:, block].reshape(rows, width).T
        swapped = jnp.where(is_sine, -pltpu.roll(flat, 1, 0), pltpu.roll(flat, width - 1, 0))
        order = block * pair_count + (pair >> 1)
        order = jnp.where(upper, NM - 1 - order, order) & 3
        odd = (order & 1) == 1
        flip = jnp.where(odd, -flat, flat)
        turned = jnp.where(order == 1, swapped, jnp.where(order == 3, -swapped, flat))
        turned = jnp.where(order == 2, -flat, turned)
        back = jnp.where(odd, -turned, turned)
        for turn, part in enumerate((flat, turned, flip, back)):
            right_ref[pl.ds(block * width, width), pl.ds(turn * rows, rows)] = part.astype(
                jnp.bfloat16
            )
    total = None
    for block in range(lon_count):
        part = jnp.dot(
            trig_ref[block],
            right_ref[pl.ds(block * width, width), :],
            preferred_element_type=jnp.float32,
        )
        total = part if total is None else total + part
    for turn in range(4):
        out_ref[turn] = total[:, turn * rows : (turn + 1) * rows]


def grid_field(trig, coeffs, pair_count):
    lon_count, quarter, width = trig.shape
    rows = coeffs.shape[0] // lon_count * coeffs.shape[1]
    return pl.pallas_call(
        functools.partial(grid_kernel, lon_count=lon_count, pair_count=pair_count),
        out_shape=jax.ShapeDtypeStruct((4, quarter, rows), jnp.float32),
        scratch_shapes=[pltpu.VMEM((lon_count * width, 4 * rows), jnp.bfloat16)],
        compiler_params=pltpu.CompilerParams(vmem_limit_bytes=VMEM_LIMIT),
        cost_estimate=pl.CostEstimate(
            flops=2 * NLON * lon_count * width * rows,
            bytes_accessed=trig.size * 2 + 2 * coeffs.size * 4,
            transcendentals=0,
        ),
        name="grid_field",
    )(trig, coeffs)


def gelu_parts(preact):
    scale = math.sqrt(2.0 / math.pi)
    square = preact * preact
    bend = jnp.tanh(scale * (preact + 0.044715 * (square * preact)))
    half = 0.5 * (1.0 + bend)
    slope = half + (0.5 * preact) * (1.0 - bend * bend) * (
        scale * (1.0 + (3.0 * 0.044715) * square)
    )
    return preact * half, slope


def forward_kernel(latents_ref, w_ref, b_ref, slope_ref, hidden_t_ref, latents_t_ref):
    latents = latents_ref[...]
    preact = jnp.dot(latents, w_ref[...], preferred_element_type=jnp.float32) + b_ref[...]
    hidden, slope = gelu_parts(preact)
    slope_ref[...] = slope
    hidden_t_ref[...] = hidden.T.astype(jnp.bfloat16)
    latents_t_ref[...] = latents.T


def forward(latents, w_hidden, b_hidden, parts):
    cells, width = latents.shape
    cols = cells // parts
    return pl.pallas_call(
        forward_kernel,
        grid=(parts,),
        out_shape=(
            jax.ShapeDtypeStruct((cells, width), jnp.float32),
            jax.ShapeDtypeStruct((parts, width, cols), jnp.bfloat16),
            jax.ShapeDtypeStruct((parts, width, cols), jnp.bfloat16),
        ),
        in_specs=[
            pl.BlockSpec((cols, width), lambda i: (i, 0)),
            pl.BlockSpec((width, width), lambda i: (0, 0)),
            pl.BlockSpec((1, width), lambda i: (0, 0)),
        ],
        out_specs=(
            pl.BlockSpec((cols, width), lambda i: (i, 0)),
            pl.BlockSpec((None, width, cols), lambda i: (i, 0, 0)),
            pl.BlockSpec((None, width, cols), lambda i: (i, 0, 0)),
        ),
        compiler_params=pltpu.CompilerParams(vmem_limit_bytes=VMEM_LIMIT),
        cost_estimate=pl.CostEstimate(
            flops=2 * cells * width * width,
            bytes_accessed=cells * width * 10,
            transcendentals=cells * width,
        ),
        name="forward",
    )(latents, w_hidden, b_hidden.reshape(1, width))


def backward_kernel(
    core_ref, grid_ref, scale_ref, place_ref, w_out_ref, slope_ref, hidden_t_ref, latents_t_ref,
    preact_ref, keep_ref, send_ref, field_ref, hidden_acc, out_acc, bias_acc, sums_ref,
):
    index = pl.program_id(0)
    total = pl.num_programs(0)
    blocks = grid_ref.shape[0]
    lon_cols = grid_ref.shape[1]
    width = hidden_acc.shape[0]
    cols = slope_ref.shape[0]
    sum_rows = sums_ref.shape[0]

    @pl.when(index == 0)
    def _():
        field = None
        for block in range(blocks):
            scaled = (grid_ref[block] * scale_ref[block]).astype(jnp.bfloat16)
            part = jnp.dot(scaled, place_ref[block], preferred_element_type=jnp.float32)
            field = part if field is None else field + part
        for row in range(field.shape[1] // LANES):
            field_ref[pl.ds(row * lon_cols, lon_cols), :] = field[
                :, row * LANES : (row + 1) * LANES
            ]
        hidden_acc[...] = jnp.zeros_like(hidden_acc)
        out_acc[...] = jnp.zeros_like(out_acc)
        bias_acc[...] = jnp.zeros_like(bias_acc)

    field = field_ref[pl.ds(pl.multiple_of(index * cols, SUBS), cols), :].astype(jnp.bfloat16)
    back = jnp.dot(field, w_out_ref[...], preferred_element_type=jnp.float32)
    preact_back = (back * slope_ref[...]).astype(jnp.bfloat16)
    preact_ref[...] = preact_back
    hidden_acc[...] += jnp.dot(
        latents_t_ref[...], preact_back, preferred_element_type=jnp.float32
    )
    out_acc[...] += jnp.dot(hidden_t_ref[...], field, preferred_element_type=jnp.float32)
    bias_acc[...] += jnp.sum(preact_back.astype(jnp.float32), axis=0, keepdims=True)

    @pl.when(index == total - 1)
    def _():
        tiles = width // LANES
        for row_tile in range(width // SUBS):
            for tile in range(tiles):
                sums_ref[pl.ds((row_tile * tiles + tile) * SUBS, SUBS), :] = hidden_acc[
                    pl.ds(row_tile * SUBS, SUBS), pl.ds(tile * LANES, LANES)
                ]
        base = width * tiles
        flipped = out_acc[...].T
        for tile in range(tiles):
            sums_ref[pl.ds(base + tile * F, F), :] = flipped[:F, tile * LANES : (tile + 1) * LANES]
        base = base + tiles * F
        sums_ref[pl.ds(base, sum_rows - base), :] = jnp.zeros((sum_rows - base, LANES), jnp.float32)
        for tile in range(tiles):
            sums_ref[pl.ds(base + tile, 1), :] = bias_acc[:, tile * LANES : (tile + 1) * LANES]
        half = sum_rows // 2
        mine = core_ref[0]
        keep_ref[...] = sums_ref[pl.ds(pl.multiple_of(mine * half, SUBS), half), :]
        send_ref[...] = sums_ref[pl.ds(pl.multiple_of((1 - mine) * half, SUBS), half), :]


def backward(core, grid, scale, place, w_out_t, slope, hidden_t, latents_t, sum_rows):
    cells, width = slope.shape
    parts, _, cols = hidden_t.shape
    half = (sum_rows // 2, LANES)
    whole3 = lambda i: (0, 0, 0)
    whole2 = lambda i: (0, 0)
    return pl.pallas_call(
        backward_kernel,
        grid=(parts,),
        out_shape=(
            jax.ShapeDtypeStruct((cells, width), jnp.bfloat16),
            jax.ShapeDtypeStruct(half, jnp.float32),
            jax.ShapeDtypeStruct(half, jnp.float32),
        ),
        in_specs=[
            pl.BlockSpec(memory_space=pltpu.SMEM),
            pl.BlockSpec(grid.shape, whole3),
            pl.BlockSpec(scale.shape, whole3),
            pl.BlockSpec(place.shape, whole3),
            pl.BlockSpec(w_out_t.shape, whole2),
            pl.BlockSpec((cols, width), lambda i: (i, 0)),
            pl.BlockSpec((None, width, cols), lambda i: (i, 0, 0)),
            pl.BlockSpec((None, width, cols), lambda i: (i, 0, 0)),
        ],
        out_specs=(
            pl.BlockSpec((cols, width), lambda i: (i, 0)),
            pl.BlockSpec(half, whole2),
            pl.BlockSpec(half, whole2),
        ),
        scratch_shapes=[
            pltpu.VMEM((cells, LANES), jnp.float32),
            pltpu.VMEM((width, width), jnp.float32),
            pltpu.VMEM((width, LANES), jnp.float32),
            pltpu.VMEM((1, width), jnp.float32),
            pltpu.VMEM((sum_rows, LANES), jnp.float32),
        ],
        compiler_params=pltpu.CompilerParams(vmem_limit_bytes=VMEM_LIMIT),
        cost_estimate=pl.CostEstimate(
            flops=2 * cells * width * (width + 2 * LANES),
            bytes_accessed=cells * width * 10,
            transcendentals=0,
        ),
        name="backward",
    )(core, grid, scale, place, w_out_t, slope, hidden_t, latents_t)


def add_kernel(index_ref, *refs, inputs, outputs, factor):
    size = refs[0].shape[0] // outputs
    for part in range(outputs):
        start = 0 if outputs == 1 else pl.multiple_of((index_ref[0] ^ part) * size, SUBS)
        total = refs[0][pl.ds(start, size), :]
        for piece in refs[1:inputs]:
            total = total + piece[pl.ds(start, size), :]
        if factor is not None:
            total = total * factor
        refs[inputs + part][...] = total


def add_pieces(index, pieces, outputs, factor=None):
    rows = pieces[0].shape[0]
    size = rows // outputs
    return pl.pallas_call(
        functools.partial(add_kernel, inputs=len(pieces), outputs=outputs, factor=factor),
        out_shape=[jax.ShapeDtypeStruct((size, LANES), jnp.float32)] * outputs,
        in_specs=[pl.BlockSpec(memory_space=pltpu.SMEM)]
        + [pl.BlockSpec(memory_space=pltpu.VMEM)] * len(pieces),
        out_specs=[pl.BlockSpec(memory_space=pltpu.VMEM)] * outputs,
        cost_estimate=pl.CostEstimate(
            flops=len(pieces) * rows * LANES,
            bytes_accessed=4 * (len(pieces) + 1) * rows * LANES,
            transcendentals=0,
        ),
        name="add_pieces",
    )(index, *pieces)


def finish_kernel(place_ref, *refs, lon_count, depth):
    hidden_ref, bias_ref, out_ref, flat_ref = refs[2 * lon_count :]
    core, lon, deep = place_ref[0], place_ref[1], place_ref[2]
    size = refs[0].shape[0] // depth
    for half in range(2):
        for part in range(lon_count):
            for piece in range(depth):
                start = (((core ^ half) * lon_count + (lon ^ part)) * depth + (deep ^ piece)) * size
                flat_ref[pl.ds(pl.multiple_of(start, SUBS), size), :] = refs[
                    half * lon_count + part
                ][pl.ds(piece * size, size), :]
    width = hidden_ref.shape[0]
    tiles = width // LANES
    for row_tile in range(width // SUBS):
        for tile in range(tiles):
            hidden_ref[pl.ds(row_tile * SUBS, SUBS), pl.ds(tile * LANES, LANES)] = flat_ref[
                pl.ds((row_tile * tiles + tile) * SUBS, SUBS), :
            ]
    base = width * tiles
    for tile in range(tiles):
        out_ref[:, pl.ds(tile * LANES, LANES)] = flat_ref[pl.ds(base + tile * F, F), :]
        bias_ref[:, pl.ds(tile * LANES, LANES)] = flat_ref[pl.ds(base + tiles * F + tile, 1), :]


def finish(place, pieces, width, depth):
    lon_count = len(pieces) // 2
    return pl.pallas_call(
        functools.partial(finish_kernel, lon_count=lon_count, depth=depth),
        out_shape=(
            jax.ShapeDtypeStruct((width, width), jnp.float32),
            jax.ShapeDtypeStruct((1, width), jnp.float32),
            jax.ShapeDtypeStruct((F, width), jnp.float32),
        ),
        in_specs=[pl.BlockSpec(memory_space=pltpu.SMEM)]
        + [pl.BlockSpec(memory_space=pltpu.VMEM)] * len(pieces),
        out_specs=(pl.BlockSpec(memory_space=pltpu.VMEM),) * 3,
        scratch_shapes=[pltpu.VMEM((len(pieces) * pieces[0].shape[0], LANES), jnp.float32)],
        name="finish",
    )(place, *pieces)


def swap(value, axis, bits):
    count = lax.axis_size(axis)
    return lax.ppermute(value, axis, [(i, i ^ bits) for i in range(count)])


def local(spectra, field_slot, field_weight, latents, w_hidden, b_hidden, w_out):
    slot_count, _, pair_count, _ = spectra.shape
    lat_rows, lon_cols, width = latents.shape
    lat_count = lax.axis_size("lat")
    lon_count = lax.axis_size("lon")
    rows_all = lat_rows * lat_count
    lat_index = lax.axis_index("lat").astype(jnp.int32)
    lon_index = lax.axis_index("lon").astype(jnp.int32)
    pair_pad = pad_to(pair_count, SUBS)
    cells = lat_rows * lon_cols
    parts = 4

    coeffs = coefficients(spectra, (lon_index * pair_count).reshape(1), rows_all, lat_rows)
    share = slot_count * lat_rows // lon_count
    coeffs = coeffs.reshape(lat_count * lon_count, share, 4 * pair_pad)
    coeffs = lax.all_to_all(coeffs, ("lat", "lon"), split_axis=0, concat_axis=0, tiled=True)

    slope, hidden_t, latents_t = forward(
        latents.reshape(cells, width), w_hidden, b_hidden, parts
    )
    trig = trig_table(pair_count, lon_count)

    lanes = lat_count * share

    def spread(values):
        values = jnp.broadcast_to(values, (lat_count, slot_count, lat_rows))
        values = values.reshape(lat_count, lon_count, share)
        return jnp.transpose(values, (1, 0, 2)).reshape(lon_count, lanes)

    field_ids = spread(field_slot.reshape(lat_count, slot_count, 1))
    row_ids = spread(jnp.arange(lat_rows, dtype=jnp.int32).reshape(1, 1, lat_rows))
    chosen = field_ids[:, :, None] == jnp.arange(F, dtype=jnp.int32)
    weight = jnp.sum(jnp.where(chosen, field_weight, 0.0), axis=2)
    sine = jnp.sin(band_angles(lat_index * lat_rows + row_ids, rows_all))
    scale = (sine * weight)[:, None, :]
    target = row_ids * LANES + field_ids
    place = (
        target[:, :, None] == jnp.arange(lat_rows * LANES, dtype=jnp.int32)[None, None, :]
    ).astype(jnp.bfloat16)
    w_out_t = jnp.concatenate([w_out.T, jnp.zeros((LANES - F, width), w_out.dtype)], axis=0)

    core_index, deep_index = lat_index & 1, lat_index >> 1
    spots = jnp.stack([core_index, lon_index, deep_index])
    coeffs, slope, hidden_t, latents_t, trig, scale, place, w_out_t, spots = (
        lax.optimization_barrier(
            (coeffs, slope, hidden_t, latents_t, trig, scale, place, w_out_t, spots)
        )
    )
    grid = grid_field(trig, coeffs, pair_count).reshape(lon_count, lon_cols, lanes)
    grid = lax.all_to_all(grid, "lon", split_axis=0, concat_axis=0, tiled=True)

    device_count = lat_count * lon_count
    used_rows = (width + F + 1) * width // LANES
    chunk = pad_to(pad_to(used_rows, device_count) // device_count, SUBS)
    depth = lat_count // 2
    preact_back, keep, send = backward(
        core_index.reshape(1), grid, scale, place, w_out_t, slope, hidden_t, latents_t,
        chunk * device_count,
    )
    latent_grad = lax.dot_general(
        preact_back, w_hidden, (((1,), (1,)), ((), ())), preferred_element_type=jnp.float32
    ).astype(jnp.bfloat16)

    pieces = add_pieces(
        lon_index.reshape(1), [keep, swap(send, "lat", 1)], lon_count
    )
    arrived = [swap(pieces[part], "lon", part) for part in range(1, lon_count)]
    arrived, latent_grad = lax.optimization_barrier((arrived, latent_grad))
    pieces = add_pieces(deep_index.reshape(1), [pieces[0]] + arrived, depth)
    arrived = [swap(pieces[part], "lat", 2 * part) for part in range(1, depth)]
    norm = 1.0 / math.sqrt(rows_all * NLON)
    total = add_pieces(deep_index.reshape(1), [pieces[0]] + arrived, 1, norm)[0]
    total = jnp.concatenate([total] + [swap(total, "lat", 2 * part) for part in range(1, depth)])
    totals = [total] + [swap(total, "lon", part) for part in range(1, lon_count)]
    totals = totals + [swap(piece, "lat", 1) for piece in totals]
    hidden_grad, bias_grad, out_grad = finish(spots, totals, width, depth)
    return (
        latent_grad.reshape(lat_rows, lon_cols, width),
        hidden_grad,
        bias_grad.reshape(width),
        out_grad.T,
    )


def solution(mesh):
    in_specs = (P("lat", None, "lon", None), P(), P(), P("lat", "lon", None), P(), P(), P())
    out_specs = (P("lat", "lon", None), P(), P(), P())
    return jax.shard_map(local, mesh=mesh, in_specs=in_specs, out_specs=out_specs, check_vma=False)
```

```python
import functools
import math

import jax
import jax.numpy as jnp
from jax import lax
from jax.experimental import pallas as pl
from jax.experimental.pallas import tpu as pltpu
from jax.sharding import PartitionSpec as P

NM = 720
NLON = 1440
F = 64
LANES = 128
SUBS = 8
STEPS = NM + 1
PAIRS = 4
TABLE_ROWS = 728
MIB = 1024 * 1024
VMEM_LIMIT = 56 * MIB


def band_angles(row_ids, rows_all):
    return jnp.pi * (NM // 2 - rows_all // 2 + row_ids.astype(jnp.float32)) / NM


def pad_to(value, multiple):
    return (value + multiple - 1) // multiple * multiple


def coeff_kernel(
    first_ref, spectra_hbm, out_ref, spectra_ref, grow_ref, factor_ref, scale_ref, table_ref,
    stage_ref, copy_sem, *, pair_count, rows_all, lat_rows, slot_count,
):
    per_block = LANES // rows_all
    vregs = pad_to(pair_count, SUBS * per_block) // (SUBS * per_block)
    step_tile = rows_all
    pair_pad = pad_to(pair_count, SUBS)
    lat_count = rows_all // lat_rows
    first_pair = first_ref[0]

    fetch = pltpu.make_async_copy(spectra_hbm, spectra_ref, copy_sem)
    fetch.start()

    lane = lax.broadcasted_iota(jnp.int32, (SUBS, LANES), 1)
    sub = lax.broadcasted_iota(jnp.int32, (SUBS, LANES), 0)
    inner = lane & (rows_all - 1)
    which = lane // rows_all
    colatitude = band_angles(inner, rows_all)
    cosine = jnp.cos(colatitude)
    log_sine = jnp.log(jnp.sin(colatitude))

    def log_total(order_column):
        total = jnp.zeros((SUBS, LANES), jnp.float32)
        for tile in range(pad_to(NM, LANES) // LANES):
            term = (lane + tile * LANES).astype(jnp.float32)
            safe = jnp.maximum(term, 1.0)
            value = jnp.log((2.0 * safe + 1.0) / (2.0 * safe))
            total = total + jnp.where((term >= 1.0) & (term <= order_column), value, 0.0)
        return jnp.sum(total, axis=1, keepdims=True)

    def seed(order_of):
        total = jnp.zeros((SUBS, LANES), jnp.float32)
        for part in range(per_block):
            column = order_of(part).astype(jnp.float32)
            total = jnp.where(which == part, log_total(column), total)
        order = order_of(which).astype(jnp.float32)
        return jnp.exp(0.5 * total - 0.5 * math.log(4.0 * math.pi) + order * log_sine)

    pairs = vregs * SUBS * per_block
    steps_pad = pad_to(STEPS, LANES)
    step = lax.broadcasted_iota(jnp.int32, (pairs, steps_pad), 1)
    pair = first_pair + lax.broadcasted_iota(jnp.int32, (pairs, steps_pad), 0)
    switch = NM - pair
    in_first = step < switch
    order = jnp.where(in_first, pair, NM - 1 - pair).astype(jnp.float32)
    degree = jnp.where(in_first, pair + step, step - 1).astype(jnp.float32)
    grow = jnp.sqrt(
        jnp.maximum(4.0 * degree * degree - 1.0, 1.0)
        / jnp.maximum(degree * degree - order * order, 1.0)
    )
    since = jnp.where(in_first, step, step - switch)
    scale = jnp.where(since >= 2, grow / pltpu.roll(grow, 1, 1), 1.0)
    shift = 2
    while shift < STEPS:
        scale = jnp.where(since >= shift, scale * pltpu.roll(scale, shift, 1), scale)
        shift = 2 * shift
    factor = grow * pltpu.roll(scale, 1, 1) / scale
    for tile in range(steps_pad // LANES):
        factor_ref[tile] = factor[:, tile * LANES : (tile + 1) * LANES]
        for row in range(0, pairs, SUBS):
            piece = scale[row : row + SUBS, tile * LANES : (tile + 1) * LANES]
            for part in range(2):
                scale_ref[tile, pl.ds(2 * row + part, SUBS, stride=2), :] = piece

    firsts, seconds, switches = [], [], []
    for v in range(vregs):
        base = first_pair + (sub + v * SUBS) * per_block

        def order_first(part, base=base):
            return base + part

        def order_second(part, base=base):
            return NM - 1 - (base + part)

        firsts.append(seed(order_first))
        seconds.append(seed(order_second))
        switches.append(NM - (base + which))
        rows = pl.ds(v * SUBS, SUBS)
        for tile in range(steps_pad // LANES):
            if per_block == 1:
                grow_ref[tile, rows, :] = factor_ref[tile, rows, :]
            else:
                even = factor_ref[tile, pl.ds(2 * v * SUBS, SUBS, stride=2), :]
                odd = factor_ref[tile, pl.ds(2 * v * SUBS + 1, SUBS, stride=2), :]
                low = lane < rows_all
                grow_ref[2 * tile, rows, :] = jnp.where(low, even, pltpu.roll(odd, rows_all, 1))
                grow_ref[2 * tile + 1, rows, :] = jnp.where(
                    low, pltpu.roll(even, rows_all, 1), odd
                )

    def advance(tile, offset, state, grows):
        previous, before = state
        index = which * rows_all + offset
        step = tile * step_tile + offset
        produced, kept = [], []
        for v in range(vregs):
            grow = jnp.take_along_axis(grows[v], index, axis=1)
            value = (grow * cosine) * previous[v] - before[v]
            restart = switches[v] == step
            value = jnp.where(restart, seconds[v], value)
            table_ref[pl.ds(v * SUBS * TABLE_ROWS + step, SUBS, stride=TABLE_ROWS), :] = value
            produced.append(value)
            kept.append(jnp.where(restart, 0.0, previous[v]))
        return (tuple(produced), tuple(kept))

    def run_tile(tile, state, count, unroll):
        grows = [grow_ref[tile, pl.ds(v * SUBS, SUBS), :] for v in range(vregs)]

        def body(offset, carry):
            return advance(tile, offset, carry, grows)

        return lax.fori_loop(0, count, body, state, unroll=unroll)

    zeros = tuple(jnp.zeros((SUBS, LANES), jnp.float32) for _ in range(vregs))
    state = (zeros, tuple(-value for value in firsts))
    whole_tiles = STEPS // step_tile
    state = lax.fori_loop(
        0, whole_tiles, lambda tile, carry: run_tile(tile, carry, step_tile, 8), state
    )
    if STEPS % step_tile:
        run_tile(whole_tiles, state, STEPS % step_tile, STEPS % step_tile % 16)

    for row in range(slot_count):
        for half in range(2):
            stage_ref[row, pl.ds((half + 1) * 2 * pair_pad - 2 * SUBS, 2 * SUBS), :] = jnp.zeros(
                (2 * SUBS, LANES), jnp.float32
            )
    fetch.wait()

    rows_half = slot_count * SUBS
    edges = (0, 256, 512, STEPS)
    dot = functools.partial(jnp.dot, preferred_element_type=jnp.float32)

    def split_parts(values):
        high = values.astype(jnp.bfloat16)
        low = (values - high.astype(jnp.float32)).astype(jnp.bfloat16)
        return high, low

    def product(left, right):
        left_high, left_low = split_parts(left)
        right_high, right_low = split_parts(right)
        rows = left.shape[0]
        both = dot(jnp.concatenate([left_high, left_low], axis=0), right_high)
        return both[:rows] + both[rows:] + dot(left_high, right_low)

    def group(start):
        values = spectra_ref[:, pl.ds(start, PAIRS), :, :].reshape(slot_count, SUBS, STEPS)
        scale = jnp.concatenate(
            [scale_ref[tile, pl.ds(2 * start, SUBS), :] for tile in range(scale_ref.shape[0])],
            axis=1,
        )
        values = values * scale[:, :STEPS]
        step = lax.broadcasted_iota(jnp.int32, (1, SUBS, STEPS), 2)
        row_pair = lax.broadcasted_iota(jnp.int32, (1, SUBS, STEPS), 1) // 2
        in_first = step < NM - (first_pair + start + row_pair)
        lower = jnp.where(in_first, values, 0.0)
        upper = jnp.where(in_first, 0.0, values)
        first_block = start // per_block
        blocks = PAIRS // per_block
        table = jnp.concatenate(
            [table_ref[pl.ds((first_block + n) * TABLE_ROWS, STEPS), :] for n in range(blocks)],
            axis=1,
        )
        begin, end = edges[0], edges[1]
        base = product(
            values[:, :, begin:end].reshape(rows_half, end - begin), table[begin:end]
        )
        rest = None
        for begin, end in zip(edges[1:-1], edges[2:]):
            left = jnp.concatenate([lower[:, :, begin:end], upper[:, :, begin:end]], axis=0)
            part = product(left.reshape(2 * rows_half, end - begin), table[begin:end])
            rest = part if rest is None else rest + part
        both = jnp.concatenate([rest[:rows_half] + base, rest[rows_half:]], axis=0)
        row_id = lax.broadcasted_iota(jnp.int32, (2 * rows_half, LANES), 0) % SUBS // 2
        lane_part = lax.broadcasted_iota(jnp.int32, (2 * rows_half, LANES), 1) // rows_all
        total = jnp.zeros((2 * rows_half, LANES), jnp.float32)
        for block in range(blocks):
            keep = row_id == block * per_block + lane_part
            total = total + jnp.where(keep, both[:, block * LANES : (block + 1) * LANES], 0.0)
        if per_block == 2:
            total = total + pltpu.roll(total, rows_all, 1)
        total = total.astype(jnp.bfloat16).astype(jnp.float32)
        for half in range(2):
            for row in range(slot_count):
                source = (half * slot_count + row) * SUBS
                stage_ref[row, pl.ds(half * 2 * pair_pad + 2 * start, SUBS), :] = total[
                    source : source + SUBS
                ]

    def group_body(index, carry):
        group(index * PAIRS)
        return carry

    lax.fori_loop(0, pair_count // PAIRS, group_body, 0)
    if pair_count % PAIRS:
        group(pair_count - PAIRS)

    for row in range(slot_count):
        flipped = stage_ref[row].T
        out_ref[:, pl.ds(row * lat_rows, lat_rows), :] = flipped[:rows_all].reshape(
            lat_count, lat_rows, 4 * pair_pad
        )


def coefficients(spectra, first_pair, rows_all, lat_rows):
    slot_count, _, pair_count, steps = spectra.shape
    per_block = LANES // rows_all
    vregs = pad_to(pair_count, SUBS * per_block) // (SUBS * per_block)
    pairs = vregs * SUBS * per_block
    tile_total = pad_to(STEPS, LANES) // rows_all
    pair_pad = pad_to(pair_count, SUBS)
    lat_count = rows_all // lat_rows
    kernel = functools.partial(
        coeff_kernel, pair_count=pair_count, rows_all=rows_all, lat_rows=lat_rows,
        slot_count=slot_count,
    )
    return pl.pallas_call(
        kernel,
        out_shape=jax.ShapeDtypeStruct(
            (lat_count, slot_count * lat_rows, 4 * pair_pad), jnp.float32
        ),
        in_specs=[
            pl.BlockSpec(memory_space=pltpu.SMEM),
            pl.BlockSpec(memory_space=pl.ANY),
        ],
        out_specs=pl.BlockSpec(memory_space=pltpu.VMEM),
        scratch_shapes=[
            pltpu.VMEM((slot_count, pair_count, 2, steps), jnp.float32),
            pltpu.VMEM((tile_total, vregs * SUBS, LANES), jnp.float32),
            pltpu.VMEM((pad_to(STEPS, LANES) // LANES, pairs, LANES), jnp.float32),
            pltpu.VMEM((pad_to(STEPS, LANES) // LANES, 2 * pairs, LANES), jnp.float32),
            pltpu.VMEM((vregs * SUBS * TABLE_ROWS, LANES), jnp.float32),
            pltpu.VMEM((slot_count, 4 * pair_pad, LANES), jnp.float32),
            pltpu.SemaphoreType.DMA,
        ],
        compiler_params=pltpu.CompilerParams(vmem_limit_bytes=VMEM_LIMIT),
        name="coefficients",
    )(first_pair, jnp.transpose(spectra, (0, 2, 1, 3)))


def trig_kernel(out_ref, *, pair_count, pair_pad, quarter, fine_total):
    block = pl.program_id(0)
    width = 4 * pair_pad
    coarse_total = pad_to(quarter // fine_total, SUBS)

    def orders(rows):
        lane = lax.broadcasted_iota(jnp.int32, (rows, width), 1)
        upper = lane >= 2 * pair_pad
        pair = jnp.where(upper, lane - 2 * pair_pad, lane)
        is_sine = (pair & 1) == 1
        pair = block * pair_count + (pair >> 1)
        return jnp.where(upper, NM - 1 - pair, pair), is_sine

    def angles(rows, spacing):
        order, _ = orders(rows)
        column = lax.broadcasted_iota(jnp.int32, (rows, width), 0) * spacing
        phase = (order * column % NLON).astype(jnp.float32) * (2.0 * math.pi / NLON)
        return jnp.cos(phase), jnp.sin(phase)

    fine_cos, fine_sin = angles(fine_total, 1)
    coarse_cos, coarse_sin = angles(coarse_total, fine_total)
    _, is_sine = orders(fine_total)
    for tile in range(quarter // fine_total):
        left, right = coarse_cos[tile : tile + 1], coarse_sin[tile : tile + 1]
        cosine = left * fine_cos - right * fine_sin
        sine = right * fine_cos + left * fine_sin
        out_ref[pl.ds(tile * fine_total, fine_total), :] = jnp.where(
            is_sine, sine, cosine
        ).astype(jnp.bfloat16)


def trig_table(pair_count, lon_count):
    pair_pad = pad_to(pair_count, SUBS)
    quarter = NLON // 4
    fine_total = 40
    return pl.pallas_call(
        functools.partial(
            trig_kernel, pair_count=pair_count, pair_pad=pair_pad, quarter=quarter,
            fine_total=fine_total,
        ),
        grid=(lon_count,),
        out_shape=jax.ShapeDtypeStruct((lon_count, quarter, 4 * pair_pad), jnp.bfloat16),
        out_specs=pl.BlockSpec((None, quarter, 4 * pair_pad), lambda b: (b, 0, 0)),
        compiler_params=pltpu.CompilerParams(vmem_limit_bytes=VMEM_LIMIT),
        cost_estimate=pl.CostEstimate(
            flops=24 * lon_count * quarter * pair_pad,
            bytes_accessed=lon_count * quarter * 8 * pair_pad,
            transcendentals=0,
        ),
        name="trig_table",
    )()


def grid_kernel(trig_ref, coeff_ref, out_ref, right_ref, *, lon_count, pair_count):
    share = coeff_ref.shape[1]
    width = coeff_ref.shape[2]
    rows = coeff_ref.shape[0] // lon_count * share
    values = coeff_ref[...].reshape(rows // share, lon_count, share, width)
    line = lax.broadcasted_iota(jnp.int32, (width, rows), 0)
    upper = line >= width // 2
    pair = jnp.where(upper, line - width // 2, line)
    is_sine = (pair & 1) == 1
    for block in range(lon_count):
        flat = values[:, block].reshape(rows, width).T
        swapped = jnp.where(is_sine, -pltpu.roll(flat, 1, 0), pltpu.roll(flat, width - 1, 0))
        order = block * pair_count + (pair >> 1)
        order = jnp.where(upper, NM - 1 - order, order) & 3
        odd = (order & 1) == 1
        flip = jnp.where(odd, -flat, flat)
        turned = jnp.where(order == 1, swapped, jnp.where(order == 3, -swapped, flat))
        turned = jnp.where(order == 2, -flat, turned)
        back = jnp.where(odd, -turned, turned)
        for turn, part in enumerate((flat, turned, flip, back)):
            right_ref[pl.ds(block * width, width), pl.ds(turn * rows, rows)] = part.astype(
                jnp.bfloat16
            )
    total = None
    for block in range(lon_count):
        part = jnp.dot(
            trig_ref[block],
            right_ref[pl.ds(block * width, width), :],
            preferred_element_type=jnp.float32,
        )
        total = part if total is None else total + part
    for turn in range(4):
        out_ref[turn] = total[:, turn * rows : (turn + 1) * rows]


def grid_field(trig, coeffs, pair_count):
    lon_count, quarter, width = trig.shape
    rows = coeffs.shape[0] // lon_count * coeffs.shape[1]
    return pl.pallas_call(
        functools.partial(grid_kernel, lon_count=lon_count, pair_count=pair_count),
        out_shape=jax.ShapeDtypeStruct((4, quarter, rows), jnp.float32),
        scratch_shapes=[pltpu.VMEM((lon_count * width, 4 * rows), jnp.bfloat16)],
        compiler_params=pltpu.CompilerParams(vmem_limit_bytes=16 * MIB),
        cost_estimate=pl.CostEstimate(
            flops=2 * NLON * lon_count * width * rows,
            bytes_accessed=trig.size * 2 + 2 * coeffs.size * 4,
            transcendentals=0,
        ),
        name="grid_field",
    )(trig, coeffs)


def gelu_parts(preact):
    scale = math.sqrt(2.0 / math.pi)
    square = preact * preact
    bend = jnp.tanh(scale * (preact + 0.044715 * (square * preact)))
    half = 0.5 * (1.0 + bend)
    slope = half + (0.5 * preact) * (1.0 - bend * bend) * (
        scale * (1.0 + (3.0 * 0.044715) * square)
    )
    return preact * half, slope


def forward_kernel(latents_ref, w_ref, b_ref, slope_ref, hidden_t_ref, latents_t_ref):
    latents = latents_ref[...]
    preact = jnp.dot(latents, w_ref[...], preferred_element_type=jnp.float32) + b_ref[...]
    hidden, slope = gelu_parts(preact)
    slope_ref[...] = slope
    hidden_t_ref[...] = hidden.T.astype(jnp.bfloat16)
    latents_t_ref[...] = latents.T


def forward(latents, w_hidden, b_hidden, parts):
    cells, width = latents.shape
    cols = cells // parts
    return pl.pallas_call(
        forward_kernel,
        grid=(parts,),
        out_shape=(
            jax.ShapeDtypeStruct((cells, width), jnp.float32),
            jax.ShapeDtypeStruct((parts, width, cols), jnp.bfloat16),
            jax.ShapeDtypeStruct((parts, width, cols), jnp.bfloat16),
        ),
        in_specs=[
            pl.BlockSpec((cols, width), lambda i: (i, 0)),
            pl.BlockSpec((width, width), lambda i: (0, 0)),
            pl.BlockSpec((1, width), lambda i: (0, 0)),
        ],
        out_specs=(
            pl.BlockSpec((cols, width), lambda i: (i, 0)),
            pl.BlockSpec((None, width, cols), lambda i: (i, 0, 0)),
            pl.BlockSpec((None, width, cols), lambda i: (i, 0, 0)),
        ),
        compiler_params=pltpu.CompilerParams(vmem_limit_bytes=32 * MIB),
        cost_estimate=pl.CostEstimate(
            flops=2 * cells * width * width,
            bytes_accessed=cells * width * 10,
            transcendentals=cells * width,
        ),
        name="forward",
    )(latents, w_hidden, b_hidden.reshape(1, width))


def backward_kernel(
    core_ref, grid_ref, scale_ref, place_ref, w_out_ref, slope_ref, hidden_t_ref, latents_t_ref,
    preact_ref, keep_ref, send_ref, field_ref, hidden_acc, out_acc, bias_acc, sums_ref,
):
    index = pl.program_id(0)
    total = pl.num_programs(0)
    blocks = grid_ref.shape[0]
    lon_cols = grid_ref.shape[1]
    width = hidden_acc.shape[0]
    cols = slope_ref.shape[0]
    sum_rows = sums_ref.shape[0]

    @pl.when(index == 0)
    def _():
        field = None
        for block in range(blocks):
            scaled = (grid_ref[block] * scale_ref[block]).astype(jnp.bfloat16)
            part = jnp.dot(scaled, place_ref[block], preferred_element_type=jnp.float32)
            field = part if field is None else field + part
        for row in range(field.shape[1] // LANES):
            field_ref[pl.ds(row * lon_cols, lon_cols), :] = field[
                :, row * LANES : (row + 1) * LANES
            ]
        hidden_acc[...] = jnp.zeros_like(hidden_acc)
        out_acc[...] = jnp.zeros_like(out_acc)
        bias_acc[...] = jnp.zeros_like(bias_acc)

    field = field_ref[pl.ds(pl.multiple_of(index * cols, SUBS), cols), :].astype(jnp.bfloat16)
    back = jnp.dot(field, w_out_ref[...], preferred_element_type=jnp.float32)
    preact_back = (back * slope_ref[...]).astype(jnp.bfloat16)
    preact_ref[...] = preact_back
    hidden_acc[...] += jnp.dot(
        latents_t_ref[...], preact_back, preferred_element_type=jnp.float32
    )
    out_acc[...] += jnp.dot(hidden_t_ref[...], field, preferred_element_type=jnp.float32)
    bias_acc[...] += jnp.sum(preact_back.astype(jnp.float32), axis=0, keepdims=True)

    @pl.when(index == total - 1)
    def _():
        tiles = width // LANES
        for row_tile in range(width // SUBS):
            for tile in range(tiles):
                sums_ref[pl.ds((row_tile * tiles + tile) * SUBS, SUBS), :] = hidden_acc[
                    pl.ds(row_tile * SUBS, SUBS), pl.ds(tile * LANES, LANES)
                ]
        base = width * tiles
        flipped = out_acc[...].T
        for tile in range(tiles):
            sums_ref[pl.ds(base + tile * F, F), :] = flipped[:F, tile * LANES : (tile + 1) * LANES]
        base = base + tiles * F
        sums_ref[pl.ds(base, sum_rows - base), :] = jnp.zeros((sum_rows - base, LANES), jnp.float32)
        for tile in range(tiles):
            sums_ref[pl.ds(base + tile, 1), :] = bias_acc[:, tile * LANES : (tile + 1) * LANES]
        half = sum_rows // 2
        mine = core_ref[0]
        keep_ref[...] = sums_ref[pl.ds(pl.multiple_of(mine * half, SUBS), half), :]
        send_ref[...] = sums_ref[pl.ds(pl.multiple_of((1 - mine) * half, SUBS), half), :]


def backward(core, grid, scale, place, w_out_t, slope, hidden_t, latents_t, sum_rows):
    cells, width = slope.shape
    parts, _, cols = hidden_t.shape
    half = (sum_rows // 2, LANES)
    whole3 = lambda i: (0, 0, 0)
    whole2 = lambda i: (0, 0)
    return pl.pallas_call(
        backward_kernel,
        grid=(parts,),
        out_shape=(
            jax.ShapeDtypeStruct((cells, width), jnp.bfloat16),
            jax.ShapeDtypeStruct(half, jnp.float32),
            jax.ShapeDtypeStruct(half, jnp.float32),
        ),
        in_specs=[
            pl.BlockSpec(memory_space=pltpu.SMEM),
            pl.BlockSpec(grid.shape, whole3),
            pl.BlockSpec(scale.shape, whole3),
            pl.BlockSpec(place.shape, whole3),
            pl.BlockSpec(w_out_t.shape, whole2),
            pl.BlockSpec((cols, width), lambda i: (i, 0)),
            pl.BlockSpec((None, width, cols), lambda i: (i, 0, 0)),
            pl.BlockSpec((None, width, cols), lambda i: (i, 0, 0)),
        ],
        out_specs=(
            pl.BlockSpec((cols, width), lambda i: (i, 0)),
            pl.BlockSpec(half, whole2),
            pl.BlockSpec(half, whole2),
        ),
        scratch_shapes=[
            pltpu.VMEM((cells, LANES), jnp.float32),
            pltpu.VMEM((width, width), jnp.float32),
            pltpu.VMEM((width, LANES), jnp.float32),
            pltpu.VMEM((1, width), jnp.float32),
            pltpu.VMEM((sum_rows, LANES), jnp.float32),
        ],
        compiler_params=pltpu.CompilerParams(vmem_limit_bytes=32 * MIB),
        cost_estimate=pl.CostEstimate(
            flops=2 * cells * width * (width + 2 * LANES),
            bytes_accessed=cells * width * 10,
            transcendentals=0,
        ),
        name="backward",
    )(core, grid, scale, place, w_out_t, slope, hidden_t, latents_t)


def add_kernel(index_ref, *refs, inputs, outputs, factor):
    size = refs[0].shape[0] // outputs
    for part in range(outputs):
        start = 0 if outputs == 1 else pl.multiple_of((index_ref[0] ^ part) * size, SUBS)
        total = refs[0][pl.ds(start, size), :]
        for piece in refs[1:inputs]:
            total = total + piece[pl.ds(start, size), :]
        if factor is not None:
            total = total * factor
        refs[inputs + part][...] = total


def add_pieces(index, pieces, outputs, factor=None):
    rows = pieces[0].shape[0]
    size = rows // outputs
    return pl.pallas_call(
        functools.partial(add_kernel, inputs=len(pieces), outputs=outputs, factor=factor),
        out_shape=[jax.ShapeDtypeStruct((size, LANES), jnp.float32)] * outputs,
        in_specs=[pl.BlockSpec(memory_space=pltpu.SMEM)]
        + [pl.BlockSpec(memory_space=pltpu.VMEM)] * len(pieces),
        out_specs=[pl.BlockSpec(memory_space=pltpu.VMEM)] * outputs,
        cost_estimate=pl.CostEstimate(
            flops=len(pieces) * rows * LANES,
            bytes_accessed=4 * (len(pieces) + 1) * rows * LANES,
            transcendentals=0,
        ),
        compiler_params=pltpu.CompilerParams(vmem_limit_bytes=6 * MIB),
        name="add_pieces",
    )(index, *pieces)


def finish_kernel(place_ref, *refs, lon_count, depth):
    hidden_ref, bias_ref, out_ref, flat_ref = refs[2 * lon_count :]
    core, lon, deep = place_ref[0], place_ref[1], place_ref[2]
    size = refs[0].shape[0] // depth
    for half in range(2):
        for part in range(lon_count):
            for piece in range(depth):
                start = (((core ^ half) * lon_count + (lon ^ part)) * depth + (deep ^ piece)) * size
                flat_ref[pl.ds(pl.multiple_of(start, SUBS), size), :] = refs[
                    half * lon_count + part
                ][pl.ds(piece * size, size), :]
    width = hidden_ref.shape[0]
    tiles = width // LANES
    for row_tile in range(width // SUBS):
        for tile in range(tiles):
            hidden_ref[pl.ds(row_tile * SUBS, SUBS), pl.ds(tile * LANES, LANES)] = flat_ref[
                pl.ds((row_tile * tiles + tile) * SUBS, SUBS), :
            ]
    base = width * tiles
    for tile in range(tiles):
        out_ref[:, pl.ds(tile * LANES, LANES)] = flat_ref[pl.ds(base + tile * F, F), :]
        bias_ref[:, pl.ds(tile * LANES, LANES)] = flat_ref[pl.ds(base + tiles * F + tile, 1), :]


def finish(place, pieces, width, depth):
    lon_count = len(pieces) // 2
    return pl.pallas_call(
        functools.partial(finish_kernel, lon_count=lon_count, depth=depth),
        out_shape=(
            jax.ShapeDtypeStruct((width, width), jnp.float32),
            jax.ShapeDtypeStruct((1, width), jnp.float32),
            jax.ShapeDtypeStruct((F, width), jnp.float32),
        ),
        in_specs=[pl.BlockSpec(memory_space=pltpu.SMEM)]
        + [pl.BlockSpec(memory_space=pltpu.VMEM)] * len(pieces),
        out_specs=(pl.BlockSpec(memory_space=pltpu.VMEM),) * 3,
        scratch_shapes=[pltpu.VMEM((len(pieces) * pieces[0].shape[0], LANES), jnp.float32)],
        compiler_params=pltpu.CompilerParams(vmem_limit_bytes=8 * MIB),
        name="finish",
    )(place, *pieces)


def swap(value, axis, bits):
    count = lax.axis_size(axis)
    return lax.ppermute(value, axis, [(i, i ^ bits) for i in range(count)])


def local(spectra, field_slot, field_weight, latents, w_hidden, b_hidden, w_out):
    slot_count, _, pair_count, _ = spectra.shape
    lat_rows, lon_cols, width = latents.shape
    lat_count = lax.axis_size("lat")
    lon_count = lax.axis_size("lon")
    rows_all = lat_rows * lat_count
    lat_index = lax.axis_index("lat").astype(jnp.int32)
    lon_index = lax.axis_index("lon").astype(jnp.int32)
    pair_pad = pad_to(pair_count, SUBS)
    cells = lat_rows * lon_cols
    parts = 4

    coeffs = coefficients(spectra, (lon_index * pair_count).reshape(1), rows_all, lat_rows)
    share = slot_count * lat_rows // lon_count
    coeffs = coeffs.reshape(lat_count * lon_count, share, 4 * pair_pad)
    coeffs = lax.all_to_all(coeffs, ("lat", "lon"), split_axis=0, concat_axis=0, tiled=True)

    slope, hidden_t, latents_t = forward(
        latents.reshape(cells, width), w_hidden, b_hidden, parts
    )
    trig = trig_table(pair_count, lon_count)

    lanes = lat_count * share

    def spread(values):
        values = jnp.broadcast_to(values, (lat_count, slot_count, lat_rows))
        values = values.reshape(lat_count, lon_count, share)
        return jnp.transpose(values, (1, 0, 2)).reshape(lon_count, lanes)

    field_ids = spread(field_slot.reshape(lat_count, slot_count, 1))
    row_ids = spread(jnp.arange(lat_rows, dtype=jnp.int32).reshape(1, 1, lat_rows))
    chosen = field_ids[:, :, None] == jnp.arange(F, dtype=jnp.int32)
    weight = jnp.sum(jnp.where(chosen, field_weight, 0.0), axis=2)
    sine = jnp.sin(band_angles(lat_index * lat_rows + row_ids, rows_all))
    scale = (sine * weight)[:, None, :]
    target = row_ids * LANES + field_ids
    place = (
        target[:, :, None] == jnp.arange(lat_rows * LANES, dtype=jnp.int32)[None, None, :]
    ).astype(jnp.bfloat16)
    w_out_t = jnp.concatenate([w_out.T, jnp.zeros((LANES - F, width), w_out.dtype)], axis=0)

    core_index, deep_index = lat_index & 1, lat_index >> 1
    spots = jnp.stack([core_index, lon_index, deep_index])
    coeffs, slope, hidden_t, latents_t, trig, scale, place, w_out_t, spots = (
        lax.optimization_barrier(
            (coeffs, slope, hidden_t, latents_t, trig, scale, place, w_out_t, spots)
        )
    )
    grid = grid_field(trig, coeffs, pair_count).reshape(lon_count, lon_cols, lanes)
    grid = lax.all_to_all(grid, "lon", split_axis=0, concat_axis=0, tiled=True)

    device_count = lat_count * lon_count
    used_rows = (width + F + 1) * width // LANES
    chunk = pad_to(pad_to(used_rows, device_count) // device_count, SUBS)
    depth = lat_count // 2
    preact_back, keep, send = backward(
        core_index.reshape(1), grid, scale, place, w_out_t, slope, hidden_t, latents_t,
        chunk * device_count,
    )
    latent_grad = lax.dot_general(
        preact_back, w_hidden, (((1,), (1,)), ((), ())), preferred_element_type=jnp.float32
    ).astype(jnp.bfloat16)

    pieces = add_pieces(
        lon_index.reshape(1), [keep, swap(send, "lat", 1)], lon_count
    )
    arrived = [swap(pieces[part], "lon", part) for part in range(1, lon_count)]
    arrived, latent_grad = lax.optimization_barrier((arrived, latent_grad))
    pieces = add_pieces(deep_index.reshape(1), [pieces[0]] + arrived, depth)
    arrived = [swap(pieces[part], "lat", 2 * part) for part in range(1, depth)]
    norm = 1.0 / math.sqrt(rows_all * NLON)
    total = add_pieces(deep_index.reshape(1), [pieces[0]] + arrived, 1, norm)[0]
    total = jnp.concatenate([total] + [swap(total, "lat", 2 * part) for part in range(1, depth)])
    totals = [total] + [swap(total, "lon", part) for part in range(1, lon_count)]
    totals = totals + [swap(piece, "lat", 1) for piece in totals]
    hidden_grad, bias_grad, out_grad = finish(spots, totals, width, depth)
    return (
        latent_grad.reshape(lat_rows, lon_cols, width),
        hidden_grad,
        bias_grad.reshape(width),
        out_grad.T,
    )


def solution(mesh):
    in_specs = (P("lat", None, "lon", None), P(), P(), P("lat", "lon", None), P(), P(), P())
    out_specs = (P("lat", "lon", None), P(), P(), P())
    return jax.shard_map(local, mesh=mesh, in_specs=in_specs, out_specs=out_specs, check_vma=False)
```

```python
import functools
import math

import jax
import jax.numpy as jnp
from jax import lax
from jax.experimental import pallas as pl
from jax.experimental.pallas import tpu as pltpu
from jax.sharding import PartitionSpec as P

NM = 720
NLON = 1440
F = 64
LANES = 128
SUBS = 8
STEPS = NM + 1
PAIRS = 4
MIB = 1024 * 1024
VMEM_LIMIT = 56 * MIB


def band_angles(row_ids, rows_all):
    return jnp.pi * (NM // 2 - rows_all // 2 + row_ids.astype(jnp.float32)) / NM


def pad_to(value, multiple):
    return (value + multiple - 1) // multiple * multiple


def coeff_kernel(
    first_ref, spectra_hbm, out_ref, spectra_ref, grow_ref, factor_ref, scale_ref, table_ref,
    stage_ref, copy_sem, *, pair_count, rows_all, lat_rows, slot_count,
):
    per_block = LANES // rows_all
    vregs = pad_to(pair_count, SUBS * per_block) // (SUBS * per_block)
    step_tile = rows_all
    stride = vregs * SUBS + 1
    pair_pad = pad_to(pair_count, SUBS)
    lat_count = rows_all // lat_rows
    first_pair = first_ref[0]

    fetch = pltpu.make_async_copy(spectra_hbm, spectra_ref, copy_sem)
    fetch.start()

    lane = lax.broadcasted_iota(jnp.int32, (SUBS, LANES), 1)
    sub = lax.broadcasted_iota(jnp.int32, (SUBS, LANES), 0)
    inner = lane & (rows_all - 1)
    which = lane // rows_all
    colatitude = band_angles(inner, rows_all)
    cosine = jnp.cos(colatitude)
    log_sine = jnp.log(jnp.sin(colatitude))

    def log_total(order_column):
        total = jnp.zeros((SUBS, LANES), jnp.float32)
        for tile in range(pad_to(NM, LANES) // LANES):
            term = (lane + tile * LANES).astype(jnp.float32)
            safe = jnp.maximum(term, 1.0)
            value = jnp.log((2.0 * safe + 1.0) / (2.0 * safe))
            total = total + jnp.where((term >= 1.0) & (term <= order_column), value, 0.0)
        return jnp.sum(total, axis=1, keepdims=True)

    def seed(order_of):
        total = jnp.zeros((SUBS, LANES), jnp.float32)
        for part in range(per_block):
            column = order_of(part).astype(jnp.float32)
            total = jnp.where(which == part, log_total(column), total)
        order = order_of(which).astype(jnp.float32)
        return jnp.exp(0.5 * total - 0.5 * math.log(4.0 * math.pi) + order * log_sine)

    pairs = vregs * SUBS * per_block
    steps_pad = pad_to(STEPS, LANES)
    step = lax.broadcasted_iota(jnp.int32, (pairs, steps_pad), 1)
    pair = first_pair + lax.broadcasted_iota(jnp.int32, (pairs, steps_pad), 0)
    switch = NM - pair
    in_first = step < switch
    order = jnp.where(in_first, pair, NM - 1 - pair).astype(jnp.float32)
    degree = jnp.where(in_first, pair + step, step - 1).astype(jnp.float32)
    grow = jnp.sqrt(
        jnp.maximum(4.0 * degree * degree - 1.0, 1.0)
        / jnp.maximum(degree * degree - order * order, 1.0)
    )
    since = jnp.where(in_first, step, step - switch)
    scale = jnp.where(since >= 2, grow / pltpu.roll(grow, 1, 1), 1.0)
    shift = 2
    while shift < STEPS:
        scale = jnp.where(since >= shift, scale * pltpu.roll(scale, shift, 1), scale)
        shift = 2 * shift
    factor = grow * pltpu.roll(scale, 1, 1) / scale
    for tile in range(steps_pad // LANES):
        factor_ref[tile] = factor[:, tile * LANES : (tile + 1) * LANES]
        for row in range(0, pairs, SUBS):
            piece = scale[row : row + SUBS, tile * LANES : (tile + 1) * LANES]
            for part in range(2):
                scale_ref[tile, pl.ds(2 * row + part, SUBS, stride=2), :] = piece

    firsts, seconds, switches = [], [], []
    for v in range(vregs):
        base = first_pair + (sub + v * SUBS) * per_block

        def order_first(part, base=base):
            return base + part

        def order_second(part, base=base):
            return NM - 1 - (base + part)

        firsts.append(seed(order_first))
        seconds.append(seed(order_second))
        switches.append(NM - (base + which))
        rows = pl.ds(v * SUBS, SUBS)
        for tile in range(steps_pad // LANES):
            if per_block == 1:
                grow_ref[tile, rows, :] = factor_ref[tile, rows, :]
            else:
                even = factor_ref[tile, pl.ds(2 * v * SUBS, SUBS, stride=2), :]
                odd = factor_ref[tile, pl.ds(2 * v * SUBS + 1, SUBS, stride=2), :]
                low = lane < rows_all
                grow_ref[2 * tile, rows, :] = jnp.where(low, even, pltpu.roll(odd, rows_all, 1))
                grow_ref[2 * tile + 1, rows, :] = jnp.where(
                    low, pltpu.roll(even, rows_all, 1), odd
                )

    def advance(tile, offset, state, grows):
        previous, before = state
        index = which * rows_all + offset
        step = tile * step_tile + offset
        produced, kept = [], []
        for v in range(vregs):
            grow = jnp.take_along_axis(grows[v], index, axis=1)
            value = (grow * cosine) * previous[v] - before[v]
            restart = switches[v] == step
            value = jnp.where(restart, seconds[v], value)
            table_ref[pl.ds(step * stride + v * SUBS, SUBS), :] = value
            produced.append(value)
            kept.append(jnp.where(restart, 0.0, previous[v]))
        return (tuple(produced), tuple(kept))

    def run_tile(tile, state, count, unroll):
        grows = [grow_ref[tile, pl.ds(v * SUBS, SUBS), :] for v in range(vregs)]

        def body(offset, carry):
            return advance(tile, offset, carry, grows)

        return lax.fori_loop(0, count, body, state, unroll=unroll)

    zeros = tuple(jnp.zeros((SUBS, LANES), jnp.float32) for _ in range(vregs))
    state = (zeros, tuple(-value for value in firsts))
    whole_tiles = STEPS // step_tile
    state = lax.fori_loop(
        0, whole_tiles, lambda tile, carry: run_tile(tile, carry, step_tile, 8), state
    )
    if STEPS % step_tile:
        run_tile(whole_tiles, state, STEPS % step_tile, STEPS % step_tile % 16)

    for row in range(slot_count):
        for half in range(2):
            stage_ref[row, pl.ds((half + 1) * 2 * pair_pad - 2 * SUBS, 2 * SUBS), :] = jnp.zeros(
                (2 * SUBS, LANES), jnp.float32
            )
    fetch.wait()

    rows_half = slot_count * SUBS
    edges = (0, 256, 512, STEPS)
    dot = functools.partial(jnp.dot, preferred_element_type=jnp.float32)

    def split_parts(values):
        high = values.astype(jnp.bfloat16)
        low = (values - high.astype(jnp.float32)).astype(jnp.bfloat16)
        return high, low

    def product(left, right):
        left_high, left_low = split_parts(left)
        right_high, right_low = split_parts(right)
        rows = left.shape[0]
        both = dot(jnp.concatenate([left_high, left_low], axis=0), right_high)
        return both[:rows] + both[rows:] + dot(left_high, right_low)

    def group(start):
        values = spectra_ref[:, pl.ds(start, PAIRS), :, :].reshape(slot_count, SUBS, STEPS)
        scale = jnp.concatenate(
            [scale_ref[tile, pl.ds(2 * start, SUBS), :] for tile in range(scale_ref.shape[0])],
            axis=1,
        )
        values = values * scale[:, :STEPS]
        step = lax.broadcasted_iota(jnp.int32, (1, SUBS, STEPS), 2)
        row_pair = lax.broadcasted_iota(jnp.int32, (1, SUBS, STEPS), 1) // 2
        in_first = step < NM - (first_pair + start + row_pair)
        lower = jnp.where(in_first, values, 0.0)
        upper = jnp.where(in_first, 0.0, values)
        first_block = start // per_block
        blocks = PAIRS // per_block
        table = jnp.concatenate(
            [table_ref[pl.ds(first_block + n, STEPS, stride=stride), :] for n in range(blocks)],
            axis=1,
        )
        begin, end = edges[0], edges[1]
        base = product(
            values[:, :, begin:end].reshape(rows_half, end - begin), table[begin:end]
        )
        rest = None
        for begin, end in zip(edges[1:-1], edges[2:]):
            left = jnp.concatenate([lower[:, :, begin:end], upper[:, :, begin:end]], axis=0)
            part = product(left.reshape(2 * rows_half, end - begin), table[begin:end])
            rest = part if rest is None else rest + part
        both = jnp.concatenate([rest[:rows_half] + base, rest[rows_half:]], axis=0)
        row_id = lax.broadcasted_iota(jnp.int32, (2 * rows_half, LANES), 0) % SUBS // 2
        lane_part = lax.broadcasted_iota(jnp.int32, (2 * rows_half, LANES), 1) // rows_all
        total = jnp.zeros((2 * rows_half, LANES), jnp.float32)
        for block in range(blocks):
            keep = row_id == block * per_block + lane_part
            total = total + jnp.where(keep, both[:, block * LANES : (block + 1) * LANES], 0.0)
        if per_block == 2:
            total = total + pltpu.roll(total, rows_all, 1)
        total = total.astype(jnp.bfloat16).astype(jnp.float32)
        for half in range(2):
            for row in range(slot_count):
                source = (half * slot_count + row) * SUBS
                stage_ref[row, pl.ds(half * 2 * pair_pad + 2 * start, SUBS), :] = total[
                    source : source + SUBS
                ]

    def group_body(index, carry):
        group(index * PAIRS)
        return carry

    lax.fori_loop(0, pair_count // PAIRS, group_body, 0)
    if pair_count % PAIRS:
        group(pair_count - PAIRS)

    for row in range(slot_count):
        flipped = stage_ref[row].T
        out_ref[:, pl.ds(row * lat_rows, lat_rows), :] = flipped[:rows_all].reshape(
            lat_count, lat_rows, 4 * pair_pad
        )


def coefficients(spectra, first_pair, rows_all, lat_rows):
    slot_count, _, pair_count, steps = spectra.shape
    per_block = LANES // rows_all
    vregs = pad_to(pair_count, SUBS * per_block) // (SUBS * per_block)
    pairs = vregs * SUBS * per_block
    tile_total = pad_to(STEPS, LANES) // rows_all
    pair_pad = pad_to(pair_count, SUBS)
    lat_count = rows_all // lat_rows
    kernel = functools.partial(
        coeff_kernel, pair_count=pair_count, rows_all=rows_all, lat_rows=lat_rows,
        slot_count=slot_count,
    )
    return pl.pallas_call(
        kernel,
        out_shape=jax.ShapeDtypeStruct(
            (lat_count, slot_count * lat_rows, 4 * pair_pad), jnp.float32
        ),
        in_specs=[
            pl.BlockSpec(memory_space=pltpu.SMEM),
            pl.BlockSpec(memory_space=pl.ANY),
        ],
        out_specs=pl.BlockSpec(memory_space=pltpu.VMEM),
        scratch_shapes=[
            pltpu.VMEM((slot_count, pair_count, 2, steps), jnp.float32),
            pltpu.VMEM((tile_total, vregs * SUBS, LANES), jnp.float32),
            pltpu.VMEM((pad_to(STEPS, LANES) // LANES, pairs, LANES), jnp.float32),
            pltpu.VMEM((pad_to(STEPS, LANES) // LANES, 2 * pairs, LANES), jnp.float32),
            pltpu.VMEM((pad_to(STEPS, SUBS) * (vregs * SUBS + 1), LANES), jnp.float32),
            pltpu.VMEM((slot_count, 4 * pair_pad, LANES), jnp.float32),
            pltpu.SemaphoreType.DMA,
        ],
        compiler_params=pltpu.CompilerParams(vmem_limit_bytes=40 * MIB),
        name="coefficients",
    )(first_pair, jnp.transpose(spectra, (0, 2, 1, 3)))


def trig_kernel(out_ref, *, pair_count, pair_pad, quarter, fine_total):
    block = pl.program_id(0)
    width = 4 * pair_pad
    coarse_total = pad_to(quarter // fine_total, SUBS)

    def orders(rows):
        lane = lax.broadcasted_iota(jnp.int32, (rows, width), 1)
        upper = lane >= 2 * pair_pad
        pair = jnp.where(upper, lane - 2 * pair_pad, lane)
        is_sine = (pair & 1) == 1
        pair = block * pair_count + (pair >> 1)
        return jnp.where(upper, NM - 1 - pair, pair), is_sine

    def angles(rows, spacing):
        order, _ = orders(rows)
        column = lax.broadcasted_iota(jnp.int32, (rows, width), 0) * spacing
        phase = (order * column % NLON).astype(jnp.float32) * (2.0 * math.pi / NLON)
        return jnp.cos(phase), jnp.sin(phase)

    fine_cos, fine_sin = angles(fine_total, 1)
    coarse_cos, coarse_sin = angles(coarse_total, fine_total)
    _, is_sine = orders(fine_total)
    for tile in range(quarter // fine_total):
        left, right = coarse_cos[tile : tile + 1], coarse_sin[tile : tile + 1]
        cosine = left * fine_cos - right * fine_sin
        sine = right * fine_cos + left * fine_sin
        out_ref[pl.ds(tile * fine_total, fine_total), :] = jnp.where(
            is_sine, sine, cosine
        ).astype(jnp.bfloat16)


def trig_table(pair_count, lon_count):
    pair_pad = pad_to(pair_count, SUBS)
    quarter = NLON // 4
    fine_total = 40
    return pl.pallas_call(
        functools.partial(
            trig_kernel, pair_count=pair_count, pair_pad=pair_pad, quarter=quarter,
            fine_total=fine_total,
        ),
        grid=(lon_count,),
        out_shape=jax.ShapeDtypeStruct((lon_count, quarter, 4 * pair_pad), jnp.bfloat16),
        out_specs=pl.BlockSpec((None, quarter, 4 * pair_pad), lambda b: (b, 0, 0)),
        compiler_params=pltpu.CompilerParams(vmem_limit_bytes=VMEM_LIMIT),
        cost_estimate=pl.CostEstimate(
            flops=24 * lon_count * quarter * pair_pad,
            bytes_accessed=lon_count * quarter * 8 * pair_pad,
            transcendentals=0,
        ),
        name="trig_table",
    )()


def grid_kernel(lon_ref, trig_ref, coeff_ref, *refs, lon_count, pair_count):
    flat_ref, right_ref = refs[lon_count:]
    share = coeff_ref.shape[1]
    width = coeff_ref.shape[2]
    rows = coeff_ref.shape[0] // lon_count * share
    values = coeff_ref[...].reshape(rows // share, lon_count, share, width)
    line = lax.broadcasted_iota(jnp.int32, (width, rows), 0)
    upper = line >= width // 2
    pair = jnp.where(upper, line - width // 2, line)
    is_sine = (pair & 1) == 1
    for block in range(lon_count):
        flat = values[:, block].reshape(rows, width).T
        swapped = jnp.where(is_sine, -pltpu.roll(flat, 1, 0), pltpu.roll(flat, width - 1, 0))
        order = block * pair_count + (pair >> 1)
        order = jnp.where(upper, NM - 1 - order, order) & 3
        odd = (order & 1) == 1
        flip = jnp.where(odd, -flat, flat)
        turned = jnp.where(order == 1, swapped, jnp.where(order == 3, -swapped, flat))
        turned = jnp.where(order == 2, -flat, turned)
        back = jnp.where(odd, -turned, turned)
        for turn, part in enumerate((flat, turned, flip, back)):
            right_ref[pl.ds(block * width, width), pl.ds(turn * rows, rows)] = part.astype(
                jnp.bfloat16
            )
    total = None
    for block in range(lon_count):
        part = jnp.dot(
            trig_ref[block],
            right_ref[pl.ds(block * width, width), :],
            preferred_element_type=jnp.float32,
        )
        total = part if total is None else total + part
    quarter = total.shape[0]
    for turn in range(4):
        flat_ref[pl.ds(turn * quarter, quarter), :] = total[:, turn * rows : (turn + 1) * rows]
    cols = NLON // lon_count
    for part in range(lon_count):
        refs[part][...] = flat_ref[pl.ds((lon_ref[0] ^ part) * cols, cols), :]


def grid_field(lon, trig, coeffs, pair_count):
    lon_count, quarter, width = trig.shape
    rows = coeffs.shape[0] // lon_count * coeffs.shape[1]
    return pl.pallas_call(
        functools.partial(grid_kernel, lon_count=lon_count, pair_count=pair_count),
        out_shape=[jax.ShapeDtypeStruct((NLON // lon_count, rows), jnp.float32)] * lon_count,
        in_specs=[pl.BlockSpec(memory_space=pltpu.SMEM)]
        + [pl.BlockSpec(memory_space=pltpu.VMEM)] * 2,
        out_specs=[pl.BlockSpec(memory_space=pltpu.VMEM)] * lon_count,
        scratch_shapes=[
            pltpu.VMEM((4 * quarter, rows), jnp.float32),
            pltpu.VMEM((lon_count * width, 4 * rows), jnp.bfloat16),
        ],
        compiler_params=pltpu.CompilerParams(vmem_limit_bytes=16 * MIB),
        cost_estimate=pl.CostEstimate(
            flops=2 * NLON * lon_count * width * rows,
            bytes_accessed=trig.size * 2 + 2 * coeffs.size * 4,
            transcendentals=0,
        ),
        name="grid_field",
    )(lon, trig, coeffs)


def gelu_parts(preact):
    scale = math.sqrt(2.0 / math.pi)
    square = preact * preact
    bend = jnp.tanh(scale * (preact + 0.044715 * (square * preact)))
    half = 0.5 * (1.0 + bend)
    slope = half + (0.5 * preact) * (1.0 - bend * bend) * (
        scale * (1.0 + (3.0 * 0.044715) * square)
    )
    return preact * half, slope


def forward_kernel(latents_ref, w_ref, b_ref, slope_ref, hidden_t_ref, latents_t_ref):
    latents = latents_ref[...]
    preact = jnp.dot(latents, w_ref[...], preferred_element_type=jnp.float32) + b_ref[...]
    hidden, slope = gelu_parts(preact)
    slope_ref[...] = slope
    hidden_t_ref[...] = hidden.T.astype(jnp.bfloat16)
    latents_t_ref[...] = latents.T


def forward(latents, w_hidden, b_hidden, parts):
    cells, width = latents.shape
    cols = cells // parts
    return pl.pallas_call(
        forward_kernel,
        grid=(parts,),
        out_shape=(
            jax.ShapeDtypeStruct((cells, width), jnp.float32),
            jax.ShapeDtypeStruct((parts, width, cols), jnp.bfloat16),
            jax.ShapeDtypeStruct((parts, width, cols), jnp.bfloat16),
        ),
        in_specs=[
            pl.BlockSpec((cols, width), lambda i: (i, 0)),
            pl.BlockSpec((width, width), lambda i: (0, 0)),
            pl.BlockSpec((1, width), lambda i: (0, 0)),
        ],
        out_specs=(
            pl.BlockSpec((cols, width), lambda i: (i, 0)),
            pl.BlockSpec((None, width, cols), lambda i: (i, 0, 0)),
            pl.BlockSpec((None, width, cols), lambda i: (i, 0, 0)),
        ),
        compiler_params=pltpu.CompilerParams(vmem_limit_bytes=32 * MIB),
        cost_estimate=pl.CostEstimate(
            flops=2 * cells * width * width,
            bytes_accessed=cells * width * 10,
            transcendentals=cells * width,
        ),
        name="forward",
    )(latents, w_hidden, b_hidden.reshape(1, width))


def backward_kernel(
    core_ref, scale_ref, place_ref, w_out_ref, slope_ref, hidden_t_ref, latents_t_ref, *refs,
    blocks,
):
    grid_refs = refs[:blocks]
    preact_ref, keep_ref, send_ref = refs[blocks : blocks + 3]
    field_ref, hidden_acc, out_acc, bias_acc, sums_ref = refs[blocks + 3 :]
    index = pl.program_id(0)
    total = pl.num_programs(0)
    lon_cols = grid_refs[0].shape[0]
    width = hidden_acc.shape[0]
    cols = slope_ref.shape[0]
    sum_rows = sums_ref.shape[0]

    @pl.when(index == 0)
    def _():
        field = None
        for block in range(blocks):
            scaled = (grid_refs[block][...] * scale_ref[block]).astype(jnp.bfloat16)
            part = jnp.dot(scaled, place_ref[block], preferred_element_type=jnp.float32)
            field = part if field is None else field + part
        for row in range(field.shape[1] // LANES):
            field_ref[pl.ds(row * lon_cols, lon_cols), :] = field[
                :, row * LANES : (row + 1) * LANES
            ]
        hidden_acc[...] = jnp.zeros_like(hidden_acc)
        out_acc[...] = jnp.zeros_like(out_acc)
        bias_acc[...] = jnp.zeros_like(bias_acc)

    field = field_ref[pl.ds(pl.multiple_of(index * cols, SUBS), cols), :].astype(jnp.bfloat16)
    back = jnp.dot(field, w_out_ref[...], preferred_element_type=jnp.float32)
    preact_back = (back * slope_ref[...]).astype(jnp.bfloat16)
    preact_ref[...] = preact_back
    hidden_acc[...] += jnp.dot(
        latents_t_ref[...], preact_back, preferred_element_type=jnp.float32
    )
    out_acc[...] += jnp.dot(hidden_t_ref[...], field, preferred_element_type=jnp.float32)
    bias_acc[...] += jnp.sum(preact_back.astype(jnp.float32), axis=0, keepdims=True)

    @pl.when(index == total - 1)
    def _():
        tiles = width // LANES
        for row_tile in range(width // SUBS):
            for tile in range(tiles):
                sums_ref[pl.ds((row_tile * tiles + tile) * SUBS, SUBS), :] = hidden_acc[
                    pl.ds(row_tile * SUBS, SUBS), pl.ds(tile * LANES, LANES)
                ]
        base = width * tiles
        flipped = out_acc[...].T
        for tile in range(tiles):
            sums_ref[pl.ds(base + tile * F, F), :] = flipped[:F, tile * LANES : (tile + 1) * LANES]
        base = base + tiles * F
        sums_ref[pl.ds(base, sum_rows - base), :] = jnp.zeros((sum_rows - base, LANES), jnp.float32)
        for tile in range(tiles):
            sums_ref[pl.ds(base + tile, 1), :] = bias_acc[:, tile * LANES : (tile + 1) * LANES]
        half = sum_rows // 2
        mine = core_ref[0]
        keep_ref[...] = sums_ref[pl.ds(pl.multiple_of(mine * half, SUBS), half), :]
        send_ref[...] = sums_ref[pl.ds(pl.multiple_of((1 - mine) * half, SUBS), half), :]


def backward(core, grids, scale, place, w_out_t, slope, hidden_t, latents_t, sum_rows):
    cells, width = slope.shape
    blocks = len(grids)
    parts, _, cols = hidden_t.shape
    half = (sum_rows // 2, LANES)
    whole3 = lambda i: (0, 0, 0)
    whole2 = lambda i: (0, 0)
    return pl.pallas_call(
        functools.partial(backward_kernel, blocks=blocks),
        grid=(parts,),
        out_shape=(
            jax.ShapeDtypeStruct((cells, width), jnp.bfloat16),
            jax.ShapeDtypeStruct(half, jnp.float32),
            jax.ShapeDtypeStruct(half, jnp.float32),
        ),
        in_specs=[
            pl.BlockSpec(memory_space=pltpu.SMEM),
            pl.BlockSpec(scale.shape, whole3),
            pl.BlockSpec(place.shape, whole3),
            pl.BlockSpec(w_out_t.shape, whole2),
            pl.BlockSpec((cols, width), lambda i: (i, 0)),
            pl.BlockSpec((None, width, cols), lambda i: (i, 0, 0)),
            pl.BlockSpec((None, width, cols), lambda i: (i, 0, 0)),
        ]
        + [pl.BlockSpec(grids[0].shape, whole2)] * blocks,
        out_specs=(
            pl.BlockSpec((cols, width), lambda i: (i, 0)),
            pl.BlockSpec(half, whole2),
            pl.BlockSpec(half, whole2),
        ),
        scratch_shapes=[
            pltpu.VMEM((cells, LANES), jnp.float32),
            pltpu.VMEM((width, width), jnp.float32),
            pltpu.VMEM((width, LANES), jnp.float32),
            pltpu.VMEM((1, width), jnp.float32),
            pltpu.VMEM((sum_rows, LANES), jnp.float32),
        ],
        compiler_params=pltpu.CompilerParams(vmem_limit_bytes=32 * MIB),
        cost_estimate=pl.CostEstimate(
            flops=2 * cells * width * (width + 2 * LANES),
            bytes_accessed=cells * width * 10,
            transcendentals=0,
        ),
        name="backward",
    )(core, scale, place, w_out_t, slope, hidden_t, latents_t, *grids)


def add_kernel(index_ref, *refs, inputs, outputs, factor):
    size = refs[0].shape[0] // outputs
    for part in range(outputs):
        start = 0 if outputs == 1 else pl.multiple_of((index_ref[0] ^ part) * size, SUBS)
        total = refs[0][pl.ds(start, size), :]
        for piece in refs[1:inputs]:
            total = total + piece[pl.ds(start, size), :]
        if factor is not None:
            total = total * factor
        refs[inputs + part][...] = total


def add_pieces(index, pieces, outputs, factor=None):
    rows = pieces[0].shape[0]
    size = rows // outputs
    return pl.pallas_call(
        functools.partial(add_kernel, inputs=len(pieces), outputs=outputs, factor=factor),
        out_shape=[jax.ShapeDtypeStruct((size, LANES), jnp.float32)] * outputs,
        in_specs=[pl.BlockSpec(memory_space=pltpu.SMEM)]
        + [pl.BlockSpec(memory_space=pltpu.VMEM)] * len(pieces),
        out_specs=[pl.BlockSpec(memory_space=pltpu.VMEM)] * outputs,
        cost_estimate=pl.CostEstimate(
            flops=len(pieces) * rows * LANES,
            bytes_accessed=4 * (len(pieces) + 1) * rows * LANES,
            transcendentals=0,
        ),
        compiler_params=pltpu.CompilerParams(vmem_limit_bytes=6 * MIB),
        name="add_pieces",
    )(index, *pieces)


def finish_kernel(place_ref, *refs, lon_count, depth):
    hidden_ref, bias_ref, out_ref, flat_ref = refs[2 * lon_count :]
    core, lon, deep = place_ref[0], place_ref[1], place_ref[2]
    size = refs[0].shape[0] // depth
    for half in range(2):
        for part in range(lon_count):
            for piece in range(depth):
                start = (((core ^ half) * lon_count + (lon ^ part)) * depth + (deep ^ piece)) * size
                flat_ref[pl.ds(pl.multiple_of(start, SUBS), size), :] = refs[
                    half * lon_count + part
                ][pl.ds(piece * size, size), :]
    width = hidden_ref.shape[0]
    tiles = width // LANES
    for row_tile in range(width // SUBS):
        for tile in range(tiles):
            hidden_ref[pl.ds(row_tile * SUBS, SUBS), pl.ds(tile * LANES, LANES)] = flat_ref[
                pl.ds((row_tile * tiles + tile) * SUBS, SUBS), :
            ]
    base = width * tiles
    for tile in range(tiles):
        out_ref[:, pl.ds(tile * LANES, LANES)] = flat_ref[pl.ds(base + tile * F, F), :]
        bias_ref[:, pl.ds(tile * LANES, LANES)] = flat_ref[pl.ds(base + tiles * F + tile, 1), :]


def finish(place, pieces, width, depth):
    lon_count = len(pieces) // 2
    return pl.pallas_call(
        functools.partial(finish_kernel, lon_count=lon_count, depth=depth),
        out_shape=(
            jax.ShapeDtypeStruct((width, width), jnp.float32),
            jax.ShapeDtypeStruct((1, width), jnp.float32),
            jax.ShapeDtypeStruct((F, width), jnp.float32),
        ),
        in_specs=[pl.BlockSpec(memory_space=pltpu.SMEM)]
        + [pl.BlockSpec(memory_space=pltpu.VMEM)] * len(pieces),
        out_specs=(pl.BlockSpec(memory_space=pltpu.VMEM),) * 3,
        scratch_shapes=[pltpu.VMEM((len(pieces) * pieces[0].shape[0], LANES), jnp.float32)],
        compiler_params=pltpu.CompilerParams(vmem_limit_bytes=8 * MIB),
        name="finish",
    )(place, *pieces)


def swap(value, axis, bits):
    count = lax.axis_size(axis)
    return lax.ppermute(value, axis, [(i, i ^ bits) for i in range(count)])


def local(spectra, field_slot, field_weight, latents, w_hidden, b_hidden, w_out):
    slot_count, _, pair_count, _ = spectra.shape
    lat_rows, lon_cols, width = latents.shape
    lat_count = lax.axis_size("lat")
    lon_count = lax.axis_size("lon")
    rows_all = lat_rows * lat_count
    lat_index = lax.axis_index("lat").astype(jnp.int32)
    lon_index = lax.axis_index("lon").astype(jnp.int32)
    pair_pad = pad_to(pair_count, SUBS)
    cells = lat_rows * lon_cols
    parts = 4

    coeffs = coefficients(spectra, (lon_index * pair_count).reshape(1), rows_all, lat_rows)
    share = slot_count * lat_rows // lon_count
    coeffs = coeffs.reshape(lat_count * lon_count, share, 4 * pair_pad)
    coeffs = lax.all_to_all(coeffs, ("lat", "lon"), split_axis=0, concat_axis=0, tiled=True)

    slope, hidden_t, latents_t = forward(
        latents.reshape(cells, width), w_hidden, b_hidden, parts
    )
    trig = trig_table(pair_count, lon_count)

    lanes = lat_count * share

    def spread(values):
        values = jnp.broadcast_to(values, (lat_count, slot_count, lat_rows))
        values = values.reshape(lat_count, lon_count, share)
        values = jnp.transpose(values, (1, 0, 2)).reshape(lon_count, lanes)
        arrival = lon_index ^ jnp.arange(lon_count, dtype=jnp.int32)
        chosen = arrival[:, None] == jnp.arange(lon_count, dtype=jnp.int32)
        return jnp.sum(jnp.where(chosen[:, :, None], values[None], 0), axis=1)

    field_ids = spread(field_slot.reshape(lat_count, slot_count, 1))
    row_ids = spread(jnp.arange(lat_rows, dtype=jnp.int32).reshape(1, 1, lat_rows))
    chosen = field_ids[:, :, None] == jnp.arange(F, dtype=jnp.int32)
    weight = jnp.sum(jnp.where(chosen, field_weight, 0.0), axis=2)
    sine = jnp.sin(band_angles(lat_index * lat_rows + row_ids, rows_all))
    scale = (sine * weight)[:, None, :]
    target = row_ids * LANES + field_ids
    place = (
        target[:, :, None] == jnp.arange(lat_rows * LANES, dtype=jnp.int32)[None, None, :]
    ).astype(jnp.bfloat16)
    w_out_t = jnp.concatenate([w_out.T, jnp.zeros((LANES - F, width), w_out.dtype)], axis=0)

    core_index, deep_index = lat_index & 1, lat_index >> 1
    spots = jnp.stack([core_index, lon_index, deep_index])
    grids = grid_field(lon_index.reshape(1), trig, coeffs, pair_count)
    grids = [grids[0]] + [swap(grids[part], "lon", part) for part in range(1, lon_count)]

    device_count = lat_count * lon_count
    used_rows = (width + F + 1) * width // LANES
    chunk = pad_to(pad_to(used_rows, device_count) // device_count, SUBS)
    depth = lat_count // 2
    preact_back, keep, send = backward(
        core_index.reshape(1), grids, scale, place, w_out_t, slope, hidden_t, latents_t,
        chunk * device_count,
    )
    latent_grad = lax.dot_general(
        preact_back, w_hidden, (((1,), (1,)), ((), ())), preferred_element_type=jnp.float32
    ).astype(jnp.bfloat16)

    pieces = add_pieces(
        lon_index.reshape(1), [keep, swap(send, "lat", 1)], lon_count
    )
    arrived = [swap(pieces[part], "lon", part) for part in range(1, lon_count)]
    arrived, latent_grad = lax.optimization_barrier((arrived, latent_grad))
    pieces = add_pieces(deep_index.reshape(1), [pieces[0]] + arrived, depth)
    arrived = [swap(pieces[part], "lat", 2 * part) for part in range(1, depth)]
    norm = 1.0 / math.sqrt(rows_all * NLON)
    total = add_pieces(deep_index.reshape(1), [pieces[0]] + arrived, 1, norm)[0]
    total = jnp.concatenate([total] + [swap(total, "lat", 2 * part) for part in range(1, depth)])
    totals = [total] + [swap(total, "lon", part) for part in range(1, lon_count)]
    totals = totals + [swap(piece, "lat", 1) for piece in totals]
    hidden_grad, bias_grad, out_grad = finish(spots, totals, width, depth)
    return (
        latent_grad.reshape(lat_rows, lon_cols, width),
        hidden_grad,
        bias_grad.reshape(width),
        out_grad.T,
    )


def solution(mesh):
    in_specs = (P("lat", None, "lon", None), P(), P(), P("lat", "lon", None), P(), P(), P())
    out_specs = (P("lat", "lon", None), P(), P(), P())
    return jax.shard_map(local, mesh=mesh, in_specs=in_specs, out_specs=out_specs, check_vma=False)
```

```python
import functools
import math

import jax
import jax.numpy as jnp
from jax import lax
from jax.experimental import pallas as pl
from jax.experimental.pallas import tpu as pltpu
from jax.sharding import PartitionSpec as P

NM = 720
NLON = 1440
F = 64
LANES = 128
SUBS = 8
STEPS = NM + 1
PAIRS = 4
MIB = 1024 * 1024
VMEM_LIMIT = 56 * MIB


def band_angles(row_ids, rows_all):
    return jnp.pi * (NM // 2 - rows_all // 2 + row_ids.astype(jnp.float32)) / NM


def pad_to(value, multiple):
    return (value + multiple - 1) // multiple * multiple


def coeff_kernel(
    first_ref, spectra_hbm, out_ref, spectra_ref, grow_ref, factor_ref, scale_ref, table_ref,
    stage_ref, copy_sem, *, pair_count, rows_all, lat_rows, slot_count,
):
    per_block = LANES // rows_all
    vregs = pad_to(pair_count, SUBS * per_block) // (SUBS * per_block)
    step_tile = rows_all
    stride = vregs * SUBS + 1
    pair_pad = pad_to(pair_count, SUBS)
    lat_count = rows_all // lat_rows
    first_pair = first_ref[0]

    fetch = pltpu.make_async_copy(spectra_hbm, spectra_ref, copy_sem)
    fetch.start()

    lane = lax.broadcasted_iota(jnp.int32, (SUBS, LANES), 1)
    sub = lax.broadcasted_iota(jnp.int32, (SUBS, LANES), 0)
    inner = lane & (rows_all - 1)
    which = lane // rows_all
    colatitude = band_angles(inner, rows_all)
    cosine = jnp.cos(colatitude)
    log_sine = jnp.log(jnp.sin(colatitude))

    def log_total(order_column):
        total = jnp.zeros((SUBS, LANES), jnp.float32)
        for tile in range(pad_to(NM, LANES) // LANES):
            term = (lane + tile * LANES).astype(jnp.float32)
            safe = jnp.maximum(term, 1.0)
            value = jnp.log((2.0 * safe + 1.0) / (2.0 * safe))
            total = total + jnp.where((term >= 1.0) & (term <= order_column), value, 0.0)
        return jnp.sum(total, axis=1, keepdims=True)

    def seed(order_of):
        total = jnp.zeros((SUBS, LANES), jnp.float32)
        for part in range(per_block):
            column = order_of(part).astype(jnp.float32)
            total = jnp.where(which == part, log_total(column), total)
        order = order_of(which).astype(jnp.float32)
        return jnp.exp(0.5 * total - 0.5 * math.log(4.0 * math.pi) + order * log_sine)

    pairs = vregs * SUBS * per_block
    steps_pad = pad_to(STEPS, LANES)
    step = lax.broadcasted_iota(jnp.int32, (pairs, steps_pad), 1)
    pair = first_pair + lax.broadcasted_iota(jnp.int32, (pairs, steps_pad), 0)
    switch = NM - pair
    in_first = step < switch
    order = jnp.where(in_first, pair, NM - 1 - pair).astype(jnp.float32)
    degree = jnp.where(in_first, pair + step, step - 1).astype(jnp.float32)
    grow = jnp.sqrt(
        jnp.maximum(4.0 * degree * degree - 1.0, 1.0)
        / jnp.maximum(degree * degree - order * order, 1.0)
    )
    since = jnp.where(in_first, step, step - switch)
    scale = jnp.where(since >= 2, grow / pltpu.roll(grow, 1, 1), 1.0)
    shift = 2
    while shift < STEPS:
        scale = jnp.where(since >= shift, scale * pltpu.roll(scale, shift, 1), scale)
        shift = 2 * shift
    factor = grow * pltpu.roll(scale, 1, 1) / scale
    for tile in range(steps_pad // LANES):
        factor_ref[tile] = factor[:, tile * LANES : (tile + 1) * LANES]
        for row in range(0, pairs, SUBS):
            piece = scale[row : row + SUBS, tile * LANES : (tile + 1) * LANES]
            for part in range(2):
                scale_ref[tile, pl.ds(2 * row + part, SUBS, stride=2), :] = piece

    firsts, seconds, switches = [], [], []
    for v in range(vregs):
        base = first_pair + (sub + v * SUBS) * per_block

        def order_first(part, base=base):
            return base + part

        def order_second(part, base=base):
            return NM - 1 - (base + part)

        firsts.append(seed(order_first))
        seconds.append(seed(order_second))
        switches.append(NM - (base + which))
        rows = pl.ds(v * SUBS, SUBS)
        for tile in range(steps_pad // LANES):
            if per_block == 1:
                grow_ref[tile, rows, :] = factor_ref[tile, rows, :]
            else:
                even = factor_ref[tile, pl.ds(2 * v * SUBS, SUBS, stride=2), :]
                odd = factor_ref[tile, pl.ds(2 * v * SUBS + 1, SUBS, stride=2), :]
                low = lane < rows_all
                grow_ref[2 * tile, rows, :] = jnp.where(low, even, pltpu.roll(odd, rows_all, 1))
                grow_ref[2 * tile + 1, rows, :] = jnp.where(
                    low, pltpu.roll(even, rows_all, 1), odd
                )

    def advance(tile, offset, state, grows):
        previous, before = state
        index = which * rows_all + offset
        step = tile * step_tile + offset
        produced, kept = [], []
        for v in range(vregs):
            grow = jnp.take_along_axis(grows[v], index, axis=1)
            value = (grow * cosine) * previous[v] - before[v]
            restart = switches[v] == step
            value = jnp.where(restart, seconds[v], value)
            table_ref[pl.ds(step * stride + v * SUBS, SUBS), :] = value
            produced.append(value)
            kept.append(jnp.where(restart, 0.0, previous[v]))
        return (tuple(produced), tuple(kept))

    def run_tile(tile, state, count, unroll):
        grows = [grow_ref[tile, pl.ds(v * SUBS, SUBS), :] for v in range(vregs)]

        def body(offset, carry):
            return advance(tile, offset, carry, grows)

        return lax.fori_loop(0, count, body, state, unroll=unroll)

    zeros = tuple(jnp.zeros((SUBS, LANES), jnp.float32) for _ in range(vregs))
    state = (zeros, tuple(-value for value in firsts))
    whole_tiles = STEPS // step_tile
    state = lax.fori_loop(
        0, whole_tiles, lambda tile, carry: run_tile(tile, carry, step_tile, 8), state
    )
    if STEPS % step_tile:
        run_tile(whole_tiles, state, STEPS % step_tile, STEPS % step_tile % 16)

    for row in range(slot_count):
        for half in range(2):
            stage_ref[row, pl.ds((half + 1) * 2 * pair_pad - 2 * SUBS, 2 * SUBS), :] = jnp.zeros(
                (2 * SUBS, LANES), jnp.float32
            )
    fetch.wait()

    rows_half = slot_count * SUBS
    edges = (0, 256, 512, STEPS)
    dot = functools.partial(jnp.dot, preferred_element_type=jnp.float32)

    def split_parts(values):
        high = values.astype(jnp.bfloat16)
        low = (values - high.astype(jnp.float32)).astype(jnp.bfloat16)
        return high, low

    def product(left, right):
        left_high, left_low = split_parts(left)
        right_high, right_low = split_parts(right)
        rows = left.shape[0]
        both = dot(jnp.concatenate([left_high, left_low], axis=0), right_high)
        return both[:rows] + both[rows:] + dot(left_high, right_low)

    def group(start):
        values = spectra_ref[:, pl.ds(start, PAIRS), :, :].reshape(slot_count, SUBS, STEPS)
        scale = jnp.concatenate(
            [scale_ref[tile, pl.ds(2 * start, SUBS), :] for tile in range(scale_ref.shape[0])],
            axis=1,
        )
        values = values * scale[:, :STEPS]
        step = lax.broadcasted_iota(jnp.int32, (1, SUBS, STEPS), 2)
        row_pair = lax.broadcasted_iota(jnp.int32, (1, SUBS, STEPS), 1) >> 1
        in_first = step < NM - (first_pair + start + row_pair)
        lower = jnp.where(in_first, values, 0.0)
        upper = jnp.where(in_first, 0.0, values)
        first_block = start // per_block
        blocks = PAIRS // per_block
        table = jnp.concatenate(
            [table_ref[pl.ds(first_block + n, STEPS, stride=stride), :] for n in range(blocks)],
            axis=1,
        )
        begin, end = edges[0], edges[1]
        base = product(
            values[:, :, begin:end].reshape(rows_half, end - begin), table[begin:end]
        )
        rest = None
        for begin, end in zip(edges[1:-1], edges[2:]):
            left = jnp.concatenate([lower[:, :, begin:end], upper[:, :, begin:end]], axis=0)
            part = product(left.reshape(2 * rows_half, end - begin), table[begin:end])
            rest = part if rest is None else rest + part
        both = jnp.concatenate([rest[:rows_half] + base, rest[rows_half:]], axis=0)
        both = both.reshape(2 * slot_count, SUBS, blocks * LANES)
        row_id = lax.broadcasted_iota(jnp.int32, (1, SUBS, LANES), 1) >> 1
        lane_part = lax.broadcasted_iota(jnp.int32, (1, SUBS, LANES), 2)
        lane_part = jnp.where(lane_part < rows_all, 0, 1)
        total = None
        for block in range(blocks):
            part = both[:, :, block * LANES : (block + 1) * LANES]
            keep = row_id == block * per_block + lane_part
            total = jnp.where(keep, part, 0.0 if total is None else total)
        total = total.reshape(2 * rows_half, LANES)
        if per_block == 2:
            total = total + pltpu.roll(total, rows_all, 1)
        total = total.astype(jnp.bfloat16).astype(jnp.float32)
        for half in range(2):
            for row in range(slot_count):
                source = (half * slot_count + row) * SUBS
                stage_ref[row, pl.ds(half * 2 * pair_pad + 2 * start, SUBS), :] = total[
                    source : source + SUBS
                ]

    def group_body(index, carry):
        group(index * PAIRS)
        return carry

    lax.fori_loop(0, pair_count // PAIRS, group_body, 0, unroll=2 - pair_count // PAIRS % 2)
    if pair_count % PAIRS:
        group(pair_count - PAIRS)

    for row in range(slot_count):
        flipped = stage_ref[row].T
        out_ref[:, pl.ds(row * lat_rows, lat_rows), :] = flipped[:rows_all].reshape(
            lat_count, lat_rows, 4 * pair_pad
        )


def coefficients(spectra, first_pair, rows_all, lat_rows):
    slot_count, _, pair_count, steps = spectra.shape
    per_block = LANES // rows_all
    vregs = pad_to(pair_count, SUBS * per_block) // (SUBS * per_block)
    pairs = vregs * SUBS * per_block
    tile_total = pad_to(STEPS, LANES) // rows_all
    pair_pad = pad_to(pair_count, SUBS)
    lat_count = rows_all // lat_rows
    kernel = functools.partial(
        coeff_kernel, pair_count=pair_count, rows_all=rows_all, lat_rows=lat_rows,
        slot_count=slot_count,
    )
    return pl.pallas_call(
        kernel,
        out_shape=jax.ShapeDtypeStruct(
            (lat_count, slot_count * lat_rows, 4 * pair_pad), jnp.float32
        ),
        in_specs=[
            pl.BlockSpec(memory_space=pltpu.SMEM),
            pl.BlockSpec(memory_space=pl.ANY),
        ],
        out_specs=pl.BlockSpec(memory_space=pltpu.VMEM),
        scratch_shapes=[
            pltpu.VMEM((slot_count, pair_count, 2, steps), jnp.float32),
            pltpu.VMEM((tile_total, vregs * SUBS, LANES), jnp.float32),
            pltpu.VMEM((pad_to(STEPS, LANES) // LANES, pairs, LANES), jnp.float32),
            pltpu.VMEM((pad_to(STEPS, LANES) // LANES, 2 * pairs, LANES), jnp.float32),
            pltpu.VMEM((pad_to(STEPS, SUBS) * (vregs * SUBS + 1), LANES), jnp.float32),
            pltpu.VMEM((slot_count, 4 * pair_pad, LANES), jnp.float32),
            pltpu.SemaphoreType.DMA,
        ],
        compiler_params=pltpu.CompilerParams(vmem_limit_bytes=VMEM_LIMIT),
        name="coefficients",
    )(first_pair, jnp.transpose(spectra, (0, 2, 1, 3)))


def trig_kernel(out_ref, *, pair_count, pair_pad, quarter, fine_total):
    block = pl.program_id(0)
    width = 4 * pair_pad
    coarse_total = pad_to(quarter // fine_total, SUBS)

    def orders(rows):
        lane = lax.broadcasted_iota(jnp.int32, (rows, width), 1)
        upper = lane >= 2 * pair_pad
        pair = jnp.where(upper, lane - 2 * pair_pad, lane)
        is_sine = (pair & 1) == 1
        pair = block * pair_count + (pair >> 1)
        return jnp.where(upper, NM - 1 - pair, pair), is_sine

    def angles(rows, spacing):
        order, _ = orders(rows)
        column = lax.broadcasted_iota(jnp.int32, (rows, width), 0) * spacing
        phase = (order * column % NLON).astype(jnp.float32) * (2.0 * math.pi / NLON)
        return jnp.cos(phase), jnp.sin(phase)

    fine_cos, fine_sin = angles(fine_total, 1)
    coarse_cos, coarse_sin = angles(coarse_total, fine_total)
    _, is_sine = orders(fine_total)
    for tile in range(quarter // fine_total):
        left, right = coarse_cos[tile : tile + 1], coarse_sin[tile : tile + 1]
        cosine = left * fine_cos - right * fine_sin
        sine = right * fine_cos + left * fine_sin
        out_ref[pl.ds(tile * fine_total, fine_total), :] = jnp.where(
            is_sine, sine, cosine
        ).astype(jnp.bfloat16)


def trig_table(pair_count, lon_count):
    pair_pad = pad_to(pair_count, SUBS)
    quarter = NLON // 4
    fine_total = 40
    return pl.pallas_call(
        functools.partial(
            trig_kernel, pair_count=pair_count, pair_pad=pair_pad, quarter=quarter,
            fine_total=fine_total,
        ),
        grid=(lon_count,),
        out_shape=jax.ShapeDtypeStruct((lon_count, quarter, 4 * pair_pad), jnp.bfloat16),
        out_specs=pl.BlockSpec((None, quarter, 4 * pair_pad), lambda b: (b, 0, 0)),
        compiler_params=pltpu.CompilerParams(vmem_limit_bytes=VMEM_LIMIT),
        cost_estimate=pl.CostEstimate(
            flops=24 * lon_count * quarter * pair_pad,
            bytes_accessed=lon_count * quarter * 8 * pair_pad,
            transcendentals=0,
        ),
        name="trig_table",
    )()


def grid_kernel(lon_ref, trig_ref, coeff_ref, *refs, lon_count, pair_count):
    flat_ref, right_ref = refs[lon_count:]
    share = coeff_ref.shape[1]
    width = coeff_ref.shape[2]
    rows = coeff_ref.shape[0] // lon_count * share
    values = coeff_ref[...].reshape(rows // share, lon_count, share, width)
    line = lax.broadcasted_iota(jnp.int32, (width, rows), 0)
    upper = line >= width // 2
    pair = jnp.where(upper, line - width // 2, line)
    is_sine = (pair & 1) == 1
    for block in range(lon_count):
        flat = values[:, block].reshape(rows, width).T
        swapped = jnp.where(is_sine, -pltpu.roll(flat, 1, 0), pltpu.roll(flat, width - 1, 0))
        order = block * pair_count + (pair >> 1)
        order = jnp.where(upper, NM - 1 - order, order) & 3
        odd = (order & 1) == 1
        flip = jnp.where(odd, -flat, flat)
        turned = jnp.where(order == 1, swapped, jnp.where(order == 3, -swapped, flat))
        turned = jnp.where(order == 2, -flat, turned)
        back = jnp.where(odd, -turned, turned)
        for turn, part in enumerate((flat, turned, flip, back)):
            right_ref[pl.ds(block * width, width), pl.ds(turn * rows, rows)] = part.astype(
                jnp.bfloat16
            )
    total = None
    for block in range(lon_count):
        part = jnp.dot(
            trig_ref[block],
            right_ref[pl.ds(block * width, width), :],
            preferred_element_type=jnp.float32,
        )
        total = part if total is None else total + part
    quarter = total.shape[0]
    for turn in range(4):
        flat_ref[pl.ds(turn * quarter, quarter), :] = total[:, turn * rows : (turn + 1) * rows]
    cols = NLON // lon_count
    for part in range(lon_count):
        refs[part][...] = flat_ref[pl.ds((lon_ref[0] ^ part) * cols, cols), :]


def grid_field(lon, trig, coeffs, pair_count):
    lon_count, quarter, width = trig.shape
    rows = coeffs.shape[0] // lon_count * coeffs.shape[1]
    return pl.pallas_call(
        functools.partial(grid_kernel, lon_count=lon_count, pair_count=pair_count),
        out_shape=[jax.ShapeDtypeStruct((NLON // lon_count, rows), jnp.float32)] * lon_count,
        in_specs=[pl.BlockSpec(memory_space=pltpu.SMEM)]
        + [pl.BlockSpec(memory_space=pltpu.VMEM)] * 2,
        out_specs=[pl.BlockSpec(memory_space=pltpu.VMEM)] * lon_count,
        scratch_shapes=[
            pltpu.VMEM((4 * quarter, rows), jnp.float32),
            pltpu.VMEM((lon_count * width, 4 * rows), jnp.bfloat16),
        ],
        compiler_params=pltpu.CompilerParams(vmem_limit_bytes=16 * MIB),
        cost_estimate=pl.CostEstimate(
            flops=2 * NLON * lon_count * width * rows,
            bytes_accessed=trig.size * 2 + 2 * coeffs.size * 4,
            transcendentals=0,
        ),
        name="grid_field",
    )(lon, trig, coeffs)


def gelu_parts(preact):
    scale = math.sqrt(2.0 / math.pi)
    square = preact * preact
    bend = jnp.tanh(scale * (preact + 0.044715 * (square * preact)))
    half = 0.5 * (1.0 + bend)
    slope = half + (0.5 * preact) * (1.0 - bend * bend) * (
        scale * (1.0 + (3.0 * 0.044715) * square)
    )
    return preact * half, slope


def forward_kernel(latents_ref, w_ref, b_ref, _, slope_ref, hidden_t_ref, latents_t_ref):
    latents = latents_ref[...]
    preact = jnp.dot(latents, w_ref[...], preferred_element_type=jnp.float32) + b_ref[...]
    hidden, slope = gelu_parts(preact)
    slope_ref[...] = slope
    hidden_t_ref[...] = hidden.T.astype(jnp.bfloat16)
    latents_t_ref[...] = latents.T


def forward(latents, w_hidden, b_hidden, after, parts):
    cells, width = latents.shape
    cols = cells // parts
    return pl.pallas_call(
        forward_kernel,
        grid=(parts,),
        out_shape=(
            jax.ShapeDtypeStruct((cells, width), jnp.float32),
            jax.ShapeDtypeStruct((parts, width, cols), jnp.bfloat16),
            jax.ShapeDtypeStruct((parts, width, cols), jnp.bfloat16),
        ),
        in_specs=[
            pl.BlockSpec((cols, width), lambda i: (i, 0)),
            pl.BlockSpec((width, width), lambda i: (0, 0)),
            pl.BlockSpec((1, width), lambda i: (0, 0)),
            pl.BlockSpec(memory_space=pl.ANY),
        ],
        out_specs=(
            pl.BlockSpec((cols, width), lambda i: (i, 0)),
            pl.BlockSpec((None, width, cols), lambda i: (i, 0, 0)),
            pl.BlockSpec((None, width, cols), lambda i: (i, 0, 0)),
        ),
        compiler_params=pltpu.CompilerParams(vmem_limit_bytes=32 * MIB),
        cost_estimate=pl.CostEstimate(
            flops=2 * cells * width * width,
            bytes_accessed=cells * width * 10,
            transcendentals=cells * width,
        ),
        name="forward",
    )(latents, w_hidden, b_hidden.reshape(1, width), after)


def backward_kernel(
    core_ref, scale_ref, place_ref, w_out_ref, slope_ref, hidden_t_ref, latents_t_ref, *refs,
    blocks,
):
    grid_refs = refs[:blocks]
    preact_ref, keep_ref, send_ref = refs[blocks : blocks + 3]
    field_ref, hidden_acc, out_acc, bias_acc, sums_ref = refs[blocks + 3 :]
    index = pl.program_id(0)
    total = pl.num_programs(0)
    lon_cols = grid_refs[0].shape[0]
    width = hidden_acc.shape[0]
    cols = slope_ref.shape[0]
    sum_rows = sums_ref.shape[0]

    @pl.when(index == 0)
    def _():
        field = None
        for block in range(blocks):
            scaled = (grid_refs[block][...] * scale_ref[block]).astype(jnp.bfloat16)
            part = jnp.dot(scaled, place_ref[block], preferred_element_type=jnp.float32)
            field = part if field is None else field + part
        for row in range(field.shape[1] // LANES):
            field_ref[pl.ds(row * lon_cols, lon_cols), :] = field[
                :, row * LANES : (row + 1) * LANES
            ]
        hidden_acc[...] = jnp.zeros_like(hidden_acc)
        out_acc[...] = jnp.zeros_like(out_acc)
        bias_acc[...] = jnp.zeros_like(bias_acc)

    field = field_ref[pl.ds(pl.multiple_of(index * cols, SUBS), cols), :].astype(jnp.bfloat16)
    back = jnp.dot(field, w_out_ref[...], preferred_element_type=jnp.float32)
    preact_back = (back * slope_ref[...]).astype(jnp.bfloat16)
    preact_ref[...] = preact_back
    hidden_acc[...] += jnp.dot(
        latents_t_ref[...], preact_back, preferred_element_type=jnp.float32
    )
    out_acc[...] += jnp.dot(hidden_t_ref[...], field, preferred_element_type=jnp.float32)
    bias_acc[...] += jnp.sum(preact_back.astype(jnp.float32), axis=0, keepdims=True)

    @pl.when(index == total - 1)
    def _():
        tiles = width // LANES
        for row_tile in range(width // SUBS):
            for tile in range(tiles):
                sums_ref[pl.ds((row_tile * tiles + tile) * SUBS, SUBS), :] = hidden_acc[
                    pl.ds(row_tile * SUBS, SUBS), pl.ds(tile * LANES, LANES)
                ]
        base = width * tiles
        flipped = out_acc[...].T
        for tile in range(tiles):
            sums_ref[pl.ds(base + tile * F, F), :] = flipped[:F, tile * LANES : (tile + 1) * LANES]
        base = base + tiles * F
        sums_ref[pl.ds(base, sum_rows - base), :] = jnp.zeros((sum_rows - base, LANES), jnp.float32)
        for tile in range(tiles):
            sums_ref[pl.ds(base + tile, 1), :] = bias_acc[:, tile * LANES : (tile + 1) * LANES]
        half = sum_rows // 2
        mine = core_ref[0]
        keep_ref[...] = sums_ref[pl.ds(pl.multiple_of(mine * half, SUBS), half), :]
        send_ref[...] = sums_ref[pl.ds(pl.multiple_of((1 - mine) * half, SUBS), half), :]


def backward(core, grids, scale, place, w_out_t, slope, hidden_t, latents_t, sum_rows):
    cells, width = slope.shape
    blocks = len(grids)
    parts, _, cols = hidden_t.shape
    half = (sum_rows // 2, LANES)
    whole3 = lambda i: (0, 0, 0)
    whole2 = lambda i: (0, 0)
    return pl.pallas_call(
        functools.partial(backward_kernel, blocks=blocks),
        grid=(parts,),
        out_shape=(
            jax.ShapeDtypeStruct((cells, width), jnp.bfloat16),
            jax.ShapeDtypeStruct(half, jnp.float32),
            jax.ShapeDtypeStruct(half, jnp.float32),
        ),
        in_specs=[
            pl.BlockSpec(memory_space=pltpu.SMEM),
            pl.BlockSpec(scale.shape, whole3),
            pl.BlockSpec(place.shape, whole3),
            pl.BlockSpec(w_out_t.shape, whole2),
            pl.BlockSpec((cols, width), lambda i: (i, 0)),
            pl.BlockSpec((None, width, cols), lambda i: (i, 0, 0)),
            pl.BlockSpec((None, width, cols), lambda i: (i, 0, 0)),
        ]
        + [pl.BlockSpec(grids[0].shape, whole2)] * blocks,
        out_specs=(
            pl.BlockSpec((cols, width), lambda i: (i, 0)),
            pl.BlockSpec(half, whole2),
            pl.BlockSpec(half, whole2),
        ),
        scratch_shapes=[
            pltpu.VMEM((cells, LANES), jnp.float32),
            pltpu.VMEM((width, width), jnp.float32),
            pltpu.VMEM((width, LANES), jnp.float32),
            pltpu.VMEM((1, width), jnp.float32),
            pltpu.VMEM((sum_rows, LANES), jnp.float32),
        ],
        compiler_params=pltpu.CompilerParams(vmem_limit_bytes=32 * MIB),
        cost_estimate=pl.CostEstimate(
            flops=2 * cells * width * (width + 2 * LANES),
            bytes_accessed=cells * width * 10,
            transcendentals=0,
        ),
        name="backward",
    )(core, scale, place, w_out_t, slope, hidden_t, latents_t, *grids)


def add_kernel(index_ref, *refs, inputs, outputs, factor):
    size = refs[0].shape[0] // outputs
    for part in range(outputs):
        start = 0 if outputs == 1 else pl.multiple_of((index_ref[0] ^ part) * size, SUBS)
        total = refs[0][pl.ds(start, size), :]
        for piece in refs[1:inputs]:
            total = total + piece[pl.ds(start, size), :]
        if factor is not None:
            total = total * factor
        refs[inputs + part][...] = total


def add_pieces(index, pieces, outputs, factor=None):
    rows = pieces[0].shape[0]
    size = rows // outputs
    return pl.pallas_call(
        functools.partial(add_kernel, inputs=len(pieces), outputs=outputs, factor=factor),
        out_shape=[jax.ShapeDtypeStruct((size, LANES), jnp.float32)] * outputs,
        in_specs=[pl.BlockSpec(memory_space=pltpu.SMEM)]
        + [pl.BlockSpec(memory_space=pltpu.VMEM)] * len(pieces),
        out_specs=[pl.BlockSpec(memory_space=pltpu.VMEM)] * outputs,
        cost_estimate=pl.CostEstimate(
            flops=len(pieces) * rows * LANES,
            bytes_accessed=4 * (len(pieces) + 1) * rows * LANES,
            transcendentals=0,
        ),
        compiler_params=pltpu.CompilerParams(vmem_limit_bytes=6 * MIB),
        name="add_pieces",
    )(index, *pieces)


def finish_kernel(place_ref, *refs, lon_count, depth):
    hidden_ref, bias_ref, out_ref, flat_ref = refs[2 * lon_count :]
    core, lon, deep = place_ref[0], place_ref[1], place_ref[2]
    size = refs[0].shape[0] // depth
    for half in range(2):
        for part in range(lon_count):
            for piece in range(depth):
                start = (((core ^ half) * lon_count + (lon ^ part)) * depth + (deep ^ piece)) * size
                flat_ref[pl.ds(pl.multiple_of(start, SUBS), size), :] = refs[
                    half * lon_count + part
                ][pl.ds(piece * size, size), :]
    width = hidden_ref.shape[0]
    tiles = width // LANES
    for row_tile in range(width // SUBS):
        for tile in range(tiles):
            hidden_ref[pl.ds(row_tile * SUBS, SUBS), pl.ds(tile * LANES, LANES)] = flat_ref[
                pl.ds((row_tile * tiles + tile) * SUBS, SUBS), :
            ]
    base = width * tiles
    for tile in range(tiles):
        out_ref[:, pl.ds(tile * LANES, LANES)] = flat_ref[pl.ds(base + tile * F, F), :]
        bias_ref[:, pl.ds(tile * LANES, LANES)] = flat_ref[pl.ds(base + tiles * F + tile, 1), :]


def finish(place, pieces, width, depth):
    lon_count = len(pieces) // 2
    return pl.pallas_call(
        functools.partial(finish_kernel, lon_count=lon_count, depth=depth),
        out_shape=(
            jax.ShapeDtypeStruct((width, width), jnp.float32),
            jax.ShapeDtypeStruct((1, width), jnp.float32),
            jax.ShapeDtypeStruct((F, width), jnp.float32),
        ),
        in_specs=[pl.BlockSpec(memory_space=pltpu.SMEM)]
        + [pl.BlockSpec(memory_space=pltpu.VMEM)] * len(pieces),
        out_specs=(pl.BlockSpec(memory_space=pltpu.VMEM),) * 3,
        scratch_shapes=[pltpu.VMEM((len(pieces) * pieces[0].shape[0], LANES), jnp.float32)],
        compiler_params=pltpu.CompilerParams(vmem_limit_bytes=8 * MIB),
        name="finish",
    )(place, *pieces)


def swap(value, axis, bits):
    count = lax.axis_size(axis)
    return lax.ppermute(value, axis, [(i, i ^ bits) for i in range(count)])


def local(spectra, field_slot, field_weight, latents, w_hidden, b_hidden, w_out):
    slot_count, _, pair_count, _ = spectra.shape
    lat_rows, lon_cols, width = latents.shape
    lat_count = lax.axis_size("lat")
    lon_count = lax.axis_size("lon")
    rows_all = lat_rows * lat_count
    lat_index = lax.axis_index("lat").astype(jnp.int32)
    lon_index = lax.axis_index("lon").astype(jnp.int32)
    pair_pad = pad_to(pair_count, SUBS)
    cells = lat_rows * lon_cols
    parts = 4

    coeffs = coefficients(spectra, (lon_index * pair_count).reshape(1), rows_all, lat_rows)
    share = slot_count * lat_rows // lon_count
    coeffs = coeffs.reshape(lat_count * lon_count, share, 4 * pair_pad)
    coeffs = lax.all_to_all(coeffs, ("lat", "lon"), split_axis=0, concat_axis=0, tiled=True)

    trig = trig_table(pair_count, lon_count)

    lanes = lat_count * share

    def spread(values):
        values = jnp.broadcast_to(values, (lat_count, slot_count, lat_rows))
        values = values.reshape(lat_count, lon_count, share)
        values = jnp.transpose(values, (1, 0, 2)).reshape(lon_count, lanes)
        arrival = lon_index ^ jnp.arange(lon_count, dtype=jnp.int32)
        chosen = arrival[:, None] == jnp.arange(lon_count, dtype=jnp.int32)
        return jnp.sum(jnp.where(chosen[:, :, None], values[None], 0), axis=1)

    field_ids = spread(field_slot.reshape(lat_count, slot_count, 1))
    row_ids = spread(jnp.arange(lat_rows, dtype=jnp.int32).reshape(1, 1, lat_rows))
    chosen = field_ids[:, :, None] == jnp.arange(F, dtype=jnp.int32)
    weight = jnp.sum(jnp.where(chosen, field_weight, 0.0), axis=2)
    sine = jnp.sin(band_angles(lat_index * lat_rows + row_ids, rows_all))
    scale = (sine * weight)[:, None, :]
    target = row_ids * LANES + field_ids
    place = (
        target[:, :, None] == jnp.arange(lat_rows * LANES, dtype=jnp.int32)[None, None, :]
    ).astype(jnp.bfloat16)
    w_out_t = jnp.concatenate([w_out.T, jnp.zeros((LANES - F, width), w_out.dtype)], axis=0)

    depth = lat_count // 2
    bits = depth.bit_length() - 1
    core_index = lat_index & 1
    deep_index = sum(((lat_index >> (bit + 1)) & 1) << (bits - 1 - bit) for bit in range(bits))
    spots = jnp.stack([core_index, lon_index, deep_index])
    grids = grid_field(lon_index.reshape(1), trig, coeffs, pair_count)
    slope, hidden_t, latents_t = forward(
        latents.reshape(cells, width), w_hidden, b_hidden, grids[0], parts
    )
    grids = [grids[0]] + [swap(grids[part], "lon", part) for part in range(1, lon_count)]

    device_count = lat_count * lon_count
    used_rows = (width + F + 1) * width // LANES
    chunk = pad_to(pad_to(used_rows, device_count) // device_count, SUBS)
    preact_back, keep, send = backward(
        core_index.reshape(1), grids, scale, place, w_out_t, slope, hidden_t, latents_t,
        chunk * device_count,
    )
    latent_grad = lax.dot_general(
        preact_back, w_hidden, (((1,), (1,)), ((), ())), preferred_element_type=jnp.float32
    ).astype(jnp.bfloat16)

    pieces = add_pieces(
        lon_index.reshape(1), [keep, swap(send, "lat", 1)], lon_count
    )
    arrived = [swap(pieces[part], "lon", part) for part in range(1, lon_count)]
    arrived, latent_grad = lax.optimization_barrier((arrived, latent_grad))
    pieces = [pieces[0]] + arrived
    for bit in range(bits):
        side = (lat_index >> (bit + 1)) & 1
        pieces = add_pieces(side.reshape(1), pieces, 2)
        pieces = [pieces[0], swap(pieces[1], "lat", 2 << bit)]
    norm = 1.0 / math.sqrt(rows_all * NLON)
    total = add_pieces(deep_index.reshape(1), pieces, 1, norm)[0]
    for bit in reversed(range(bits)):
        total = jnp.concatenate([total, swap(total, "lat", 2 << bit)])
    totals = [total] + [swap(total, "lon", part) for part in range(1, lon_count)]
    totals = totals + [swap(piece, "lat", 1) for piece in totals]
    hidden_grad, bias_grad, out_grad = finish(spots, totals, width, depth)
    return (
        latent_grad.reshape(lat_rows, lon_cols, width),
        hidden_grad,
        bias_grad.reshape(width),
        out_grad.T,
    )


def solution(mesh):
    in_specs = (P("lat", None, "lon", None), P(), P(), P("lat", "lon", None), P(), P(), P())
    out_specs = (P("lat", "lon", None), P(), P(), P())
    return jax.shard_map(local, mesh=mesh, in_specs=in_specs, out_specs=out_specs, check_vma=False)
```

```python
import functools
import math

import jax
import jax.numpy as jnp
from jax import lax
from jax.experimental import pallas as pl
from jax.experimental.pallas import tpu as pltpu
from jax.sharding import PartitionSpec as P

NM = 720
NLON = 1440
F = 64
LANES = 128
SUBS = 8
STEPS = NM + 1
PAIRS = 4
MIB = 1024 * 1024
VMEM_LIMIT = 56 * MIB


def band_angles(row_ids, rows_all):
    return jnp.pi * (NM // 2 - rows_all // 2 + row_ids.astype(jnp.float32)) / NM


def pad_to(value, multiple):
    return (value + multiple - 1) // multiple * multiple


def coeff_kernel(
    first_ref, spectra_hbm, out_ref, spectra_ref, grow_ref, factor_ref, scale_ref, table_ref,
    stage_ref, copy_sem, *, pair_count, rows_all, lat_rows, slot_count,
):
    per_block = LANES // rows_all
    vregs = pad_to(pair_count, SUBS * per_block) // (SUBS * per_block)
    step_tile = rows_all
    stride = vregs * SUBS + 1
    pair_pad = pad_to(pair_count, SUBS)
    lat_count = rows_all // lat_rows
    first_pair = first_ref[0]

    fetch = pltpu.make_async_copy(spectra_hbm, spectra_ref, copy_sem)
    fetch.start()

    lane = lax.broadcasted_iota(jnp.int32, (SUBS, LANES), 1)
    sub = lax.broadcasted_iota(jnp.int32, (SUBS, LANES), 0)
    inner = lane & (rows_all - 1)
    which = lane // rows_all
    colatitude = band_angles(inner, rows_all)
    cosine = jnp.cos(colatitude)
    log_sine = jnp.log(jnp.sin(colatitude))

    def log_total(order_column):
        total = jnp.zeros((SUBS, LANES), jnp.float32)
        for tile in range(pad_to(NM, LANES) // LANES):
            term = (lane + tile * LANES).astype(jnp.float32)
            safe = jnp.maximum(term, 1.0)
            value = jnp.log((2.0 * safe + 1.0) / (2.0 * safe))
            total = total + jnp.where((term >= 1.0) & (term <= order_column), value, 0.0)
        return jnp.sum(total, axis=1, keepdims=True)

    def seed(order_of):
        total = jnp.zeros((SUBS, LANES), jnp.float32)
        for part in range(per_block):
            column = order_of(part).astype(jnp.float32)
            total = jnp.where(which == part, log_total(column), total)
        order = order_of(which).astype(jnp.float32)
        return jnp.exp(0.5 * total - 0.5 * math.log(4.0 * math.pi) + order * log_sine)

    pairs = vregs * SUBS * per_block
    steps_pad = pad_to(STEPS, LANES)
    step = lax.broadcasted_iota(jnp.int32, (pairs, steps_pad), 1)
    pair = first_pair + lax.broadcasted_iota(jnp.int32, (pairs, steps_pad), 0)
    switch = NM - pair
    in_first = step < switch
    order = jnp.where(in_first, pair, NM - 1 - pair).astype(jnp.float32)
    degree = jnp.where(in_first, pair + step, step - 1).astype(jnp.float32)
    grow = jnp.sqrt(
        jnp.maximum(4.0 * degree * degree - 1.0, 1.0)
        / jnp.maximum(degree * degree - order * order, 1.0)
    )
    since = jnp.where(in_first, step, step - switch)
    scale = jnp.where(since >= 2, grow / pltpu.roll(grow, 1, 1), 1.0)
    shift = 2
    while shift < STEPS:
        scale = jnp.where(since >= shift, scale * pltpu.roll(scale, shift, 1), scale)
        shift = 2 * shift
    factor = grow * pltpu.roll(scale, 1, 1) / scale
    for tile in range(steps_pad // LANES):
        factor_ref[tile] = factor[:, tile * LANES : (tile + 1) * LANES]
        for row in range(0, pairs, SUBS):
            piece = scale[row : row + SUBS, tile * LANES : (tile + 1) * LANES]
            for part in range(2):
                scale_ref[tile, pl.ds(2 * row + part, SUBS, stride=2), :] = piece

    firsts, seconds, switches = [], [], []
    for v in range(vregs):
        base = first_pair + (sub + v * SUBS) * per_block

        def order_first(part, base=base):
            return base + part

        def order_second(part, base=base):
            return NM - 1 - (base + part)

        firsts.append(seed(order_first))
        seconds.append(seed(order_second))
        switches.append(NM - (base + which))
        rows = pl.ds(v * SUBS, SUBS)
        for tile in range(steps_pad // LANES):
            if per_block == 1:
                grow_ref[tile, rows, :] = factor_ref[tile, rows, :]
            else:
                even = factor_ref[tile, pl.ds(2 * v * SUBS, SUBS, stride=2), :]
                odd = factor_ref[tile, pl.ds(2 * v * SUBS + 1, SUBS, stride=2), :]
                low = lane < rows_all
                grow_ref[2 * tile, rows, :] = jnp.where(low, even, pltpu.roll(odd, rows_all, 1))
                grow_ref[2 * tile + 1, rows, :] = jnp.where(
                    low, pltpu.roll(even, rows_all, 1), odd
                )

    def advance(tile, offset, state, grows, plain):
        previous, before = state
        index = which * rows_all + offset
        step = tile * step_tile + offset
        produced, kept = [], []
        for v in range(vregs):
            grow = jnp.take_along_axis(grows[v], index, axis=1)
            value = (grow * cosine) * previous[v] - before[v]
            older = previous[v]
            if not plain:
                restart = switches[v] == step
                value = jnp.where(restart, seconds[v], value)
                older = jnp.where(restart, 0.0, older)
            table_ref[pl.ds(step * stride + v * SUBS, SUBS), :] = value
            produced.append(value)
            kept.append(older)
        return (tuple(produced), tuple(kept))

    def run_tile(tile, state, count, unroll, plain=False):
        grows = [grow_ref[tile, pl.ds(v * SUBS, SUBS), :] for v in range(vregs)]

        def body(offset, carry):
            return advance(tile, offset, carry, grows, plain)

        return lax.fori_loop(0, count, body, state, unroll=unroll)

    zeros = tuple(jnp.zeros((SUBS, LANES), jnp.float32) for _ in range(vregs))
    state = (zeros, tuple(-value for value in firsts))
    whole_tiles = STEPS // step_tile
    plain_tiles = (NM // 2 + 1) // step_tile
    state = lax.fori_loop(
        0, plain_tiles, lambda tile, carry: run_tile(tile, carry, step_tile, 16, True), state
    )
    state = lax.fori_loop(
        plain_tiles, whole_tiles, lambda tile, carry: run_tile(tile, carry, step_tile, 16), state
    )
    if STEPS % step_tile:
        run_tile(whole_tiles, state, STEPS % step_tile, STEPS % step_tile % 16)

    for row in range(slot_count):
        for half in range(2):
            stage_ref[row, pl.ds((half + 1) * 2 * pair_pad - 2 * SUBS, 2 * SUBS), :] = jnp.zeros(
                (2 * SUBS, LANES), jnp.float32
            )
    fetch.wait()

    rows_half = slot_count * SUBS
    edges = (0, 256, 512, STEPS)
    dot = functools.partial(jnp.dot, preferred_element_type=jnp.float32)

    def split_parts(values):
        high = values.astype(jnp.bfloat16)
        low = (values - high.astype(jnp.float32)).astype(jnp.bfloat16)
        return high, low

    def product(left, right):
        left_high, left_low = split_parts(left)
        right_high, right_low = split_parts(right)
        rows = left.shape[0]
        both = dot(jnp.concatenate([left_high, left_low], axis=0), right_high)
        return both[:rows] + both[rows:] + dot(left_high, right_low)

    def group(start, kinds):
        values = spectra_ref[:, pl.ds(start, PAIRS), :, :].reshape(slot_count, SUBS, STEPS)
        scale = jnp.concatenate(
            [scale_ref[tile, pl.ds(2 * start, SUBS), :] for tile in range(scale_ref.shape[0])],
            axis=1,
        )
        values = values * scale[:, :STEPS]
        row_pair = lax.broadcasted_iota(jnp.int32, (1, SUBS, STEPS), 1) >> 1
        step = lax.broadcasted_iota(jnp.int32, (1, SUBS, STEPS), 2)
        in_first = step < NM - (first_pair + start + row_pair)
        first_block = start // per_block
        blocks = PAIRS // per_block
        table = jnp.concatenate(
            [table_ref[pl.ds(first_block + n, STEPS, stride=stride), :] for n in range(blocks)],
            axis=1,
        )
        sums = [None, None]
        for begin, end, kind in zip(edges[:-1], edges[1:], ("low",) + kinds):
            piece = values[:, :, begin:end]
            if kind == "both":
                first = in_first[:, :, begin:end]
                piece = jnp.concatenate(
                    [jnp.where(first, piece, 0.0), jnp.where(first, 0.0, piece)], axis=0
                )
            part = product(piece.reshape(-1, end - begin), table[begin:end])
            if kind == "both":
                halves = ((0, part[:rows_half]), (1, part[rows_half:]))
            else:
                halves = ((0 if kind == "low" else 1, part),)
            for half, value in halves:
                sums[half] = value if sums[half] is None else sums[half] + value
        both = jnp.concatenate(sums, axis=0).reshape(2 * slot_count, SUBS, blocks * LANES)
        row_id = lax.broadcasted_iota(jnp.int32, (1, SUBS, LANES), 1) >> 1
        lane_part = lax.broadcasted_iota(jnp.int32, (1, SUBS, LANES), 2)
        lane_part = jnp.where(lane_part < rows_all, 0, 1)
        total = None
        for block in range(blocks):
            part = both[:, :, block * LANES : (block + 1) * LANES]
            keep = row_id == block * per_block + lane_part
            total = jnp.where(keep, part, 0.0 if total is None else total)
        total = total.reshape(2 * rows_half, LANES)
        if per_block == 2:
            total = total + pltpu.roll(total, rows_all, 1)
        total = total.astype(jnp.bfloat16).astype(jnp.float32)
        for half in range(2):
            for row in range(slot_count):
                source = (half * slot_count + row) * SUBS
                stage_ref[row, pl.ds(half * 2 * pair_pad + 2 * start, SUBS), :] = total[
                    source : source + SUBS
                ]

    def twice(kinds):
        def body(index, carry):
            group(index * 2 * PAIRS, kinds)
            group(index * 2 * PAIRS + PAIRS, kinds)
            return carry

        return body

    turns = pair_count // (2 * PAIRS)
    border = NM - edges[2]
    low_turns = jnp.clip((border + 1 - first_pair) // (2 * PAIRS), 0, turns)
    high_turn = jnp.clip((border - first_pair + 2 * PAIRS - 1) // (2 * PAIRS), low_turns, turns)
    lax.fori_loop(0, low_turns, twice(("low", "both")), 0)
    lax.fori_loop(low_turns, high_turn, twice(("both", "both")), 0)
    lax.fori_loop(high_turn, turns, twice(("both", "high")), 0)
    start = turns * 2 * PAIRS
    while start < pair_count:
        group(min(start, pair_count - PAIRS), ("both", "both"))
        start = start + PAIRS

    for row in range(slot_count):
        flipped = stage_ref[row].T
        out_ref[:, pl.ds(row * lat_rows, lat_rows), :] = flipped[:rows_all].reshape(
            lat_count, lat_rows, 4 * pair_pad
        )


def coefficients(spectra, first_pair, rows_all, lat_rows):
    slot_count, _, pair_count, steps = spectra.shape
    per_block = LANES // rows_all
    vregs = pad_to(pair_count, SUBS * per_block) // (SUBS * per_block)
    pairs = vregs * SUBS * per_block
    tile_total = pad_to(STEPS, LANES) // rows_all
    pair_pad = pad_to(pair_count, SUBS)
    lat_count = rows_all // lat_rows
    kernel = functools.partial(
        coeff_kernel, pair_count=pair_count, rows_all=rows_all, lat_rows=lat_rows,
        slot_count=slot_count,
    )
    return pl.pallas_call(
        kernel,
        out_shape=jax.ShapeDtypeStruct(
            (lat_count, slot_count * lat_rows, 4 * pair_pad), jnp.float32
        ),
        in_specs=[
            pl.BlockSpec(memory_space=pltpu.SMEM),
            pl.BlockSpec(memory_space=pl.ANY),
        ],
        out_specs=pl.BlockSpec(memory_space=pltpu.VMEM),
        scratch_shapes=[
            pltpu.VMEM((slot_count, pair_count, 2, steps), jnp.float32),
            pltpu.VMEM((tile_total, vregs * SUBS, LANES), jnp.float32),
            pltpu.VMEM((pad_to(STEPS, LANES) // LANES, pairs, LANES), jnp.float32),
            pltpu.VMEM((pad_to(STEPS, LANES) // LANES, 2 * pairs, LANES), jnp.float32),
            pltpu.VMEM((pad_to(STEPS, SUBS) * (vregs * SUBS + 1), LANES), jnp.float32),
            pltpu.VMEM((slot_count, 4 * pair_pad, LANES), jnp.float32),
            pltpu.SemaphoreType.DMA,
        ],
        compiler_params=pltpu.CompilerParams(vmem_limit_bytes=VMEM_LIMIT),
        name="coefficients",
    )(first_pair, jnp.transpose(spectra, (0, 2, 1, 3)))


def trig_kernel(out_ref, *, pair_count, pair_pad, quarter, fine_total):
    block = pl.program_id(0)
    width = 4 * pair_pad
    coarse_total = pad_to(quarter // fine_total, SUBS)

    def orders(rows):
        lane = lax.broadcasted_iota(jnp.int32, (rows, width), 1)
        upper = lane >= 2 * pair_pad
        pair = jnp.where(upper, lane - 2 * pair_pad, lane)
        is_sine = (pair & 1) == 1
        pair = block * pair_count + (pair >> 1)
        return jnp.where(upper, NM - 1 - pair, pair), is_sine

    def angles(rows, spacing):
        order, _ = orders(rows)
        column = lax.broadcasted_iota(jnp.int32, (rows, width), 0) * spacing
        phase = (order * column % NLON).astype(jnp.float32) * (2.0 * math.pi / NLON)
        return jnp.cos(phase), jnp.sin(phase)

    fine_cos, fine_sin = angles(fine_total, 1)
    coarse_cos, coarse_sin = angles(coarse_total, fine_total)
    _, is_sine = orders(fine_total)
    for tile in range(quarter // fine_total):
        left, right = coarse_cos[tile : tile + 1], coarse_sin[tile : tile + 1]
        cosine = left * fine_cos - right * fine_sin
        sine = right * fine_cos + left * fine_sin
        out_ref[pl.ds(tile * fine_total, fine_total), :] = jnp.where(
            is_sine, sine, cosine
        ).astype(jnp.bfloat16)


def trig_table(pair_count, lon_count):
    pair_pad = pad_to(pair_count, SUBS)
    quarter = NLON // 4
    fine_total = 40
    return pl.pallas_call(
        functools.partial(
            trig_kernel, pair_count=pair_count, pair_pad=pair_pad, quarter=quarter,
            fine_total=fine_total,
        ),
        grid=(lon_count,),
        out_shape=jax.ShapeDtypeStruct((lon_count, quarter, 4 * pair_pad), jnp.bfloat16),
        out_specs=pl.BlockSpec((None, quarter, 4 * pair_pad), lambda b: (b, 0, 0)),
        compiler_params=pltpu.CompilerParams(vmem_limit_bytes=12 * MIB),
        cost_estimate=pl.CostEstimate(
            flops=24 * lon_count * quarter * pair_pad,
            bytes_accessed=lon_count * quarter * 8 * pair_pad,
            transcendentals=0,
        ),
        name="trig_table",
    )()


def grid_kernel(lon_ref, trig_ref, coeff_ref, *refs, lon_count, pair_count):
    flat_ref, right_ref = refs[lon_count:]
    share = coeff_ref.shape[1]
    width = coeff_ref.shape[2]
    rows = coeff_ref.shape[0] // lon_count * share
    values = coeff_ref[...].reshape(rows // share, lon_count, share, width)
    line = lax.broadcasted_iota(jnp.int32, (width, rows), 0)
    upper = line >= width // 2
    pair = jnp.where(upper, line - width // 2, line)
    is_sine = (pair & 1) == 1
    for block in range(lon_count):
        flat = values[:, block].reshape(rows, width).T
        swapped = jnp.where(is_sine, -pltpu.roll(flat, 1, 0), pltpu.roll(flat, width - 1, 0))
        order = block * pair_count + (pair >> 1)
        order = jnp.where(upper, NM - 1 - order, order) & 3
        odd = (order & 1) == 1
        flip = jnp.where(odd, -flat, flat)
        turned = jnp.where(order == 1, swapped, jnp.where(order == 3, -swapped, flat))
        turned = jnp.where(order == 2, -flat, turned)
        back = jnp.where(odd, -turned, turned)
        for turn, part in enumerate((flat, turned, flip, back)):
            right_ref[pl.ds(block * width, width), pl.ds(turn * rows, rows)] = part.astype(
                jnp.bfloat16
            )
    total = None
    for block in range(lon_count):
        part = jnp.dot(
            trig_ref[block],
            right_ref[pl.ds(block * width, width), :],
            preferred_element_type=jnp.float32,
        )
        total = part if total is None else total + part
    quarter = total.shape[0]
    for turn in range(4):
        flat_ref[pl.ds(turn * quarter, quarter), :] = total[:, turn * rows : (turn + 1) * rows]
    cols = NLON // lon_count
    for part in range(lon_count):
        refs[part][...] = flat_ref[pl.ds((lon_ref[0] ^ part) * cols, cols), :]


def grid_field(lon, trig, coeffs, pair_count):
    lon_count, quarter, width = trig.shape
    rows = coeffs.shape[0] // lon_count * coeffs.shape[1]
    return pl.pallas_call(
        functools.partial(grid_kernel, lon_count=lon_count, pair_count=pair_count),
        out_shape=[jax.ShapeDtypeStruct((NLON // lon_count, rows), jnp.float32)] * lon_count,
        in_specs=[pl.BlockSpec(memory_space=pltpu.SMEM)]
        + [pl.BlockSpec(memory_space=pltpu.VMEM)] * 2,
        out_specs=[pl.BlockSpec(memory_space=pltpu.VMEM)] * lon_count,
        scratch_shapes=[
            pltpu.VMEM((4 * quarter, rows), jnp.float32),
            pltpu.VMEM((lon_count * width, 4 * rows), jnp.bfloat16),
        ],
        compiler_params=pltpu.CompilerParams(vmem_limit_bytes=16 * MIB),
        cost_estimate=pl.CostEstimate(
            flops=2 * NLON * lon_count * width * rows,
            bytes_accessed=trig.size * 2 + 2 * coeffs.size * 4,
            transcendentals=0,
        ),
        name="grid_field",
    )(lon, trig, coeffs)


def gelu_parts(preact):
    scale = math.sqrt(2.0 / math.pi)
    square = preact * preact
    bend = jnp.tanh(scale * (preact + 0.044715 * (square * preact)))
    half = 0.5 * (1.0 + bend)
    slope = half + (0.5 * preact) * (1.0 - bend * bend) * (
        scale * (1.0 + (3.0 * 0.044715) * square)
    )
    return preact * half, slope


def forward_kernel(latents_ref, w_ref, b_ref, _, slope_ref, hidden_t_ref, latents_t_ref):
    latents = latents_ref[...]
    preact = jnp.dot(latents, w_ref[...], preferred_element_type=jnp.float32) + b_ref[...]
    hidden, slope = gelu_parts(preact)
    slope_ref[...] = slope
    hidden_t_ref[...] = hidden.T.astype(jnp.bfloat16)
    latents_t_ref[...] = latents.T


def forward(latents, w_hidden, b_hidden, after, parts):
    cells, width = latents.shape
    cols = cells // parts
    return pl.pallas_call(
        forward_kernel,
        grid=(parts,),
        out_shape=(
            jax.ShapeDtypeStruct((cells, width), jnp.float32),
            jax.ShapeDtypeStruct((parts, width, cols), jnp.bfloat16),
            jax.ShapeDtypeStruct((parts, width, cols), jnp.bfloat16),
        ),
        in_specs=[
            pl.BlockSpec((cols, width), lambda i: (i, 0)),
            pl.BlockSpec((width, width), lambda i: (0, 0)),
            pl.BlockSpec((1, width), lambda i: (0, 0)),
            pl.BlockSpec(memory_space=pl.ANY),
        ],
        out_specs=(
            pl.BlockSpec((cols, width), lambda i: (i, 0)),
            pl.BlockSpec((None, width, cols), lambda i: (i, 0, 0)),
            pl.BlockSpec((None, width, cols), lambda i: (i, 0, 0)),
        ),
        compiler_params=pltpu.CompilerParams(vmem_limit_bytes=32 * MIB),
        cost_estimate=pl.CostEstimate(
            flops=2 * cells * width * width,
            bytes_accessed=cells * width * 10,
            transcendentals=cells * width,
        ),
        name="forward",
    )(latents, w_hidden, b_hidden.reshape(1, width), after)


def backward_kernel(
    core_ref, scale_ref, place_ref, w_out_ref, slope_ref, hidden_t_ref, latents_t_ref, *refs,
    blocks,
):
    grid_refs = refs[:blocks]
    preact_ref, keep_ref, send_ref = refs[blocks : blocks + 3]
    field_ref, hidden_acc, out_acc, bias_acc, sums_ref = refs[blocks + 3 :]
    index = pl.program_id(0)
    total = pl.num_programs(0)
    lon_cols = grid_refs[0].shape[0]
    width = hidden_acc.shape[0]
    cols = slope_ref.shape[0]
    sum_rows = sums_ref.shape[0]

    @pl.when(index == 0)
    def _():
        field = None
        for block in range(blocks):
            scaled = (grid_refs[block][...] * scale_ref[block]).astype(jnp.bfloat16)
            part = jnp.dot(scaled, place_ref[block], preferred_element_type=jnp.float32)
            field = part if field is None else field + part
        for row in range(field.shape[1] // LANES):
            field_ref[pl.ds(row * lon_cols, lon_cols), :] = field[
                :, row * LANES : (row + 1) * LANES
            ]
        hidden_acc[...] = jnp.zeros_like(hidden_acc)
        out_acc[...] = jnp.zeros_like(out_acc)
        bias_acc[...] = jnp.zeros_like(bias_acc)

    field = field_ref[pl.ds(pl.multiple_of(index * cols, SUBS), cols), :].astype(jnp.bfloat16)
    back = jnp.dot(field, w_out_ref[...], preferred_element_type=jnp.float32)
    preact_back = (back * slope_ref[...]).astype(jnp.bfloat16)
    preact_ref[...] = preact_back
    hidden_acc[...] += jnp.dot(
        latents_t_ref[...], preact_back, preferred_element_type=jnp.float32
    )
    out_acc[...] += jnp.dot(hidden_t_ref[...], field, preferred_element_type=jnp.float32)
    bias_acc[...] += jnp.sum(preact_back.astype(jnp.float32), axis=0, keepdims=True)

    @pl.when(index == total - 1)
    def _():
        tiles = width // LANES
        for row_tile in range(width // SUBS):
            for tile in range(tiles):
                sums_ref[pl.ds((row_tile * tiles + tile) * SUBS, SUBS), :] = hidden_acc[
                    pl.ds(row_tile * SUBS, SUBS), pl.ds(tile * LANES, LANES)
                ]
        base = width * tiles
        flipped = out_acc[...].T
        for tile in range(tiles):
            sums_ref[pl.ds(base + tile * F, F), :] = flipped[:F, tile * LANES : (tile + 1) * LANES]
        base = base + tiles * F
        sums_ref[pl.ds(base, sum_rows - base), :] = jnp.zeros((sum_rows - base, LANES), jnp.float32)
        for tile in range(tiles):
            sums_ref[pl.ds(base + tile, 1), :] = bias_acc[:, tile * LANES : (tile + 1) * LANES]
        half = sum_rows // 2
        mine = core_ref[0]
        keep_ref[...] = sums_ref[pl.ds(pl.multiple_of(mine * half, SUBS), half), :]
        send_ref[...] = sums_ref[pl.ds(pl.multiple_of((1 - mine) * half, SUBS), half), :]


def backward(core, grids, scale, place, w_out_t, slope, hidden_t, latents_t, sum_rows):
    cells, width = slope.shape
    blocks = len(grids)
    parts, _, cols = hidden_t.shape
    half = (sum_rows // 2, LANES)
    whole3 = lambda i: (0, 0, 0)
    whole2 = lambda i: (0, 0)
    return pl.pallas_call(
        functools.partial(backward_kernel, blocks=blocks),
        grid=(parts,),
        out_shape=(
            jax.ShapeDtypeStruct((cells, width), jnp.bfloat16),
            jax.ShapeDtypeStruct(half, jnp.float32),
            jax.ShapeDtypeStruct(half, jnp.float32),
        ),
        in_specs=[
            pl.BlockSpec(memory_space=pltpu.SMEM),
            pl.BlockSpec(scale.shape, whole3),
            pl.BlockSpec(place.shape, whole3),
            pl.BlockSpec(w_out_t.shape, whole2),
            pl.BlockSpec((cols, width), lambda i: (i, 0)),
            pl.BlockSpec((None, width, cols), lambda i: (i, 0, 0)),
            pl.BlockSpec((None, width, cols), lambda i: (i, 0, 0)),
        ]
        + [pl.BlockSpec(grids[0].shape, whole2)] * blocks,
        out_specs=(
            pl.BlockSpec((cols, width), lambda i: (i, 0)),
            pl.BlockSpec(half, whole2),
            pl.BlockSpec(half, whole2),
        ),
        scratch_shapes=[
            pltpu.VMEM((cells, LANES), jnp.float32),
            pltpu.VMEM((width, width), jnp.float32),
            pltpu.VMEM((width, LANES), jnp.float32),
            pltpu.VMEM((1, width), jnp.float32),
            pltpu.VMEM((sum_rows, LANES), jnp.float32),
        ],
        compiler_params=pltpu.CompilerParams(vmem_limit_bytes=32 * MIB),
        cost_estimate=pl.CostEstimate(
            flops=2 * cells * width * (width + 2 * LANES),
            bytes_accessed=cells * width * 10,
            transcendentals=0,
        ),
        name="backward",
    )(core, scale, place, w_out_t, slope, hidden_t, latents_t, *grids)


def add_kernel(index_ref, *refs, inputs, outputs, factor):
    size = refs[0].shape[0] // outputs
    for part in range(outputs):
        start = 0 if outputs == 1 else pl.multiple_of((index_ref[0] ^ part) * size, SUBS)
        total = refs[0][pl.ds(start, size), :]
        for piece in refs[1:inputs]:
            total = total + piece[pl.ds(start, size), :]
        if factor is not None:
            total = total * factor
        refs[inputs + part][...] = total


def add_pieces(index, pieces, outputs, factor=None):
    rows = pieces[0].shape[0]
    size = rows // outputs
    return pl.pallas_call(
        functools.partial(add_kernel, inputs=len(pieces), outputs=outputs, factor=factor),
        out_shape=[jax.ShapeDtypeStruct((size, LANES), jnp.float32)] * outputs,
        in_specs=[pl.BlockSpec(memory_space=pltpu.SMEM)]
        + [pl.BlockSpec(memory_space=pltpu.VMEM)] * len(pieces),
        out_specs=[pl.BlockSpec(memory_space=pltpu.VMEM)] * outputs,
        cost_estimate=pl.CostEstimate(
            flops=len(pieces) * rows * LANES,
            bytes_accessed=4 * (len(pieces) + 1) * rows * LANES,
            transcendentals=0,
        ),
        compiler_params=pltpu.CompilerParams(vmem_limit_bytes=6 * MIB),
        name="add_pieces",
    )(index, *pieces)


def finish_kernel(place_ref, *refs, lon_count, depth):
    hidden_ref, bias_ref, out_ref, flat_ref = refs[2 * lon_count :]
    core, lon, deep = place_ref[0], place_ref[1], place_ref[2]
    size = refs[0].shape[0] // depth
    for half in range(2):
        for part in range(lon_count):
            for piece in range(depth):
                start = (((core ^ half) * lon_count + (lon ^ part)) * depth + (deep ^ piece)) * size
                flat_ref[pl.ds(pl.multiple_of(start, SUBS), size), :] = refs[
                    half * lon_count + part
                ][pl.ds(piece * size, size), :]
    width = hidden_ref.shape[0]
    tiles = width // LANES
    for row_tile in range(width // SUBS):
        for tile in range(tiles):
            hidden_ref[pl.ds(row_tile * SUBS, SUBS), pl.ds(tile * LANES, LANES)] = flat_ref[
                pl.ds((row_tile * tiles + tile) * SUBS, SUBS), :
            ]
    base = width * tiles
    for tile in range(tiles):
        out_ref[:, pl.ds(tile * LANES, LANES)] = flat_ref[pl.ds(base + tile * F, F), :]
        bias_ref[:, pl.ds(tile * LANES, LANES)] = flat_ref[pl.ds(base + tiles * F + tile, 1), :]


def finish(place, pieces, width, depth):
    lon_count = len(pieces) // 2
    return pl.pallas_call(
        functools.partial(finish_kernel, lon_count=lon_count, depth=depth),
        out_shape=(
            jax.ShapeDtypeStruct((width, width), jnp.float32),
            jax.ShapeDtypeStruct((1, width), jnp.float32),
            jax.ShapeDtypeStruct((F, width), jnp.float32),
        ),
        in_specs=[pl.BlockSpec(memory_space=pltpu.SMEM)]
        + [pl.BlockSpec(memory_space=pltpu.VMEM)] * len(pieces),
        out_specs=(pl.BlockSpec(memory_space=pltpu.VMEM),) * 3,
        scratch_shapes=[pltpu.VMEM((len(pieces) * pieces[0].shape[0], LANES), jnp.float32)],
        compiler_params=pltpu.CompilerParams(vmem_limit_bytes=8 * MIB),
        name="finish",
    )(place, *pieces)


def swap(value, axis, bits):
    count = lax.axis_size(axis)
    return lax.ppermute(value, axis, [(i, i ^ bits) for i in range(count)])


def local(spectra, field_slot, field_weight, latents, w_hidden, b_hidden, w_out):
    slot_count, _, pair_count, _ = spectra.shape
    lat_rows, lon_cols, width = latents.shape
    lat_count = lax.axis_size("lat")
    lon_count = lax.axis_size("lon")
    rows_all = lat_rows * lat_count
    lat_index = lax.axis_index("lat").astype(jnp.int32)
    lon_index = lax.axis_index("lon").astype(jnp.int32)
    pair_pad = pad_to(pair_count, SUBS)
    cells = lat_rows * lon_cols
    parts = 4

    coeffs = coefficients(spectra, (lon_index * pair_count).reshape(1), rows_all, lat_rows)
    share = slot_count * lat_rows // lon_count
    coeffs = coeffs.reshape(lat_count * lon_count, share, 4 * pair_pad)
    coeffs = lax.all_to_all(coeffs, ("lat", "lon"), split_axis=0, concat_axis=0, tiled=True)

    trig = trig_table(pair_count, lon_count)

    lanes = lat_count * share

    def spread(values):
        values = jnp.broadcast_to(values, (lat_count, slot_count, lat_rows))
        values = values.reshape(lat_count, lon_count, share)
        values = jnp.transpose(values, (1, 0, 2)).reshape(lon_count, lanes)
        arrival = lon_index ^ jnp.arange(lon_count, dtype=jnp.int32)
        chosen = arrival[:, None] == jnp.arange(lon_count, dtype=jnp.int32)
        return jnp.sum(jnp.where(chosen[:, :, None], values[None], 0), axis=1)

    field_ids = spread(field_slot.reshape(lat_count, slot_count, 1))
    row_ids = spread(jnp.arange(lat_rows, dtype=jnp.int32).reshape(1, 1, lat_rows))
    chosen = field_ids[:, :, None] == jnp.arange(F, dtype=jnp.int32)
    weight = jnp.sum(jnp.where(chosen, field_weight, 0.0), axis=2)
    sine = jnp.sin(band_angles(lat_index * lat_rows + row_ids, rows_all))
    scale = (sine * weight)[:, None, :]
    target = row_ids * LANES + field_ids
    place = (
        target[:, :, None] == jnp.arange(lat_rows * LANES, dtype=jnp.int32)[None, None, :]
    ).astype(jnp.bfloat16)
    w_out_t = jnp.concatenate([w_out.T, jnp.zeros((LANES - F, width), w_out.dtype)], axis=0)

    core_index, deep_index = lat_index & 1, lat_index >> 1
    depth = lat_count // 2
    spots = jnp.stack([core_index, lon_index, deep_index])
    grids = grid_field(lon_index.reshape(1), trig, coeffs, pair_count)
    slope, hidden_t, latents_t = forward(
        latents.reshape(cells, width), w_hidden, b_hidden, grids[0], parts
    )
    grids = [grids[0]] + [swap(grids[part], "lon", part) for part in range(1, lon_count)]

    device_count = lat_count * lon_count
    used_rows = (width + F + 1) * width // LANES
    chunk = pad_to(pad_to(used_rows, device_count) // device_count, SUBS)
    preact_back, keep, send = backward(
        core_index.reshape(1), grids, scale, place, w_out_t, slope, hidden_t, latents_t,
        chunk * device_count,
    )
    latent_grad = lax.dot_general(
        preact_back, w_hidden, (((1,), (1,)), ((), ())), preferred_element_type=jnp.float32
    ).astype(jnp.bfloat16)

    pieces = add_pieces(
        lon_index.reshape(1), [keep, swap(send, "lat", 1)], lon_count
    )
    arrived = [swap(pieces[part], "lon", part) for part in range(1, lon_count)]
    arrived, latent_grad = lax.optimization_barrier((arrived, latent_grad))
    pieces = add_pieces(deep_index.reshape(1), [pieces[0]] + arrived, depth)
    arrived = [swap(pieces[part], "lat", 2 * part) for part in range(1, depth)]
    norm = 1.0 / math.sqrt(rows_all * NLON)
    total = add_pieces(deep_index.reshape(1), [pieces[0]] + arrived, 1, norm)[0]
    total = jnp.concatenate([total] + [swap(total, "lat", 2 * part) for part in range(1, depth)])
    totals = [total] + [swap(total, "lon", part) for part in range(1, lon_count)]
    totals = totals + [swap(piece, "lat", 1) for piece in totals]
    hidden_grad, bias_grad, out_grad = finish(spots, totals, width, depth)
    return (
        latent_grad.reshape(lat_rows, lon_cols, width),
        hidden_grad,
        bias_grad.reshape(width),
        out_grad.T,
    )


def solution(mesh):
    in_specs = (P("lat", None, "lon", None), P(), P(), P("lat", "lon", None), P(), P(), P())
    out_specs = (P("lat", "lon", None), P(), P(), P())
    return jax.shard_map(local, mesh=mesh, in_specs=in_specs, out_specs=out_specs, check_vma=False)
```

```python
import functools
import math

import jax
import jax.numpy as jnp
from jax import lax
from jax.experimental import pallas as pl
from jax.experimental.pallas import tpu as pltpu
from jax.sharding import PartitionSpec as P

NM = 720
NLON = 1440
F = 64
LANES = 128
SUBS = 8
STEPS = NM + 1
PAIRS = 4
MIB = 1024 * 1024
VMEM_LIMIT = 56 * MIB


def band_angles(row_ids, rows_all):
    return jnp.pi * (NM // 2 - rows_all // 2 + row_ids.astype(jnp.float32)) / NM


def pad_to(value, multiple):
    return (value + multiple - 1) // multiple * multiple


def coeff_kernel(
    first_ref, spectra_hbm, out_ref, spectra_ref, grow_ref, factor_ref, scale_ref, table_ref,
    stage_ref, copy_sem, *, pair_count, rows_all, lat_rows, slot_count,
):
    per_block = LANES // rows_all
    vregs = pad_to(pair_count, SUBS * per_block) // (SUBS * per_block)
    step_tile = rows_all
    stride = vregs * SUBS + 1
    pair_pad = pad_to(pair_count, SUBS)
    lat_count = rows_all // lat_rows
    first_pair = first_ref[0]

    fetch = pltpu.make_async_copy(spectra_hbm, spectra_ref, copy_sem)
    fetch.start()

    lane = lax.broadcasted_iota(jnp.int32, (SUBS, LANES), 1)
    sub = lax.broadcasted_iota(jnp.int32, (SUBS, LANES), 0)
    inner = lane & (rows_all - 1)
    which = lane // rows_all
    colatitude = band_angles(inner, rows_all)
    cosine = jnp.cos(colatitude)
    log_sine = jnp.log(jnp.sin(colatitude))

    def log_total(order_column):
        total = jnp.zeros((SUBS, LANES), jnp.float32)
        for tile in range(pad_to(NM, LANES) // LANES):
            term = (lane + tile * LANES).astype(jnp.float32)
            safe = jnp.maximum(term, 1.0)
            value = jnp.log((2.0 * safe + 1.0) / (2.0 * safe))
            total = total + jnp.where((term >= 1.0) & (term <= order_column), value, 0.0)
        return jnp.sum(total, axis=1, keepdims=True)

    def seed(order_of):
        total = jnp.zeros((SUBS, LANES), jnp.float32)
        for part in range(per_block):
            column = order_of(part).astype(jnp.float32)
            total = jnp.where(which == part, log_total(column), total)
        order = order_of(which).astype(jnp.float32)
        return jnp.exp(0.5 * total - 0.5 * math.log(4.0 * math.pi) + order * log_sine)

    pairs = vregs * SUBS * per_block
    steps_pad = pad_to(STEPS, LANES)
    step = lax.broadcasted_iota(jnp.int32, (pairs, steps_pad), 1)
    pair = first_pair + lax.broadcasted_iota(jnp.int32, (pairs, steps_pad), 0)
    switch = NM - pair
    in_first = step < switch
    order = jnp.where(in_first, pair, NM - 1 - pair).astype(jnp.float32)
    degree = jnp.where(in_first, pair + step, step - 1).astype(jnp.float32)
    grow = jnp.sqrt(
        jnp.maximum(4.0 * degree * degree - 1.0, 1.0)
        / jnp.maximum(degree * degree - order * order, 1.0)
    )
    since = jnp.where(in_first, step, step - switch)
    scale = jnp.where(since >= 2, grow / pltpu.roll(grow, 1, 1), 1.0)
    shift = 2
    while shift < STEPS:
        scale = jnp.where(since >= shift, scale * pltpu.roll(scale, shift, 1), scale)
        shift = 2 * shift
    factor = grow * pltpu.roll(scale, 1, 1) / scale
    for tile in range(steps_pad // LANES):
        factor_ref[tile] = factor[:, tile * LANES : (tile + 1) * LANES]
        for row in range(0, pairs, SUBS):
            piece = scale[row : row + SUBS, tile * LANES : (tile + 1) * LANES]
            for part in range(2):
                scale_ref[tile, pl.ds(2 * row + part, SUBS, stride=2), :] = piece

    firsts, seconds, switches = [], [], []
    for v in range(vregs):
        base = first_pair + (sub + v * SUBS) * per_block

        def order_first(part, base=base):
            return base + part

        def order_second(part, base=base):
            return NM - 1 - (base + part)

        firsts.append(seed(order_first))
        seconds.append(seed(order_second))
        switches.append(NM - (base + which))
        rows = pl.ds(v * SUBS, SUBS)
        for tile in range(steps_pad // LANES):
            if per_block == 1:
                grow_ref[tile, rows, :] = factor_ref[tile, rows, :]
            else:
                even = factor_ref[tile, pl.ds(2 * v * SUBS, SUBS, stride=2), :]
                odd = factor_ref[tile, pl.ds(2 * v * SUBS + 1, SUBS, stride=2), :]
                low = lane < rows_all
                grow_ref[2 * tile, rows, :] = jnp.where(low, even, pltpu.roll(odd, rows_all, 1))
                grow_ref[2 * tile + 1, rows, :] = jnp.where(
                    low, pltpu.roll(even, rows_all, 1), odd
                )

    def advance(tile, offset, state, grows, plain):
        previous, before = state
        index = which * rows_all + offset
        step = tile * step_tile + offset
        produced, kept = [], []
        for v in range(vregs):
            grow = jnp.take_along_axis(grows[v], index, axis=1)
            value = (grow * cosine) * previous[v] - before[v]
            older = previous[v]
            if not plain:
                restart = switches[v] == step
                value = jnp.where(restart, seconds[v], value)
                older = jnp.where(restart, 0.0, older)
            table_ref[pl.ds(step * stride + v * SUBS, SUBS), :] = value
            produced.append(value)
            kept.append(older)
        return (tuple(produced), tuple(kept))

    def run_tile(tile, state, count, unroll, plain=False):
        grows = [grow_ref[tile, pl.ds(v * SUBS, SUBS), :] for v in range(vregs)]

        def body(offset, carry):
            return advance(tile, offset, carry, grows, plain)

        return lax.fori_loop(0, count, body, state, unroll=unroll)

    zeros = tuple(jnp.zeros((SUBS, LANES), jnp.float32) for _ in range(vregs))
    state = (zeros, tuple(-value for value in firsts))
    whole_tiles = STEPS // step_tile
    plain_tiles = (NM // 2 + 1) // step_tile
    state = lax.fori_loop(
        0, plain_tiles, lambda tile, carry: run_tile(tile, carry, step_tile, 16, True), state
    )
    state = lax.fori_loop(
        plain_tiles, whole_tiles, lambda tile, carry: run_tile(tile, carry, step_tile, 16), state
    )
    if STEPS % step_tile:
        run_tile(whole_tiles, state, STEPS % step_tile, STEPS % step_tile % 16)

    for row in range(slot_count):
        for half in range(2):
            stage_ref[row, pl.ds((half + 1) * 2 * pair_pad - 2 * SUBS, 2 * SUBS), :] = jnp.zeros(
                (2 * SUBS, LANES), jnp.float32
            )
    fetch.wait()

    rows_half = slot_count * SUBS
    edges = (0, 256, 512, STEPS)
    dot = functools.partial(jnp.dot, preferred_element_type=jnp.float32)

    def split_parts(values):
        high = values.astype(jnp.bfloat16)
        low = (values - high.astype(jnp.float32)).astype(jnp.bfloat16)
        return high, low

    def product(left, right):
        left_high, left_low = split_parts(left)
        right_high, right_low = split_parts(right)
        rows = left.shape[0]
        both = dot(jnp.concatenate([left_high, left_low], axis=0), right_high)
        return both[:rows] + both[rows:] + dot(left_high, right_low)

    def group(start, kinds):
        values = spectra_ref[:, pl.ds(start, PAIRS), :, :].reshape(slot_count, SUBS, STEPS)
        scale = jnp.concatenate(
            [scale_ref[tile, pl.ds(2 * start, SUBS), :] for tile in range(scale_ref.shape[0])],
            axis=1,
        )
        values = values * scale[:, :STEPS]
        row_pair = lax.broadcasted_iota(jnp.int32, (1, SUBS, STEPS), 1) >> 1
        step = lax.broadcasted_iota(jnp.int32, (1, SUBS, STEPS), 2)
        in_first = step < NM - (first_pair + start + row_pair)
        first_block = start // per_block
        blocks = PAIRS // per_block
        table = jnp.concatenate(
            [table_ref[pl.ds(first_block + n, STEPS, stride=stride), :] for n in range(blocks)],
            axis=1,
        )
        sums = [None, None]
        for begin, end, kind in zip(edges[:-1], edges[1:], ("low",) + kinds):
            piece = values[:, :, begin:end]
            if kind == "both":
                first = in_first[:, :, begin:end]
                piece = jnp.concatenate(
                    [jnp.where(first, piece, 0.0), jnp.where(first, 0.0, piece)], axis=0
                )
            part = product(piece.reshape(-1, end - begin), table[begin:end])
            if kind == "both":
                halves = ((0, part[:rows_half]), (1, part[rows_half:]))
            else:
                halves = ((0 if kind == "low" else 1, part),)
            for half, value in halves:
                sums[half] = value if sums[half] is None else sums[half] + value
        both = jnp.concatenate(sums, axis=0).reshape(2 * slot_count, SUBS, blocks * LANES)
        row_id = lax.broadcasted_iota(jnp.int32, (1, SUBS, LANES), 1) >> 1
        lane_part = lax.broadcasted_iota(jnp.int32, (1, SUBS, LANES), 2)
        lane_part = jnp.where(lane_part < rows_all, 0, 1)
        total = None
        for block in range(blocks):
            part = both[:, :, block * LANES : (block + 1) * LANES]
            keep = row_id == block * per_block + lane_part
            total = jnp.where(keep, part, 0.0 if total is None else total)
        total = total.reshape(2 * rows_half, LANES)
        if per_block == 2:
            total = total + pltpu.roll(total, rows_all, 1)
        total = total.astype(jnp.bfloat16).astype(jnp.float32)
        for half in range(2):
            for row in range(slot_count):
                source = (half * slot_count + row) * SUBS
                stage_ref[row, pl.ds(half * 2 * pair_pad + 2 * start, SUBS), :] = total[
                    source : source + SUBS
                ]

    def twice(kinds):
        def body(index, carry):
            group(index * 2 * PAIRS, kinds)
            group(index * 2 * PAIRS + PAIRS, kinds)
            return carry

        return body

    turns = pair_count // (2 * PAIRS)
    border = NM - edges[2]
    low_turns = jnp.clip((border + 1 - first_pair) // (2 * PAIRS), 0, turns)
    high_turn = jnp.clip((border - first_pair + 2 * PAIRS - 1) // (2 * PAIRS), low_turns, turns)
    lax.fori_loop(0, low_turns, twice(("low", "both")), 0)
    lax.fori_loop(low_turns, high_turn, twice(("both", "both")), 0)
    lax.fori_loop(high_turn, turns, twice(("both", "high")), 0)
    start = turns * 2 * PAIRS
    while start < pair_count:
        group(min(start, pair_count - PAIRS), ("both", "both"))
        start = start + PAIRS

    for row in range(slot_count):
        flipped = stage_ref[row].T
        out_ref[:, pl.ds(row * lat_rows, lat_rows), :] = flipped[:rows_all].reshape(
            lat_count, lat_rows, 4 * pair_pad
        )


def coefficients(spectra, first_pair, rows_all, lat_rows):
    slot_count, _, pair_count, steps = spectra.shape
    per_block = LANES // rows_all
    vregs = pad_to(pair_count, SUBS * per_block) // (SUBS * per_block)
    pairs = vregs * SUBS * per_block
    tile_total = pad_to(STEPS, LANES) // rows_all
    pair_pad = pad_to(pair_count, SUBS)
    lat_count = rows_all // lat_rows
    kernel = functools.partial(
        coeff_kernel, pair_count=pair_count, rows_all=rows_all, lat_rows=lat_rows,
        slot_count=slot_count,
    )
    return pl.pallas_call(
        kernel,
        out_shape=jax.ShapeDtypeStruct(
            (lat_count, slot_count * lat_rows, 4 * pair_pad), jnp.float32
        ),
        in_specs=[
            pl.BlockSpec(memory_space=pltpu.SMEM),
            pl.BlockSpec(memory_space=pl.ANY),
        ],
        out_specs=pl.BlockSpec(memory_space=pltpu.VMEM),
        scratch_shapes=[
            pltpu.VMEM((slot_count, pair_count, 2, steps), jnp.float32),
            pltpu.VMEM((tile_total, vregs * SUBS, LANES), jnp.float32),
            pltpu.VMEM((pad_to(STEPS, LANES) // LANES, pairs, LANES), jnp.float32),
            pltpu.VMEM((pad_to(STEPS, LANES) // LANES, 2 * pairs, LANES), jnp.float32),
            pltpu.VMEM((pad_to(STEPS, SUBS) * (vregs * SUBS + 1), LANES), jnp.float32),
            pltpu.VMEM((slot_count, 4 * pair_pad, LANES), jnp.float32),
            pltpu.SemaphoreType.DMA,
        ],
        compiler_params=pltpu.CompilerParams(vmem_limit_bytes=VMEM_LIMIT),
        name="coefficients",
    )(first_pair, jnp.transpose(spectra, (0, 2, 1, 3)))


def trig_kernel(out_ref, *, pair_count, pair_pad, quarter, fine_total):
    block = pl.program_id(0)
    width = 4 * pair_pad
    coarse_total = pad_to(quarter // fine_total, SUBS)

    def orders(rows):
        lane = lax.broadcasted_iota(jnp.int32, (rows, width), 1)
        upper = lane >= 2 * pair_pad
        pair = jnp.where(upper, lane - 2 * pair_pad, lane)
        is_sine = (pair & 1) == 1
        pair = block * pair_count + (pair >> 1)
        return jnp.where(upper, NM - 1 - pair, pair), is_sine

    def angles(rows, spacing):
        order, _ = orders(rows)
        column = lax.broadcasted_iota(jnp.int32, (rows, width), 0) * spacing
        phase = (order * column % NLON).astype(jnp.float32) * (2.0 * math.pi / NLON)
        return jnp.cos(phase), jnp.sin(phase)

    fine_cos, fine_sin = angles(fine_total, 1)
    coarse_cos, coarse_sin = angles(coarse_total, fine_total)
    _, is_sine = orders(fine_total)
    for tile in range(quarter // fine_total):
        left, right = coarse_cos[tile : tile + 1], coarse_sin[tile : tile + 1]
        cosine = left * fine_cos - right * fine_sin
        sine = right * fine_cos + left * fine_sin
        out_ref[pl.ds(tile * fine_total, fine_total), :] = jnp.where(
            is_sine, sine, cosine
        ).astype(jnp.bfloat16)


def trig_table(pair_count, lon_count):
    pair_pad = pad_to(pair_count, SUBS)
    quarter = NLON // 4
    fine_total = 40
    return pl.pallas_call(
        functools.partial(
            trig_kernel, pair_count=pair_count, pair_pad=pair_pad, quarter=quarter,
            fine_total=fine_total,
        ),
        grid=(lon_count,),
        out_shape=jax.ShapeDtypeStruct((lon_count, quarter, 4 * pair_pad), jnp.bfloat16),
        out_specs=pl.BlockSpec((None, quarter, 4 * pair_pad), lambda b: (b, 0, 0)),
        compiler_params=pltpu.CompilerParams(vmem_limit_bytes=12 * MIB),
        cost_estimate=pl.CostEstimate(
            flops=24 * lon_count * quarter * pair_pad,
            bytes_accessed=lon_count * quarter * 8 * pair_pad,
            transcendentals=0,
        ),
        name="trig_table",
    )()


def grid_kernel(lon_ref, trig_ref, coeff_ref, *refs, lon_count, pair_count):
    flat_ref, right_ref = refs[lon_count:]
    share = coeff_ref.shape[1]
    width = coeff_ref.shape[2]
    rows = coeff_ref.shape[0] // lon_count * share
    values = coeff_ref[...].reshape(rows // share, lon_count, share, width)
    line = lax.broadcasted_iota(jnp.int32, (width, rows), 0)
    upper = line >= width // 2
    pair = jnp.where(upper, line - width // 2, line)
    is_sine = (pair & 1) == 1
    for block in range(lon_count):
        flat = values[:, block].reshape(rows, width).T
        swapped = jnp.where(is_sine, -pltpu.roll(flat, 1, 0), pltpu.roll(flat, width - 1, 0))
        order = block * pair_count + (pair >> 1)
        order = jnp.where(upper, NM - 1 - order, order) & 3
        odd = (order & 1) == 1
        flip = jnp.where(odd, -flat, flat)
        turned = jnp.where(order == 1, swapped, jnp.where(order == 3, -swapped, flat))
        turned = jnp.where(order == 2, -flat, turned)
        back = jnp.where(odd, -turned, turned)
        for turn, part in enumerate((flat, turned, flip, back)):
            right_ref[pl.ds(block * width, width), pl.ds(turn * rows, rows)] = part.astype(
                jnp.bfloat16
            )
    total = None
    for block in range(lon_count):
        part = jnp.dot(
            trig_ref[block],
            right_ref[pl.ds(block * width, width), :],
            preferred_element_type=jnp.float32,
        )
        total = part if total is None else total + part
    quarter = total.shape[0]
    for turn in range(4):
        flat_ref[pl.ds(turn * quarter, quarter), :] = total[:, turn * rows : (turn + 1) * rows]
    cols = NLON // lon_count
    for part in range(lon_count):
        refs[part][...] = flat_ref[pl.ds((lon_ref[0] ^ part) * cols, cols), :]


def grid_field(lon, trig, coeffs, pair_count):
    lon_count, quarter, width = trig.shape
    rows = coeffs.shape[0] // lon_count * coeffs.shape[1]
    return pl.pallas_call(
        functools.partial(grid_kernel, lon_count=lon_count, pair_count=pair_count),
        out_shape=[jax.ShapeDtypeStruct((NLON // lon_count, rows), jnp.float32)] * lon_count,
        in_specs=[pl.BlockSpec(memory_space=pltpu.SMEM)]
        + [pl.BlockSpec(memory_space=pltpu.VMEM)] * 2,
        out_specs=[pl.BlockSpec(memory_space=pltpu.VMEM)] * lon_count,
        scratch_shapes=[
            pltpu.VMEM((4 * quarter, rows), jnp.float32),
            pltpu.VMEM((lon_count * width, 4 * rows), jnp.bfloat16),
        ],
        compiler_params=pltpu.CompilerParams(vmem_limit_bytes=16 * MIB),
        cost_estimate=pl.CostEstimate(
            flops=2 * NLON * lon_count * width * rows,
            bytes_accessed=trig.size * 2 + 2 * coeffs.size * 4,
            transcendentals=0,
        ),
        name="grid_field",
    )(lon, trig, coeffs)


def gelu_parts(preact):
    scale = math.sqrt(2.0 / math.pi)
    square = preact * preact
    bend = jnp.tanh(scale * (preact + 0.044715 * (square * preact)))
    half = 0.5 * (1.0 + bend)
    slope = half + (0.5 * preact) * (1.0 - bend * bend) * (
        scale * (1.0 + (3.0 * 0.044715) * square)
    )
    return preact * half, slope


def forward_kernel(latents_ref, w_ref, b_ref, _, slope_ref, hidden_t_ref, latents_t_ref):
    latents = latents_ref[...]
    preact = jnp.dot(latents, w_ref[...], preferred_element_type=jnp.float32) + b_ref[...]
    hidden, slope = gelu_parts(preact)
    slope_ref[...] = slope
    hidden_t_ref[...] = hidden.T.astype(jnp.bfloat16)
    latents_t_ref[...] = latents.T


def forward(latents, w_hidden, b_hidden, after, parts):
    cells, width = latents.shape
    cols = cells // parts
    return pl.pallas_call(
        forward_kernel,
        grid=(parts,),
        out_shape=(
            jax.ShapeDtypeStruct((cells, width), jnp.float32),
            jax.ShapeDtypeStruct((parts, width, cols), jnp.bfloat16),
            jax.ShapeDtypeStruct((parts, width, cols), jnp.bfloat16),
        ),
        in_specs=[
            pl.BlockSpec((cols, width), lambda i: (i, 0)),
            pl.BlockSpec((width, width), lambda i: (0, 0)),
            pl.BlockSpec((1, width), lambda i: (0, 0)),
            pl.BlockSpec(memory_space=pl.ANY),
        ],
        out_specs=(
            pl.BlockSpec((cols, width), lambda i: (i, 0)),
            pl.BlockSpec((None, width, cols), lambda i: (i, 0, 0)),
            pl.BlockSpec((None, width, cols), lambda i: (i, 0, 0)),
        ),
        compiler_params=pltpu.CompilerParams(vmem_limit_bytes=46 * MIB),
        cost_estimate=pl.CostEstimate(
            flops=2 * cells * width * width,
            bytes_accessed=cells * width * 10,
            transcendentals=cells * width,
        ),
        name="forward",
    )(latents, w_hidden, b_hidden.reshape(1, width), after)


def backward_kernel(
    core_ref, scale_ref, place_ref, w_out_ref, slope_ref, hidden_t_ref, latents_t_ref, *refs,
    blocks,
):
    grid_refs = refs[:blocks]
    preact_ref, keep_ref, send_ref = refs[blocks : blocks + 3]
    field_ref, hidden_acc, out_acc, bias_acc, sums_ref = refs[blocks + 3 :]
    index = pl.program_id(0)
    total = pl.num_programs(0)
    lon_cols = grid_refs[0].shape[0]
    width = hidden_acc.shape[0]
    cols = slope_ref.shape[0]
    sum_rows = sums_ref.shape[0]

    @pl.when(index == 0)
    def _():
        field = None
        for block in range(blocks):
            scaled = (grid_refs[block][...] * scale_ref[block]).astype(jnp.bfloat16)
            part = jnp.dot(scaled, place_ref[block], preferred_element_type=jnp.float32)
            field = part if field is None else field + part
        for row in range(field.shape[1] // LANES):
            field_ref[pl.ds(row * lon_cols, lon_cols), :] = field[
                :, row * LANES : (row + 1) * LANES
            ]
        hidden_acc[...] = jnp.zeros_like(hidden_acc)
        out_acc[...] = jnp.zeros_like(out_acc)
        bias_acc[...] = jnp.zeros_like(bias_acc)

    field = field_ref[pl.ds(pl.multiple_of(index * cols, SUBS), cols), :].astype(jnp.bfloat16)
    back = jnp.dot(field, w_out_ref[...], preferred_element_type=jnp.float32)
    preact_back = (back * slope_ref[...]).astype(jnp.bfloat16)
    preact_ref[...] = preact_back
    hidden_acc[...] += jnp.dot(
        latents_t_ref[...], preact_back, preferred_element_type=jnp.float32
    )
    out_acc[...] += jnp.dot(hidden_t_ref[...], field, preferred_element_type=jnp.float32)
    bias_acc[...] += jnp.sum(preact_back.astype(jnp.float32), axis=0, keepdims=True)

    @pl.when(index == total - 1)
    def _():
        tiles = width // LANES
        for row_tile in range(width // SUBS):
            for tile in range(tiles):
                sums_ref[pl.ds((row_tile * tiles + tile) * SUBS, SUBS), :] = hidden_acc[
                    pl.ds(row_tile * SUBS, SUBS), pl.ds(tile * LANES, LANES)
                ]
        base = width * tiles
        flipped = out_acc[...].T
        for tile in range(tiles):
            sums_ref[pl.ds(base + tile * F, F), :] = flipped[:F, tile * LANES : (tile + 1) * LANES]
        base = base + tiles * F
        sums_ref[pl.ds(base, sum_rows - base), :] = jnp.zeros((sum_rows - base, LANES), jnp.float32)
        for tile in range(tiles):
            sums_ref[pl.ds(base + tile, 1), :] = bias_acc[:, tile * LANES : (tile + 1) * LANES]
        half = sum_rows // 2
        mine = core_ref[0]
        keep_ref[...] = sums_ref[pl.ds(pl.multiple_of(mine * half, SUBS), half), :]
        send_ref[...] = sums_ref[pl.ds(pl.multiple_of((1 - mine) * half, SUBS), half), :]


def backward(core, grids, scale, place, w_out_t, slope, hidden_t, latents_t, sum_rows):
    cells, width = slope.shape
    blocks = len(grids)
    parts, _, cols = hidden_t.shape
    half = (sum_rows // 2, LANES)
    whole3 = lambda i: (0, 0, 0)
    whole2 = lambda i: (0, 0)
    return pl.pallas_call(
        functools.partial(backward_kernel, blocks=blocks),
        grid=(parts,),
        out_shape=(
            jax.ShapeDtypeStruct((cells, width), jnp.bfloat16),
            jax.ShapeDtypeStruct(half, jnp.float32),
            jax.ShapeDtypeStruct(half, jnp.float32),
        ),
        in_specs=[
            pl.BlockSpec(memory_space=pltpu.SMEM),
            pl.BlockSpec(scale.shape, whole3),
            pl.BlockSpec(place.shape, whole3),
            pl.BlockSpec(w_out_t.shape, whole2),
            pl.BlockSpec((cols, width), lambda i: (i, 0)),
            pl.BlockSpec((None, width, cols), lambda i: (i, 0, 0)),
            pl.BlockSpec((None, width, cols), lambda i: (i, 0, 0)),
        ]
        + [pl.BlockSpec(grids[0].shape, whole2)] * blocks,
        out_specs=(
            pl.BlockSpec((cols, width), lambda i: (i, 0)),
            pl.BlockSpec(half, whole2),
            pl.BlockSpec(half, whole2),
        ),
        scratch_shapes=[
            pltpu.VMEM((cells, LANES), jnp.float32),
            pltpu.VMEM((width, width), jnp.float32),
            pltpu.VMEM((width, LANES), jnp.float32),
            pltpu.VMEM((1, width), jnp.float32),
            pltpu.VMEM((sum_rows, LANES), jnp.float32),
        ],
        compiler_params=pltpu.CompilerParams(vmem_limit_bytes=32 * MIB),
        cost_estimate=pl.CostEstimate(
            flops=2 * cells * width * (width + 2 * LANES),
            bytes_accessed=cells * width * 10,
            transcendentals=0,
        ),
        name="backward",
    )(core, scale, place, w_out_t, slope, hidden_t, latents_t, *grids)


def add_kernel(index_ref, *refs, inputs, outputs, factor):
    size = refs[0].shape[0] // outputs
    for part in range(outputs):
        start = 0 if outputs == 1 else pl.multiple_of((index_ref[0] ^ part) * size, SUBS)
        total = refs[0][pl.ds(start, size), :]
        for piece in refs[1:inputs]:
            total = total + piece[pl.ds(start, size), :]
        if factor is not None:
            total = total * factor
        refs[inputs + part][...] = total


def add_pieces(index, pieces, outputs, factor=None):
    rows = pieces[0].shape[0]
    size = rows // outputs
    return pl.pallas_call(
        functools.partial(add_kernel, inputs=len(pieces), outputs=outputs, factor=factor),
        out_shape=[jax.ShapeDtypeStruct((size, LANES), jnp.float32)] * outputs,
        in_specs=[pl.BlockSpec(memory_space=pltpu.SMEM)]
        + [pl.BlockSpec(memory_space=pltpu.VMEM)] * len(pieces),
        out_specs=[pl.BlockSpec(memory_space=pltpu.VMEM)] * outputs,
        cost_estimate=pl.CostEstimate(
            flops=len(pieces) * rows * LANES,
            bytes_accessed=4 * (len(pieces) + 1) * rows * LANES,
            transcendentals=0,
        ),
        compiler_params=pltpu.CompilerParams(vmem_limit_bytes=6 * MIB),
        name="add_pieces",
    )(index, *pieces)


def finish_kernel(place_ref, *refs, lon_count, depth):
    hidden_ref, bias_ref, out_ref, flat_ref = refs[2 * lon_count :]
    core, lon, deep = place_ref[0], place_ref[1], place_ref[2]
    size = refs[0].shape[0] // depth
    for half in range(2):
        for part in range(lon_count):
            for piece in range(depth):
                start = (((core ^ half) * lon_count + (lon ^ part)) * depth + (deep ^ piece)) * size
                flat_ref[pl.ds(pl.multiple_of(start, SUBS), size), :] = refs[
                    half * lon_count + part
                ][pl.ds(piece * size, size), :]
    width = hidden_ref.shape[0]
    tiles = width // LANES
    for row_tile in range(width // SUBS):
        for tile in range(tiles):
            hidden_ref[pl.ds(row_tile * SUBS, SUBS), pl.ds(tile * LANES, LANES)] = flat_ref[
                pl.ds((row_tile * tiles + tile) * SUBS, SUBS), :
            ]
    base = width * tiles
    for tile in range(tiles):
        out_ref[:, pl.ds(tile * LANES, LANES)] = flat_ref[pl.ds(base + tile * F, F), :]
        bias_ref[:, pl.ds(tile * LANES, LANES)] = flat_ref[pl.ds(base + tiles * F + tile, 1), :]


def finish(place, pieces, width, depth):
    lon_count = len(pieces) // 2
    return pl.pallas_call(
        functools.partial(finish_kernel, lon_count=lon_count, depth=depth),
        out_shape=(
            jax.ShapeDtypeStruct((width, width), jnp.float32),
            jax.ShapeDtypeStruct((1, width), jnp.float32),
            jax.ShapeDtypeStruct((F, width), jnp.float32),
        ),
        in_specs=[pl.BlockSpec(memory_space=pltpu.SMEM)]
        + [pl.BlockSpec(memory_space=pltpu.VMEM)] * len(pieces),
        out_specs=(pl.BlockSpec(memory_space=pltpu.VMEM),) * 3,
        scratch_shapes=[pltpu.VMEM((len(pieces) * pieces[0].shape[0], LANES), jnp.float32)],
        compiler_params=pltpu.CompilerParams(vmem_limit_bytes=8 * MIB),
        name="finish",
    )(place, *pieces)


def swap(value, axis, bits):
    count = lax.axis_size(axis)
    return lax.ppermute(value, axis, [(i, i ^ bits) for i in range(count)])


def local(spectra, field_slot, field_weight, latents, w_hidden, b_hidden, w_out):
    slot_count, _, pair_count, _ = spectra.shape
    lat_rows, lon_cols, width = latents.shape
    lat_count = lax.axis_size("lat")
    lon_count = lax.axis_size("lon")
    rows_all = lat_rows * lat_count
    lat_index = lax.axis_index("lat").astype(jnp.int32)
    lon_index = lax.axis_index("lon").astype(jnp.int32)
    pair_pad = pad_to(pair_count, SUBS)
    cells = lat_rows * lon_cols
    parts = 4

    coeffs = coefficients(spectra, (lon_index * pair_count).reshape(1), rows_all, lat_rows)
    share = slot_count * lat_rows // lon_count
    coeffs = coeffs.reshape(lat_count * lon_count, share, 4 * pair_pad)
    coeffs = lax.all_to_all(coeffs, ("lat", "lon"), split_axis=0, concat_axis=0, tiled=True)

    trig = trig_table(pair_count, lon_count)

    lanes = lat_count * share

    def spread(values):
        values = jnp.broadcast_to(values, (lat_count, slot_count, lat_rows))
        values = values.reshape(lat_count, lon_count, share)
        values = jnp.transpose(values, (1, 0, 2)).reshape(lon_count, lanes)
        arrival = lon_index ^ jnp.arange(lon_count, dtype=jnp.int32)
        chosen = arrival[:, None] == jnp.arange(lon_count, dtype=jnp.int32)
        return jnp.sum(jnp.where(chosen[:, :, None], values[None], 0), axis=1)

    field_ids = spread(field_slot.reshape(lat_count, slot_count, 1))
    row_ids = spread(jnp.arange(lat_rows, dtype=jnp.int32).reshape(1, 1, lat_rows))
    chosen = field_ids[:, :, None] == jnp.arange(F, dtype=jnp.int32)
    weight = jnp.sum(jnp.where(chosen, field_weight, 0.0), axis=2)
    sine = jnp.sin(band_angles(lat_index * lat_rows + row_ids, rows_all))
    scale = (sine * weight)[:, None, :]
    target = row_ids * LANES + field_ids
    place = (
        target[:, :, None] == jnp.arange(lat_rows * LANES, dtype=jnp.int32)[None, None, :]
    ).astype(jnp.bfloat16)
    w_out_t = jnp.concatenate([w_out.T, jnp.zeros((LANES - F, width), w_out.dtype)], axis=0)

    core_index, deep_index = lat_index & 1, lat_index >> 1
    depth = lat_count // 2
    spots = jnp.stack([core_index, lon_index, deep_index])
    grids = grid_field(lon_index.reshape(1), trig, coeffs, pair_count)
    slope, hidden_t, latents_t = forward(
        latents.reshape(cells, width), w_hidden, b_hidden, grids[0], parts
    )
    grids = [grids[0]] + [swap(grids[part], "lon", part) for part in range(1, lon_count)]

    device_count = lat_count * lon_count
    used_rows = (width + F + 1) * width // LANES
    chunk = pad_to(pad_to(used_rows, device_count) // device_count, SUBS)
    preact_back, keep, send = backward(
        core_index.reshape(1), grids, scale, place, w_out_t, slope, hidden_t, latents_t,
        chunk * device_count,
    )
    latent_grad = lax.dot_general(
        preact_back, w_hidden, (((1,), (1,)), ((), ())), preferred_element_type=jnp.float32
    ).astype(jnp.bfloat16)

    pieces = add_pieces(
        lon_index.reshape(1), [keep, swap(send, "lat", 1)], lon_count
    )
    arrived = [swap(pieces[part], "lon", part) for part in range(1, lon_count)]
    arrived, latent_grad = lax.optimization_barrier((arrived, latent_grad))
    pieces = add_pieces(deep_index.reshape(1), [pieces[0]] + arrived, depth)
    arrived = [swap(pieces[part], "lat", 2 * part) for part in range(1, depth)]
    norm = 1.0 / math.sqrt(rows_all * NLON)
    total = add_pieces(deep_index.reshape(1), [pieces[0]] + arrived, 1, norm)[0]
    total = jnp.concatenate([total] + [swap(total, "lat", 2 * part) for part in range(1, depth)])
    totals = [total] + [swap(total, "lon", part) for part in range(1, lon_count)]
    totals = totals + [swap(piece, "lat", 1) for piece in totals]
    hidden_grad, bias_grad, out_grad = finish(spots, totals, width, depth)
    return (
        latent_grad.reshape(lat_rows, lon_cols, width),
        hidden_grad,
        bias_grad.reshape(width),
        out_grad.T,
    )


def solution(mesh):
    in_specs = (P("lat", None, "lon", None), P(), P(), P("lat", "lon", None), P(), P(), P())
    out_specs = (P("lat", "lon", None), P(), P(), P())
    return jax.shard_map(local, mesh=mesh, in_specs=in_specs, out_specs=out_specs, check_vma=False)
```

```python
import functools
import math

import jax
import jax.numpy as jnp
from jax import lax
from jax.experimental import pallas as pl
from jax.experimental.pallas import tpu as pltpu
from jax.sharding import PartitionSpec as P

NM = 720
NLON = 1440
F = 64
LANES = 128
SUBS = 8
STEPS = NM + 1
PAIRS = 4
MIB = 1024 * 1024
VMEM_LIMIT = 56 * MIB


def band_angles(row_ids, rows_all):
    return jnp.pi * (NM // 2 - rows_all // 2 + row_ids.astype(jnp.float32)) / NM


def pad_to(value, multiple):
    return (value + multiple - 1) // multiple * multiple


def coeff_kernel(
    first_ref, spectra_hbm, out_ref, spectra_ref, grow_ref, factor_ref, scale_ref, table_ref,
    stage_ref, copy_sem, *, pair_count, rows_all, lat_rows, slot_count,
):
    per_block = LANES // rows_all
    vregs = pad_to(pair_count, SUBS * per_block) // (SUBS * per_block)
    step_tile = rows_all
    stride = vregs * SUBS + 1
    pair_pad = pad_to(pair_count, SUBS)
    lat_count = rows_all // lat_rows
    first_pair = first_ref[0]

    fetch = pltpu.make_async_copy(spectra_hbm, spectra_ref, copy_sem)
    fetch.start()

    lane = lax.broadcasted_iota(jnp.int32, (SUBS, LANES), 1)
    sub = lax.broadcasted_iota(jnp.int32, (SUBS, LANES), 0)
    inner = lane & (rows_all - 1)
    which = lane // rows_all
    colatitude = band_angles(inner, rows_all)
    cosine = jnp.cos(colatitude)
    log_sine = jnp.log(jnp.sin(colatitude))

    def log_total(order_column):
        total = jnp.zeros((SUBS, LANES), jnp.float32)
        for tile in range(pad_to(NM, LANES) // LANES):
            term = (lane + tile * LANES).astype(jnp.float32)
            safe = jnp.maximum(term, 1.0)
            value = jnp.log((2.0 * safe + 1.0) / (2.0 * safe))
            total = total + jnp.where((term >= 1.0) & (term <= order_column), value, 0.0)
        return jnp.sum(total, axis=1, keepdims=True)

    def seed(order_of):
        total = jnp.zeros((SUBS, LANES), jnp.float32)
        for part in range(per_block):
            column = order_of(part).astype(jnp.float32)
            total = jnp.where(which == part, log_total(column), total)
        order = order_of(which).astype(jnp.float32)
        return jnp.exp(0.5 * total - 0.5 * math.log(4.0 * math.pi) + order * log_sine)

    pairs = vregs * SUBS * per_block
    steps_pad = pad_to(STEPS, LANES)
    step = lax.broadcasted_iota(jnp.int32, (pairs, steps_pad), 1)
    pair = first_pair + lax.broadcasted_iota(jnp.int32, (pairs, steps_pad), 0)
    switch = NM - pair
    in_first = step < switch
    order = jnp.where(in_first, pair, NM - 1 - pair).astype(jnp.float32)
    degree = jnp.where(in_first, pair + step, step - 1).astype(jnp.float32)
    grow = jnp.sqrt(
        jnp.maximum(4.0 * degree * degree - 1.0, 1.0)
        / jnp.maximum(degree * degree - order * order, 1.0)
    )
    since = jnp.where(in_first, step, step - switch)
    scale = jnp.where(since >= 2, grow / pltpu.roll(grow, 1, 1), 1.0)
    shift = 2
    while shift < STEPS:
        scale = jnp.where(since >= shift, scale * pltpu.roll(scale, shift, 1), scale)
        shift = 2 * shift
    factor = grow * pltpu.roll(scale, 1, 1) / scale
    for tile in range(steps_pad // LANES):
        factor_ref[tile] = factor[:, tile * LANES : (tile + 1) * LANES]
        for row in range(0, pairs, SUBS):
            piece = scale[row : row + SUBS, tile * LANES : (tile + 1) * LANES]
            for part in range(2):
                scale_ref[tile, pl.ds(2 * row + part, SUBS, stride=2), :] = piece

    firsts, seconds, switches = [], [], []
    for v in range(vregs):
        base = first_pair + (sub + v * SUBS) * per_block

        def order_first(part, base=base):
            return base + part

        def order_second(part, base=base):
            return NM - 1 - (base + part)

        firsts.append(seed(order_first))
        seconds.append(seed(order_second))
        switches.append(NM - (base + which))
        rows = pl.ds(v * SUBS, SUBS)
        for tile in range(steps_pad // LANES):
            if per_block == 1:
                grow_ref[tile, rows, :] = factor_ref[tile, rows, :]
            else:
                even = factor_ref[tile, pl.ds(2 * v * SUBS, SUBS, stride=2), :]
                odd = factor_ref[tile, pl.ds(2 * v * SUBS + 1, SUBS, stride=2), :]
                low = lane < rows_all
                grow_ref[2 * tile, rows, :] = jnp.where(low, even, pltpu.roll(odd, rows_all, 1))
                grow_ref[2 * tile + 1, rows, :] = jnp.where(
                    low, pltpu.roll(even, rows_all, 1), odd
                )

    def advance(tile, offset, state, grows, plain):
        previous, before = state
        index = which * rows_all + offset
        step = tile * step_tile + offset
        produced, kept = [], []
        for v in range(vregs):
            grow = jnp.take_along_axis(grows[v], index, axis=1)
            value = (grow * cosine) * previous[v] - before[v]
            older = previous[v]
            if not plain:
                restart = switches[v] == step
                value = jnp.where(restart, seconds[v], value)
                older = jnp.where(restart, 0.0, older)
            table_ref[pl.ds(step * stride + v * SUBS, SUBS), :] = value
            produced.append(value)
            kept.append(older)
        return (tuple(produced), tuple(kept))

    def run_tile(tile, state, count, unroll, plain=False):
        grows = [grow_ref[tile, pl.ds(v * SUBS, SUBS), :] for v in range(vregs)]

        def body(offset, carry):
            return advance(tile, offset, carry, grows, plain)

        return lax.fori_loop(0, count, body, state, unroll=unroll)

    zeros = tuple(jnp.zeros((SUBS, LANES), jnp.float32) for _ in range(vregs))
    state = (zeros, tuple(-value for value in firsts))
    whole_tiles = STEPS // step_tile
    plain_tiles = (NM // 2 + 1) // step_tile
    state = lax.fori_loop(
        0, plain_tiles, lambda tile, carry: run_tile(tile, carry, step_tile, 16, True), state
    )
    state = lax.fori_loop(
        plain_tiles, whole_tiles, lambda tile, carry: run_tile(tile, carry, step_tile, 16), state
    )
    if STEPS % step_tile:
        run_tile(whole_tiles, state, STEPS % step_tile, STEPS % step_tile % 16)

    for row in range(slot_count):
        for half in range(2):
            stage_ref[row, pl.ds((half + 1) * 2 * pair_pad - 2 * SUBS, 2 * SUBS), :] = jnp.zeros(
                (2 * SUBS, LANES), jnp.float32
            )
    fetch.wait()

    rows_half = slot_count * SUBS
    edges = (0, 256, 512, STEPS)
    dot = functools.partial(jnp.dot, preferred_element_type=jnp.float32)

    def split_parts(values):
        high = values.astype(jnp.bfloat16)
        low = (values - high.astype(jnp.float32)).astype(jnp.bfloat16)
        return high, low

    def product(left, right):
        left_high, left_low = split_parts(left)
        right_high, right_low = split_parts(right)
        rows = left.shape[0]
        both = dot(jnp.concatenate([left_high, left_low], axis=0), right_high)
        return both[:rows] + both[rows:] + dot(left_high, right_low)

    def group(start, kinds):
        values = spectra_ref[:, pl.ds(start, PAIRS), :, :].reshape(slot_count, SUBS, STEPS)
        scale = jnp.concatenate(
            [scale_ref[tile, pl.ds(2 * start, SUBS), :] for tile in range(scale_ref.shape[0])],
            axis=1,
        )
        values = values * scale[:, :STEPS]
        row_pair = lax.broadcasted_iota(jnp.int32, (1, SUBS, STEPS), 1) >> 1
        step = lax.broadcasted_iota(jnp.int32, (1, SUBS, STEPS), 2)
        in_first = step < NM - (first_pair + start + row_pair)
        first_block = start // per_block
        blocks = PAIRS // per_block
        table = jnp.concatenate(
            [table_ref[pl.ds(first_block + n, STEPS, stride=stride), :] for n in range(blocks)],
            axis=1,
        )
        sums = [None, None]
        for begin, end, kind in zip(edges[:-1], edges[1:], ("low",) + kinds):
            piece = values[:, :, begin:end]
            if kind == "both":
                first = in_first[:, :, begin:end]
                piece = jnp.concatenate(
                    [jnp.where(first, piece, 0.0), jnp.where(first, 0.0, piece)], axis=0
                )
            part = product(piece.reshape(-1, end - begin), table[begin:end])
            if kind == "both":
                halves = ((0, part[:rows_half]), (1, part[rows_half:]))
            else:
                halves = ((0 if kind == "low" else 1, part),)
            for half, value in halves:
                sums[half] = value if sums[half] is None else sums[half] + value
        both = jnp.concatenate(sums, axis=0).reshape(2 * slot_count, SUBS, blocks * LANES)
        row_id = lax.broadcasted_iota(jnp.int32, (1, SUBS, LANES), 1) >> 1
        lane_part = lax.broadcasted_iota(jnp.int32, (1, SUBS, LANES), 2)
        lane_part = jnp.where(lane_part < rows_all, 0, 1)
        total = None
        for block in range(blocks):
            part = both[:, :, block * LANES : (block + 1) * LANES]
            keep = row_id == block * per_block + lane_part
            total = jnp.where(keep, part, 0.0 if total is None else total)
        total = total.reshape(2 * rows_half, LANES)
        if per_block == 2:
            total = total + pltpu.roll(total, rows_all, 1)
        total = total.astype(jnp.bfloat16).astype(jnp.float32)
        for half in range(2):
            for row in range(slot_count):
                source = (half * slot_count + row) * SUBS
                stage_ref[row, pl.ds(half * 2 * pair_pad + 2 * start, SUBS), :] = total[
                    source : source + SUBS
                ]

    def twice(kinds):
        def body(index, carry):
            group(index * 2 * PAIRS, kinds)
            group(index * 2 * PAIRS + PAIRS, kinds)
            return carry

        return body

    turns = pair_count // (2 * PAIRS)
    border = NM - edges[2]
    low_turns = jnp.clip((border + 1 - first_pair) // (2 * PAIRS), 0, turns)
    high_turn = jnp.clip((border - first_pair + 2 * PAIRS - 1) // (2 * PAIRS), low_turns, turns)
    lax.fori_loop(0, low_turns, twice(("low", "both")), 0)
    lax.fori_loop(low_turns, high_turn, twice(("both", "both")), 0)
    lax.fori_loop(high_turn, turns, twice(("both", "high")), 0)
    start = turns * 2 * PAIRS
    while start < pair_count:
        group(min(start, pair_count - PAIRS), ("both", "both"))
        start = start + PAIRS

    for row in range(slot_count):
        flipped = stage_ref[row].T
        out_ref[:, pl.ds(row * lat_rows, lat_rows), :] = flipped[:rows_all].reshape(
            lat_count, lat_rows, 4 * pair_pad
        )


def coefficients(spectra, first_pair, rows_all, lat_rows):
    slot_count, _, pair_count, steps = spectra.shape
    per_block = LANES // rows_all
    vregs = pad_to(pair_count, SUBS * per_block) // (SUBS * per_block)
    pairs = vregs * SUBS * per_block
    tile_total = pad_to(STEPS, LANES) // rows_all
    pair_pad = pad_to(pair_count, SUBS)
    lat_count = rows_all // lat_rows
    kernel = functools.partial(
        coeff_kernel, pair_count=pair_count, rows_all=rows_all, lat_rows=lat_rows,
        slot_count=slot_count,
    )
    return pl.pallas_call(
        kernel,
        out_shape=jax.ShapeDtypeStruct(
            (lat_count, slot_count * lat_rows, 4 * pair_pad), jnp.float32
        ),
        in_specs=[
            pl.BlockSpec(memory_space=pltpu.SMEM),
            pl.BlockSpec(memory_space=pl.ANY),
        ],
        out_specs=pl.BlockSpec(memory_space=pltpu.VMEM),
        scratch_shapes=[
            pltpu.VMEM((slot_count, pair_count, 2, steps), jnp.float32),
            pltpu.VMEM((tile_total, vregs * SUBS, LANES), jnp.float32),
            pltpu.VMEM((pad_to(STEPS, LANES) // LANES, pairs, LANES), jnp.float32),
            pltpu.VMEM((pad_to(STEPS, LANES) // LANES, 2 * pairs, LANES), jnp.float32),
            pltpu.VMEM((pad_to(STEPS, SUBS) * (vregs * SUBS + 1), LANES), jnp.float32),
            pltpu.VMEM((slot_count, 4 * pair_pad, LANES), jnp.float32),
            pltpu.SemaphoreType.DMA,
        ],
        compiler_params=pltpu.CompilerParams(vmem_limit_bytes=VMEM_LIMIT),
        name="coefficients",
    )(first_pair, jnp.transpose(spectra, (0, 2, 1, 3)))


def trig_kernel(out_ref, *, pair_count, pair_pad, quarter, fine_total):
    block = pl.program_id(0)
    width = 4 * pair_pad
    coarse_total = pad_to(quarter // fine_total, SUBS)

    def orders(rows):
        lane = lax.broadcasted_iota(jnp.int32, (rows, width), 1)
        upper = lane >= 2 * pair_pad
        pair = jnp.where(upper, lane - 2 * pair_pad, lane)
        is_sine = (pair & 1) == 1
        pair = block * pair_count + (pair >> 1)
        return jnp.where(upper, NM - 1 - pair, pair), is_sine

    def angles(rows, spacing):
        order, _ = orders(rows)
        column = lax.broadcasted_iota(jnp.int32, (rows, width), 0) * spacing
        phase = (order * column % NLON).astype(jnp.float32) * (2.0 * math.pi / NLON)
        return jnp.cos(phase), jnp.sin(phase)

    fine_cos, fine_sin = angles(fine_total, 1)
    coarse_cos, coarse_sin = angles(coarse_total, fine_total)
    _, is_sine = orders(fine_total)
    for tile in range(quarter // fine_total):
        left, right = coarse_cos[tile : tile + 1], coarse_sin[tile : tile + 1]
        cosine = left * fine_cos - right * fine_sin
        sine = right * fine_cos + left * fine_sin
        out_ref[pl.ds(tile * fine_total, fine_total), :] = jnp.where(
            is_sine, sine, cosine
        ).astype(jnp.bfloat16)


def trig_table(pair_count, lon_count):
    pair_pad = pad_to(pair_count, SUBS)
    quarter = NLON // 4
    fine_total = 40
    return pl.pallas_call(
        functools.partial(
            trig_kernel, pair_count=pair_count, pair_pad=pair_pad, quarter=quarter,
            fine_total=fine_total,
        ),
        grid=(lon_count,),
        out_shape=jax.ShapeDtypeStruct((lon_count, quarter, 4 * pair_pad), jnp.bfloat16),
        out_specs=pl.BlockSpec((None, quarter, 4 * pair_pad), lambda b: (b, 0, 0)),
        compiler_params=pltpu.CompilerParams(vmem_limit_bytes=12 * MIB),
        cost_estimate=pl.CostEstimate(
            flops=24 * lon_count * quarter * pair_pad,
            bytes_accessed=lon_count * quarter * 8 * pair_pad,
            transcendentals=0,
        ),
        name="trig_table",
    )()


def grid_kernel(lon_ref, trig_ref, coeff_ref, *refs, lon_count, pair_count):
    flat_ref, right_ref = refs[lon_count:]
    share = coeff_ref.shape[1]
    width = coeff_ref.shape[2]
    rows = coeff_ref.shape[0] // lon_count * share
    values = coeff_ref[...].reshape(rows // share, lon_count, share, width)
    line = lax.broadcasted_iota(jnp.int32, (width, rows), 0)
    upper = line >= width // 2
    pair = jnp.where(upper, line - width // 2, line)
    is_sine = (pair & 1) == 1
    for block in range(lon_count):
        flat = values[:, block].reshape(rows, width).T
        swapped = jnp.where(is_sine, -pltpu.roll(flat, 1, 0), pltpu.roll(flat, width - 1, 0))
        order = block * pair_count + (pair >> 1)
        order = jnp.where(upper, NM - 1 - order, order) & 3
        odd = (order & 1) == 1
        flip = jnp.where(odd, -flat, flat)
        turned = jnp.where(order == 1, swapped, jnp.where(order == 3, -swapped, flat))
        turned = jnp.where(order == 2, -flat, turned)
        back = jnp.where(odd, -turned, turned)
        for turn, part in enumerate((flat, turned, flip, back)):
            right_ref[pl.ds(block * width, width), pl.ds(turn * rows, rows)] = part.astype(
                jnp.bfloat16
            )
    total = None
    for block in range(lon_count):
        part = jnp.dot(
            trig_ref[block],
            right_ref[pl.ds(block * width, width), :],
            preferred_element_type=jnp.float32,
        )
        total = part if total is None else total + part
    quarter = total.shape[0]
    for turn in range(4):
        flat_ref[pl.ds(turn * quarter, quarter), :] = total[:, turn * rows : (turn + 1) * rows]
    cols = NLON // lon_count
    for part in range(lon_count):
        refs[part][...] = flat_ref[pl.ds((lon_ref[0] ^ part) * cols, cols), :]


def grid_field(lon, trig, coeffs, pair_count):
    lon_count, quarter, width = trig.shape
    rows = coeffs.shape[0] // lon_count * coeffs.shape[1]
    return pl.pallas_call(
        functools.partial(grid_kernel, lon_count=lon_count, pair_count=pair_count),
        out_shape=[jax.ShapeDtypeStruct((NLON // lon_count, rows), jnp.float32)] * lon_count,
        in_specs=[pl.BlockSpec(memory_space=pltpu.SMEM)]
        + [pl.BlockSpec(memory_space=pltpu.VMEM)] * 2,
        out_specs=[pl.BlockSpec(memory_space=pltpu.VMEM)] * lon_count,
        scratch_shapes=[
            pltpu.VMEM((4 * quarter, rows), jnp.float32),
            pltpu.VMEM((lon_count * width, 4 * rows), jnp.bfloat16),
        ],
        compiler_params=pltpu.CompilerParams(vmem_limit_bytes=16 * MIB),
        cost_estimate=pl.CostEstimate(
            flops=2 * NLON * lon_count * width * rows,
            bytes_accessed=trig.size * 2 + 2 * coeffs.size * 4,
            transcendentals=0,
        ),
        name="grid_field",
    )(lon, trig, coeffs)


def gelu_parts(preact):
    scale = math.sqrt(2.0 / math.pi)
    square = preact * preact
    bend = jnp.tanh(scale * (preact + 0.044715 * (square * preact)))
    half = 0.5 * (1.0 + bend)
    slope = half + (0.5 * preact) * (1.0 - bend * bend) * (
        scale * (1.0 + (3.0 * 0.044715) * square)
    )
    return preact * half, slope


def forward_kernel(latents_ref, w_ref, b_ref, _, slope_ref, hidden_t_ref, latents_t_ref):
    latents = latents_ref[...]
    preact = jnp.dot(latents, w_ref[...], preferred_element_type=jnp.float32) + b_ref[...]
    hidden, slope = gelu_parts(preact)
    slope_ref[...] = slope
    hidden_t_ref[...] = hidden.astype(jnp.bfloat16).T
    latents_t_ref[...] = latents.T


def forward(latents, w_hidden, b_hidden, after, parts):
    cells, width = latents.shape
    cols = cells // parts
    return pl.pallas_call(
        forward_kernel,
        grid=(parts,),
        out_shape=(
            jax.ShapeDtypeStruct((cells, width), jnp.float32),
            jax.ShapeDtypeStruct((parts, width, cols), jnp.bfloat16),
            jax.ShapeDtypeStruct((parts, width, cols), jnp.bfloat16),
        ),
        in_specs=[
            pl.BlockSpec((cols, width), lambda i: (i, 0)),
            pl.BlockSpec((width, width), lambda i: (0, 0)),
            pl.BlockSpec((1, width), lambda i: (0, 0)),
            pl.BlockSpec(memory_space=pl.ANY),
        ],
        out_specs=(
            pl.BlockSpec((cols, width), lambda i: (i, 0)),
            pl.BlockSpec((None, width, cols), lambda i: (i, 0, 0)),
            pl.BlockSpec((None, width, cols), lambda i: (i, 0, 0)),
        ),
        compiler_params=pltpu.CompilerParams(vmem_limit_bytes=32 * MIB),
        cost_estimate=pl.CostEstimate(
            flops=2 * cells * width * width,
            bytes_accessed=cells * width * 10,
            transcendentals=cells * width,
        ),
        name="forward",
    )(latents, w_hidden, b_hidden.reshape(1, width), after)


def backward_kernel(
    core_ref, scale_ref, place_ref, w_out_ref, slope_ref, hidden_t_ref, latents_t_ref, *refs,
    blocks,
):
    grid_refs = refs[:blocks]
    preact_ref, keep_ref, send_ref = refs[blocks : blocks + 3]
    field_ref, hidden_acc, out_acc, bias_acc, sums_ref = refs[blocks + 3 :]
    index = pl.program_id(0)
    total = pl.num_programs(0)
    lon_cols = grid_refs[0].shape[0]
    width = hidden_acc.shape[0]
    cols = slope_ref.shape[0]
    sum_rows = sums_ref.shape[0]

    @pl.when(index == 0)
    def _():
        field = None
        for block in range(blocks):
            scaled = (grid_refs[block][...] * scale_ref[block]).astype(jnp.bfloat16)
            part = jnp.dot(scaled, place_ref[block], preferred_element_type=jnp.float32)
            field = part if field is None else field + part
        for row in range(field.shape[1] // LANES):
            field_ref[pl.ds(row * lon_cols, lon_cols), :] = field[
                :, row * LANES : (row + 1) * LANES
            ]
        hidden_acc[...] = jnp.zeros_like(hidden_acc)
        out_acc[...] = jnp.zeros_like(out_acc)
        bias_acc[...] = jnp.zeros_like(bias_acc)

    field = field_ref[pl.ds(pl.multiple_of(index * cols, SUBS), cols), :].astype(jnp.bfloat16)
    back = jnp.dot(field[:, :F], w_out_ref[...], preferred_element_type=jnp.float32)
    preact_back = (back * slope_ref[...]).astype(jnp.bfloat16)
    preact_ref[...] = preact_back
    hidden_acc[...] += jnp.dot(
        latents_t_ref[...], preact_back, preferred_element_type=jnp.float32
    )
    out_acc[...] += jnp.dot(hidden_t_ref[...], field, preferred_element_type=jnp.float32)
    bias_acc[...] += jnp.sum(preact_back.astype(jnp.float32), axis=0, keepdims=True)

    @pl.when(index == total - 1)
    def _():
        tiles = width // LANES
        for row_tile in range(width // SUBS):
            for tile in range(tiles):
                sums_ref[pl.ds((row_tile * tiles + tile) * SUBS, SUBS), :] = hidden_acc[
                    pl.ds(row_tile * SUBS, SUBS), pl.ds(tile * LANES, LANES)
                ]
        base = width * tiles
        flipped = out_acc[...].T
        for tile in range(tiles):
            sums_ref[pl.ds(base + tile * F, F), :] = flipped[:F, tile * LANES : (tile + 1) * LANES]
        base = base + tiles * F
        sums_ref[pl.ds(base, sum_rows - base), :] = jnp.zeros((sum_rows - base, LANES), jnp.float32)
        for tile in range(tiles):
            sums_ref[pl.ds(base + tile, 1), :] = bias_acc[:, tile * LANES : (tile + 1) * LANES]
        half = sum_rows // 2
        mine = core_ref[0]
        keep_ref[...] = sums_ref[pl.ds(pl.multiple_of(mine * half, SUBS), half), :]
        send_ref[...] = sums_ref[pl.ds(pl.multiple_of((1 - mine) * half, SUBS), half), :]


def backward(core, grids, scale, place, w_out_t, slope, hidden_t, latents_t, sum_rows):
    cells, width = slope.shape
    blocks = len(grids)
    parts, _, cols = hidden_t.shape
    half = (sum_rows // 2, LANES)
    whole3 = lambda i: (0, 0, 0)
    whole2 = lambda i: (0, 0)
    return pl.pallas_call(
        functools.partial(backward_kernel, blocks=blocks),
        grid=(parts,),
        out_shape=(
            jax.ShapeDtypeStruct((cells, width), jnp.bfloat16),
            jax.ShapeDtypeStruct(half, jnp.float32),
            jax.ShapeDtypeStruct(half, jnp.float32),
        ),
        in_specs=[
            pl.BlockSpec(memory_space=pltpu.SMEM),
            pl.BlockSpec(scale.shape, whole3),
            pl.BlockSpec(place.shape, whole3),
            pl.BlockSpec(w_out_t.shape, whole2),
            pl.BlockSpec((cols, width), lambda i: (i, 0)),
            pl.BlockSpec((None, width, cols), lambda i: (i, 0, 0)),
            pl.BlockSpec((None, width, cols), lambda i: (i, 0, 0)),
        ]
        + [pl.BlockSpec(grids[0].shape, whole2)] * blocks,
        out_specs=(
            pl.BlockSpec((cols, width), lambda i: (i, 0)),
            pl.BlockSpec(half, whole2),
            pl.BlockSpec(half, whole2),
        ),
        scratch_shapes=[
            pltpu.VMEM((cells, LANES), jnp.float32),
            pltpu.VMEM((width, width), jnp.float32),
            pltpu.VMEM((width, LANES), jnp.float32),
            pltpu.VMEM((1, width), jnp.float32),
            pltpu.VMEM((sum_rows, LANES), jnp.float32),
        ],
        compiler_params=pltpu.CompilerParams(vmem_limit_bytes=32 * MIB),
        cost_estimate=pl.CostEstimate(
            flops=2 * cells * width * (width + 2 * LANES),
            bytes_accessed=cells * width * 10,
            transcendentals=0,
        ),
        name="backward",
    )(core, scale, place, w_out_t, slope, hidden_t, latents_t, *grids)


def latent_kernel(preact_hbm, w_ref, _, out_ref, preact_ref, copy_sem, *, parts):
    fetch = pltpu.make_async_copy(preact_hbm, preact_ref, copy_sem)
    fetch.start()
    fetch.wait()
    cols = preact_ref.shape[0] // parts
    for part in range(parts):
        rows = pl.ds(part * cols, cols)
        out_ref[rows, :] = lax.dot_general(
            preact_ref[rows, :],
            w_ref[...],
            (((1,), (1,)), ((), ())),
            preferred_element_type=jnp.float32,
        ).astype(jnp.bfloat16)


def latent_gradient(preact_back, w_hidden, after, parts):
    cells, width = preact_back.shape
    return pl.pallas_call(
        functools.partial(latent_kernel, parts=parts),
        out_shape=jax.ShapeDtypeStruct((cells, width), jnp.bfloat16),
        in_specs=[
            pl.BlockSpec(memory_space=pltpu.HBM),
            pl.BlockSpec(memory_space=pltpu.VMEM),
            pl.BlockSpec(memory_space=pl.ANY),
        ],
        out_specs=pl.BlockSpec(memory_space=pltpu.VMEM),
        scratch_shapes=[pltpu.VMEM((cells, width), jnp.bfloat16), pltpu.SemaphoreType.DMA],
        compiler_params=pltpu.CompilerParams(vmem_limit_bytes=16 * MIB),
        cost_estimate=pl.CostEstimate(
            flops=2 * cells * width * width, bytes_accessed=4 * cells * width, transcendentals=0
        ),
        name="latent_gradient",
    )(preact_back, w_hidden, after)


def add_kernel(index_ref, *refs, inputs, outputs, factor):
    size = refs[0].shape[0] // outputs
    for part in range(outputs):
        start = 0 if outputs == 1 else pl.multiple_of((index_ref[0] ^ part) * size, SUBS)
        total = refs[0][pl.ds(start, size), :]
        for piece in refs[1:inputs]:
            total = total + piece[pl.ds(start, size), :]
        if factor is not None:
            total = total * factor
        refs[inputs + part][...] = total


def add_pieces(index, pieces, outputs, factor=None):
    rows = pieces[0].shape[0]
    size = rows // outputs
    return pl.pallas_call(
        functools.partial(add_kernel, inputs=len(pieces), outputs=outputs, factor=factor),
        out_shape=[jax.ShapeDtypeStruct((size, LANES), jnp.float32)] * outputs,
        in_specs=[pl.BlockSpec(memory_space=pltpu.SMEM)]
        + [pl.BlockSpec(memory_space=pltpu.VMEM)] * len(pieces),
        out_specs=[pl.BlockSpec(memory_space=pltpu.VMEM)] * outputs,
        cost_estimate=pl.CostEstimate(
            flops=len(pieces) * rows * LANES,
            bytes_accessed=4 * (len(pieces) + 1) * rows * LANES,
            transcendentals=0,
        ),
        compiler_params=pltpu.CompilerParams(vmem_limit_bytes=6 * MIB),
        name="add_pieces",
    )(index, *pieces)


def finish_kernel(place_ref, *refs, lon_count, depth):
    hidden_ref, bias_ref, out_ref, flat_ref = refs[2 * lon_count :]
    core, lon, deep = place_ref[0], place_ref[1], place_ref[2]
    size = refs[0].shape[0] // depth
    for half in range(2):
        for part in range(lon_count):
            for piece in range(depth):
                start = (((core ^ half) * lon_count + (lon ^ part)) * depth + (deep ^ piece)) * size
                flat_ref[pl.ds(pl.multiple_of(start, SUBS), size), :] = refs[
                    half * lon_count + part
                ][pl.ds(piece * size, size), :]
    width = hidden_ref.shape[0]
    tiles = width // LANES
    for row_tile in range(width // SUBS):
        for tile in range(tiles):
            hidden_ref[pl.ds(row_tile * SUBS, SUBS), pl.ds(tile * LANES, LANES)] = flat_ref[
                pl.ds((row_tile * tiles + tile) * SUBS, SUBS), :
            ]
    base = width * tiles
    for tile in range(tiles):
        out_ref[:, pl.ds(tile * LANES, LANES)] = flat_ref[pl.ds(base + tile * F, F), :]
        bias_ref[:, pl.ds(tile * LANES, LANES)] = flat_ref[pl.ds(base + tiles * F + tile, 1), :]


def finish(place, pieces, width, depth):
    lon_count = len(pieces) // 2
    return pl.pallas_call(
        functools.partial(finish_kernel, lon_count=lon_count, depth=depth),
        out_shape=(
            jax.ShapeDtypeStruct((width, width), jnp.float32),
            jax.ShapeDtypeStruct((1, width), jnp.float32),
            jax.ShapeDtypeStruct((F, width), jnp.float32),
        ),
        in_specs=[pl.BlockSpec(memory_space=pltpu.SMEM)]
        + [pl.BlockSpec(memory_space=pltpu.VMEM)] * len(pieces),
        out_specs=(pl.BlockSpec(memory_space=pltpu.VMEM),) * 3,
        scratch_shapes=[pltpu.VMEM((len(pieces) * pieces[0].shape[0], LANES), jnp.float32)],
        compiler_params=pltpu.CompilerParams(vmem_limit_bytes=8 * MIB),
        name="finish",
    )(place, *pieces)


def swap(value, axis, bits):
    count = lax.axis_size(axis)
    return lax.ppermute(value, axis, [(i, i ^ bits) for i in range(count)])


def local(spectra, field_slot, field_weight, latents, w_hidden, b_hidden, w_out):
    slot_count, _, pair_count, _ = spectra.shape
    lat_rows, lon_cols, width = latents.shape
    lat_count = lax.axis_size("lat")
    lon_count = lax.axis_size("lon")
    rows_all = lat_rows * lat_count
    lat_index = lax.axis_index("lat").astype(jnp.int32)
    lon_index = lax.axis_index("lon").astype(jnp.int32)
    pair_pad = pad_to(pair_count, SUBS)
    cells = lat_rows * lon_cols
    parts = 4

    coeffs = coefficients(spectra, (lon_index * pair_count).reshape(1), rows_all, lat_rows)
    share = slot_count * lat_rows // lon_count
    coeffs = coeffs.reshape(lat_count * lon_count, share, 4 * pair_pad)
    coeffs = lax.all_to_all(coeffs, ("lat", "lon"), split_axis=0, concat_axis=0, tiled=True)

    trig = trig_table(pair_count, lon_count)

    lanes = lat_count * share

    def spread(values):
        values = jnp.broadcast_to(values, (lat_count, slot_count, lat_rows))
        values = values.reshape(lat_count, lon_count, share)
        values = jnp.transpose(values, (1, 0, 2)).reshape(lon_count, lanes)
        arrival = lon_index ^ jnp.arange(lon_count, dtype=jnp.int32)
        chosen = arrival[:, None] == jnp.arange(lon_count, dtype=jnp.int32)
        return jnp.sum(jnp.where(chosen[:, :, None], values[None], 0), axis=1)

    field_ids = spread(field_slot.reshape(lat_count, slot_count, 1))
    row_ids = spread(jnp.arange(lat_rows, dtype=jnp.int32).reshape(1, 1, lat_rows))
    chosen = field_ids[:, :, None] == jnp.arange(F, dtype=jnp.int32)
    weight = jnp.sum(jnp.where(chosen, field_weight, 0.0), axis=2)
    sine = jnp.sin(band_angles(lat_index * lat_rows + row_ids, rows_all))
    scale = (sine * weight)[:, None, :]
    target = row_ids * LANES + field_ids
    place = (
        target[:, :, None] == jnp.arange(lat_rows * LANES, dtype=jnp.int32)[None, None, :]
    ).astype(jnp.bfloat16)
    w_out_t = w_out.T

    core_index, deep_index = lat_index & 1, lat_index >> 1
    depth = lat_count // 2
    spots = jnp.stack([core_index, lon_index, deep_index])
    grids = grid_field(lon_index.reshape(1), trig, coeffs, pair_count)
    slope, hidden_t, latents_t = forward(
        latents.reshape(cells, width), w_hidden, b_hidden, grids[0], parts
    )
    grids = [grids[0]] + [swap(grids[part], "lon", part) for part in range(1, lon_count)]

    device_count = lat_count * lon_count
    used_rows = (width + F + 1) * width // LANES
    chunk = pad_to(pad_to(used_rows, device_count) // device_count, SUBS)
    preact_back, keep, send = backward(
        core_index.reshape(1), grids, scale, place, w_out_t, slope, hidden_t, latents_t,
        chunk * device_count,
    )
    pieces = add_pieces(
        lon_index.reshape(1), [keep, swap(send, "lat", 1)], lon_count
    )
    arrived = [swap(pieces[part], "lon", part) for part in range(1, lon_count)]
    latent_grad = latent_gradient(preact_back, w_hidden, pieces[0], parts)
    arrived, latent_grad = lax.optimization_barrier((arrived, latent_grad))
    pieces = add_pieces(deep_index.reshape(1), [pieces[0]] + arrived, depth)
    arrived = [swap(pieces[part], "lat", 2 * part) for part in range(1, depth)]
    norm = 1.0 / math.sqrt(rows_all * NLON)
    total = add_pieces(deep_index.reshape(1), [pieces[0]] + arrived, 1, norm)[0]
    total = jnp.concatenate([total] + [swap(total, "lat", 2 * part) for part in range(1, depth)])
    totals = [total] + [swap(total, "lon", part) for part in range(1, lon_count)]
    totals = totals + [swap(piece, "lat", 1) for piece in totals]
    hidden_grad, bias_grad, out_grad = finish(spots, totals, width, depth)
    return (
        latent_grad.reshape(lat_rows, lon_cols, width),
        hidden_grad,
        bias_grad.reshape(width),
        out_grad.T,
    )


def solution(mesh):
    in_specs = (P("lat", None, "lon", None), P(), P(), P("lat", "lon", None), P(), P(), P())
    out_specs = (P("lat", "lon", None), P(), P(), P())
    return jax.shard_map(local, mesh=mesh, in_specs=in_specs, out_specs=out_specs, check_vma=False)
```

```python
import functools
import math

import jax
import jax.numpy as jnp
from jax import lax
from jax.experimental import pallas as pl
from jax.experimental.pallas import tpu as pltpu
from jax.sharding import PartitionSpec as P

NM = 720
NLON = 1440
F = 64
LANES = 128
SUBS = 8
STEPS = NM + 1
PAIRS = 4
MIB = 1024 * 1024
VMEM_LIMIT = 56 * MIB


def band_angles(row_ids, rows_all):
    return jnp.pi * (NM // 2 - rows_all // 2 + row_ids.astype(jnp.float32)) / NM


def pad_to(value, multiple):
    return (value + multiple - 1) // multiple * multiple


def coeff_kernel(
    first_ref, spectra_hbm, out_ref, spectra_ref, grow_ref, factor_ref, scale_ref, table_ref,
    stage_ref, copy_sem, *, pair_count, rows_all, lat_rows, slot_count,
):
    per_block = LANES // rows_all
    vregs = pad_to(pair_count, SUBS * per_block) // (SUBS * per_block)
    step_tile = rows_all
    stride = vregs * SUBS + 1
    pair_pad = pad_to(pair_count, SUBS)
    lat_count = rows_all // lat_rows
    first_pair = first_ref[0]

    fetch = pltpu.make_async_copy(spectra_hbm, spectra_ref, copy_sem)
    fetch.start()

    lane = lax.broadcasted_iota(jnp.int32, (SUBS, LANES), 1)
    sub = lax.broadcasted_iota(jnp.int32, (SUBS, LANES), 0)
    inner = lane & (rows_all - 1)
    which = lane // rows_all
    colatitude = band_angles(inner, rows_all)
    cosine = jnp.cos(colatitude)
    log_sine = jnp.log(jnp.sin(colatitude))

    def log_total(order_column):
        total = jnp.zeros((SUBS, LANES), jnp.float32)
        for tile in range(pad_to(NM, LANES) // LANES):
            term = (lane + tile * LANES).astype(jnp.float32)
            safe = jnp.maximum(term, 1.0)
            value = jnp.log((2.0 * safe + 1.0) / (2.0 * safe))
            total = total + jnp.where((term >= 1.0) & (term <= order_column), value, 0.0)
        return jnp.sum(total, axis=1, keepdims=True)

    def seed(order_of):
        total = jnp.zeros((SUBS, LANES), jnp.float32)
        for part in range(per_block):
            column = order_of(part).astype(jnp.float32)
            total = jnp.where(which == part, log_total(column), total)
        order = order_of(which).astype(jnp.float32)
        return jnp.exp(0.5 * total - 0.5 * math.log(4.0 * math.pi) + order * log_sine)

    pairs = vregs * SUBS * per_block
    steps_pad = pad_to(STEPS, LANES)
    step = lax.broadcasted_iota(jnp.int32, (pairs, steps_pad), 1)
    pair = first_pair + lax.broadcasted_iota(jnp.int32, (pairs, steps_pad), 0)
    switch = NM - pair
    in_first = step < switch
    order = jnp.where(in_first, pair, NM - 1 - pair).astype(jnp.float32)
    degree = jnp.where(in_first, pair + step, step - 1).astype(jnp.float32)
    grow = jnp.sqrt(
        jnp.maximum(4.0 * degree * degree - 1.0, 1.0)
        / jnp.maximum(degree * degree - order * order, 1.0)
    )
    since = jnp.where(in_first, step, step - switch)
    scale = jnp.where(since >= 2, grow / pltpu.roll(grow, 1, 1), 1.0)
    shift = 2
    while shift < STEPS:
        scale = jnp.where(since >= shift, scale * pltpu.roll(scale, shift, 1), scale)
        shift = 2 * shift
    factor = grow * pltpu.roll(scale, 1, 1) / scale
    for tile in range(steps_pad // LANES):
        factor_ref[tile] = factor[:, tile * LANES : (tile + 1) * LANES]
        for row in range(0, pairs, SUBS):
            piece = scale[row : row + SUBS, tile * LANES : (tile + 1) * LANES]
            for part in range(2):
                scale_ref[tile, pl.ds(2 * row + part, SUBS, stride=2), :] = piece

    firsts, seconds, switches = [], [], []
    for v in range(vregs):
        base = first_pair + (sub + v * SUBS) * per_block

        def order_first(part, base=base):
            return base + part

        def order_second(part, base=base):
            return NM - 1 - (base + part)

        firsts.append(seed(order_first))
        seconds.append(seed(order_second))
        switches.append(NM - (base + which))
        rows = pl.ds(v * SUBS, SUBS)
        for tile in range(steps_pad // LANES):
            if per_block == 1:
                grow_ref[tile, rows, :] = factor_ref[tile, rows, :]
            else:
                even = factor_ref[tile, pl.ds(2 * v * SUBS, SUBS, stride=2), :]
                odd = factor_ref[tile, pl.ds(2 * v * SUBS + 1, SUBS, stride=2), :]
                low = lane < rows_all
                grow_ref[2 * tile, rows, :] = jnp.where(low, even, pltpu.roll(odd, rows_all, 1))
                grow_ref[2 * tile + 1, rows, :] = jnp.where(
                    low, pltpu.roll(even, rows_all, 1), odd
                )

    def advance(tile, offset, state, grows, plain):
        previous, before = state
        index = which * rows_all + offset
        step = tile * step_tile + offset
        produced, kept = [], []
        for v in range(vregs):
            grow = jnp.take_along_axis(grows[v], index, axis=1)
            value = (grow * cosine) * previous[v] - before[v]
            older = previous[v]
            if not plain:
                restart = switches[v] == step
                value = jnp.where(restart, seconds[v], value)
                older = jnp.where(restart, 0.0, older)
            table_ref[pl.ds(step * stride + v * SUBS, SUBS), :] = value
            produced.append(value)
            kept.append(older)
        return (tuple(produced), tuple(kept))

    def run_tile(tile, state, count, unroll, plain=False):
        grows = [grow_ref[tile, pl.ds(v * SUBS, SUBS), :] for v in range(vregs)]

        def body(offset, carry):
            return advance(tile, offset, carry, grows, plain)

        return lax.fori_loop(0, count, body, state, unroll=unroll)

    zeros = tuple(jnp.zeros((SUBS, LANES), jnp.float32) for _ in range(vregs))
    state = (zeros, tuple(-value for value in firsts))
    whole_tiles = STEPS // step_tile
    plain_tiles = (NM // 2 + 1) // step_tile
    state = lax.fori_loop(
        0, plain_tiles, lambda tile, carry: run_tile(tile, carry, step_tile, 32, True), state
    )
    state = lax.fori_loop(
        plain_tiles, whole_tiles, lambda tile, carry: run_tile(tile, carry, step_tile, 32), state
    )
    if STEPS % step_tile:
        run_tile(whole_tiles, state, STEPS % step_tile, STEPS % step_tile % 16)

    for row in range(slot_count):
        for half in range(2):
            stage_ref[row, pl.ds((half + 1) * 2 * pair_pad - 2 * SUBS, 2 * SUBS), :] = jnp.zeros(
                (2 * SUBS, LANES), jnp.float32
            )
    fetch.wait()

    rows_half = slot_count * SUBS
    edges = (0, 256, 512, STEPS)
    dot = functools.partial(jnp.dot, preferred_element_type=jnp.float32)

    def split_parts(values):
        high = values.astype(jnp.bfloat16)
        low = (values - high.astype(jnp.float32)).astype(jnp.bfloat16)
        return high, low

    def product(left, right):
        left_high, left_low = split_parts(left)
        right_high, right_low = split_parts(right)
        rows = left.shape[0]
        both = dot(jnp.concatenate([left_high, left_low], axis=0), right_high)
        return both[:rows] + both[rows:] + dot(left_high, right_low)

    def group(start, kinds):
        values = spectra_ref[:, pl.ds(start, PAIRS), :, :].reshape(slot_count, SUBS, STEPS)
        scale = jnp.concatenate(
            [scale_ref[tile, pl.ds(2 * start, SUBS), :] for tile in range(scale_ref.shape[0])],
            axis=1,
        )
        values = values * scale[:, :STEPS]
        row_pair = lax.broadcasted_iota(jnp.int32, (1, SUBS, STEPS), 1) >> 1
        step = lax.broadcasted_iota(jnp.int32, (1, SUBS, STEPS), 2)
        in_first = step < NM - (first_pair + start + row_pair)
        first_block = start // per_block
        blocks = PAIRS // per_block
        table = jnp.concatenate(
            [table_ref[pl.ds(first_block + n, STEPS, stride=stride), :] for n in range(blocks)],
            axis=1,
        )
        sums = [None, None]
        for begin, end, kind in zip(edges[:-1], edges[1:], ("low",) + kinds):
            piece = values[:, :, begin:end]
            if kind == "both":
                first = in_first[:, :, begin:end]
                piece = jnp.concatenate(
                    [jnp.where(first, piece, 0.0), jnp.where(first, 0.0, piece)], axis=0
                )
            part = product(piece.reshape(-1, end - begin), table[begin:end])
            if kind == "both":
                halves = ((0, part[:rows_half]), (1, part[rows_half:]))
            else:
                halves = ((0 if kind == "low" else 1, part),)
            for half, value in halves:
                sums[half] = value if sums[half] is None else sums[half] + value
        both = jnp.concatenate(sums, axis=0).reshape(2 * slot_count, SUBS, blocks * LANES)
        row_id = lax.broadcasted_iota(jnp.int32, (1, SUBS, LANES), 1) >> 1
        lane_part = lax.broadcasted_iota(jnp.int32, (1, SUBS, LANES), 2)
        lane_part = jnp.where(lane_part < rows_all, 0, 1)
        total = None
        for block in range(blocks):
            part = both[:, :, block * LANES : (block + 1) * LANES]
            keep = row_id == block * per_block + lane_part
            total = jnp.where(keep, part, 0.0 if total is None else total)
        total = total.reshape(2 * rows_half, LANES)
        if per_block == 2:
            total = total + pltpu.roll(total, rows_all, 1)
        total = total.astype(jnp.bfloat16).astype(jnp.float32)
        for half in range(2):
            for row in range(slot_count):
                source = (half * slot_count + row) * SUBS
                stage_ref[row, pl.ds(half * 2 * pair_pad + 2 * start, SUBS), :] = total[
                    source : source + SUBS
                ]

    span = 4 * PAIRS

    def several(kinds):
        def body(index, carry):
            for part in range(0, span, PAIRS):
                group(index * span + part, kinds)
            return carry

        return body

    turns = pair_count // span
    border = NM - edges[2]
    low_turns = jnp.clip((border + 1 - first_pair) // span, 0, turns)
    high_turn = jnp.clip((border - first_pair + span - 1) // span, low_turns, turns)
    lax.fori_loop(0, low_turns, several(("low", "both")), 0)
    lax.fori_loop(low_turns, high_turn, several(("both", "both")), 0)
    lax.fori_loop(high_turn, turns, several(("both", "high")), 0)
    start = turns * span
    while start < pair_count:
        group(min(start, pair_count - PAIRS), ("both", "both"))
        start = start + PAIRS

    for row in range(slot_count):
        flipped = stage_ref[row].T
        out_ref[:, pl.ds(row * lat_rows, lat_rows), :] = flipped[:rows_all].reshape(
            lat_count, lat_rows, 4 * pair_pad
        )


def coefficients(spectra, first_pair, rows_all, lat_rows):
    slot_count, _, pair_count, steps = spectra.shape
    per_block = LANES // rows_all
    vregs = pad_to(pair_count, SUBS * per_block) // (SUBS * per_block)
    pairs = vregs * SUBS * per_block
    tile_total = pad_to(STEPS, LANES) // rows_all
    pair_pad = pad_to(pair_count, SUBS)
    lat_count = rows_all // lat_rows
    kernel = functools.partial(
        coeff_kernel, pair_count=pair_count, rows_all=rows_all, lat_rows=lat_rows,
        slot_count=slot_count,
    )
    return pl.pallas_call(
        kernel,
        out_shape=jax.ShapeDtypeStruct(
            (lat_count, slot_count * lat_rows, 4 * pair_pad), jnp.float32
        ),
        in_specs=[
            pl.BlockSpec(memory_space=pltpu.SMEM),
            pl.BlockSpec(memory_space=pl.ANY),
        ],
        out_specs=pl.BlockSpec(memory_space=pltpu.VMEM),
        scratch_shapes=[
            pltpu.VMEM((slot_count, pair_count, 2, steps), jnp.float32),
            pltpu.VMEM((tile_total, vregs * SUBS, LANES), jnp.float32),
            pltpu.VMEM((pad_to(STEPS, LANES) // LANES, pairs, LANES), jnp.float32),
            pltpu.VMEM((pad_to(STEPS, LANES) // LANES, 2 * pairs, LANES), jnp.float32),
            pltpu.VMEM((pad_to(STEPS, SUBS) * (vregs * SUBS + 1), LANES), jnp.float32),
            pltpu.VMEM((slot_count, 4 * pair_pad, LANES), jnp.float32),
            pltpu.SemaphoreType.DMA,
        ],
        compiler_params=pltpu.CompilerParams(vmem_limit_bytes=VMEM_LIMIT),
        name="coefficients",
    )(first_pair, jnp.transpose(spectra, (0, 2, 1, 3)))


def trig_kernel(out_ref, *, pair_count, pair_pad, quarter, fine_total):
    block = pl.program_id(0)
    width = 4 * pair_pad
    coarse_total = pad_to(quarter // fine_total, SUBS)

    def orders(rows):
        lane = lax.broadcasted_iota(jnp.int32, (rows, width), 1)
        upper = lane >= 2 * pair_pad
        pair = jnp.where(upper, lane - 2 * pair_pad, lane)
        is_sine = (pair & 1) == 1
        pair = block * pair_count + (pair >> 1)
        return jnp.where(upper, NM - 1 - pair, pair), is_sine

    def angles(rows, spacing):
        order, _ = orders(rows)
        column = lax.broadcasted_iota(jnp.int32, (rows, width), 0) * spacing
        phase = (order * column % NLON).astype(jnp.float32) * (2.0 * math.pi / NLON)
        return jnp.cos(phase), jnp.sin(phase)

    fine_cos, fine_sin = angles(fine_total, 1)
    coarse_cos, coarse_sin = angles(coarse_total, fine_total)
    _, is_sine = orders(fine_total)
    for tile in range(quarter // fine_total):
        left, right = coarse_cos[tile : tile + 1], coarse_sin[tile : tile + 1]
        cosine = left * fine_cos - right * fine_sin
        sine = right * fine_cos + left * fine_sin
        out_ref[pl.ds(tile * fine_total, fine_total), :] = jnp.where(
            is_sine, sine, cosine
        ).astype(jnp.bfloat16)


def trig_table(pair_count, lon_count):
    pair_pad = pad_to(pair_count, SUBS)
    quarter = NLON // 4
    fine_total = 40
    return pl.pallas_call(
        functools.partial(
            trig_kernel, pair_count=pair_count, pair_pad=pair_pad, quarter=quarter,
            fine_total=fine_total,
        ),
        grid=(lon_count,),
        out_shape=jax.ShapeDtypeStruct((lon_count, quarter, 4 * pair_pad), jnp.bfloat16),
        out_specs=pl.BlockSpec((None, quarter, 4 * pair_pad), lambda b: (b, 0, 0)),
        compiler_params=pltpu.CompilerParams(vmem_limit_bytes=12 * MIB),
        cost_estimate=pl.CostEstimate(
            flops=24 * lon_count * quarter * pair_pad,
            bytes_accessed=lon_count * quarter * 8 * pair_pad,
            transcendentals=0,
        ),
        name="trig_table",
    )()


def grid_kernel(lon_ref, trig_ref, coeff_ref, *refs, lon_count, pair_count):
    token_ref, flat_ref, right_ref = refs[lon_count:]
    token_ref[...] = jnp.zeros_like(token_ref)
    share = coeff_ref.shape[1]
    width = coeff_ref.shape[2]
    rows = coeff_ref.shape[0] // lon_count * share
    values = coeff_ref[...].reshape(rows // share, lon_count, share, width)
    line = lax.broadcasted_iota(jnp.int32, (width, rows), 0)
    upper = line >= width // 2
    pair = jnp.where(upper, line - width // 2, line)
    is_sine = (pair & 1) == 1
    for block in range(lon_count):
        flat = values[:, block].reshape(rows, width).T
        swapped = jnp.where(is_sine, -pltpu.roll(flat, 1, 0), pltpu.roll(flat, width - 1, 0))
        order = block * pair_count + (pair >> 1)
        order = jnp.where(upper, NM - 1 - order, order) & 3
        odd = (order & 1) == 1
        flip = jnp.where(odd, -flat, flat)
        turned = jnp.where(order == 1, swapped, jnp.where(order == 3, -swapped, flat))
        turned = jnp.where(order == 2, -flat, turned)
        back = jnp.where(odd, -turned, turned)
        for turn, part in enumerate((flat, turned, flip, back)):
            right_ref[pl.ds(block * width, width), pl.ds(turn * rows, rows)] = part.astype(
                jnp.bfloat16
            )
    total = None
    for block in range(lon_count):
        part = jnp.dot(
            trig_ref[block],
            right_ref[pl.ds(block * width, width), :],
            preferred_element_type=jnp.float32,
        )
        total = part if total is None else total + part
    quarter = total.shape[0]
    for turn in range(4):
        flat_ref[pl.ds(turn * quarter, quarter), :] = total[:, turn * rows : (turn + 1) * rows]
    cols = NLON // lon_count
    for part in range(lon_count):
        refs[part][...] = flat_ref[pl.ds((lon_ref[0] ^ part) * cols, cols), :]


def grid_field(lon, trig, coeffs, pair_count):
    lon_count, quarter, width = trig.shape
    rows = coeffs.shape[0] // lon_count * coeffs.shape[1]
    return pl.pallas_call(
        functools.partial(grid_kernel, lon_count=lon_count, pair_count=pair_count),
        out_shape=[jax.ShapeDtypeStruct((NLON // lon_count, rows), jnp.float32)] * lon_count
        + [jax.ShapeDtypeStruct((SUBS, LANES), jnp.float32)],
        in_specs=[pl.BlockSpec(memory_space=pltpu.SMEM)]
        + [pl.BlockSpec(memory_space=pltpu.VMEM)] * 2,
        out_specs=[pl.BlockSpec(memory_space=pltpu.VMEM)] * (lon_count + 1),
        scratch_shapes=[
            pltpu.VMEM((4 * quarter, rows), jnp.float32),
            pltpu.VMEM((lon_count * width, 4 * rows), jnp.bfloat16),
        ],
        compiler_params=pltpu.CompilerParams(vmem_limit_bytes=16 * MIB),
        cost_estimate=pl.CostEstimate(
            flops=2 * NLON * lon_count * width * rows,
            bytes_accessed=trig.size * 2 + 2 * coeffs.size * 4,
            transcendentals=0,
        ),
        name="grid_field",
    )(lon, trig, coeffs)


def gelu_parts(preact):
    scale = math.sqrt(2.0 / math.pi)
    square = preact * preact
    bend = jnp.tanh(scale * (preact + 0.044715 * (square * preact)))
    half = 0.5 * (1.0 + bend)
    slope = half + (0.5 * preact) * (1.0 - bend * bend) * (
        scale * (1.0 + (3.0 * 0.044715) * square)
    )
    return preact * half, slope


def forward_kernel(latents_ref, w_ref, b_ref, _, slope_ref, hidden_t_ref, latents_t_ref):
    latents = latents_ref[...]
    preact = jnp.dot(latents, w_ref[...], preferred_element_type=jnp.float32) + b_ref[...]
    hidden, slope = gelu_parts(preact)
    slope_ref[...] = slope
    hidden_t_ref[...] = hidden.astype(jnp.bfloat16).T
    latents_t_ref[...] = latents.T


def forward(latents, w_hidden, b_hidden, after, parts):
    cells, width = latents.shape
    cols = cells // parts
    return pl.pallas_call(
        forward_kernel,
        grid=(parts,),
        out_shape=(
            jax.ShapeDtypeStruct((cells, width), jnp.float32),
            jax.ShapeDtypeStruct((parts, width, cols), jnp.bfloat16),
            jax.ShapeDtypeStruct((parts, width, cols), jnp.bfloat16),
        ),
        in_specs=[
            pl.BlockSpec((cols, width), lambda i: (i, 0)),
            pl.BlockSpec((width, width), lambda i: (0, 0)),
            pl.BlockSpec((1, width), lambda i: (0, 0)),
            pl.BlockSpec((SUBS, LANES), lambda i: (0, 0)),
        ],
        out_specs=(
            pl.BlockSpec((cols, width), lambda i: (i, 0)),
            pl.BlockSpec((None, width, cols), lambda i: (i, 0, 0)),
            pl.BlockSpec((None, width, cols), lambda i: (i, 0, 0)),
        ),
        compiler_params=pltpu.CompilerParams(vmem_limit_bytes=32 * MIB),
        cost_estimate=pl.CostEstimate(
            flops=2 * cells * width * width,
            bytes_accessed=cells * width * 10,
            transcendentals=cells * width,
        ),
        name="forward",
    )(latents, w_hidden, b_hidden.reshape(1, width), after)


def backward_kernel(
    core_ref, scale_ref, place_ref, w_out_ref, slope_ref, hidden_t_ref, latents_t_ref, *refs,
    blocks,
):
    grid_refs = refs[:blocks]
    preact_ref, keep_ref, send_ref = refs[blocks : blocks + 3]
    field_ref, hidden_acc, out_acc, bias_acc, sums_ref = refs[blocks + 3 :]
    index = pl.program_id(0)
    total = pl.num_programs(0)
    lon_cols = grid_refs[0].shape[0]
    width = hidden_acc.shape[0]
    cols = slope_ref.shape[0]
    sum_rows = sums_ref.shape[0]

    @pl.when(index == 0)
    def _():
        field = None
        for block in range(blocks):
            scaled = (grid_refs[block][...] * scale_ref[block]).astype(jnp.bfloat16)
            part = jnp.dot(scaled, place_ref[block], preferred_element_type=jnp.float32)
            field = part if field is None else field + part
        for row in range(field.shape[1] // LANES):
            field_ref[pl.ds(row * lon_cols, lon_cols), :] = field[
                :, row * LANES : (row + 1) * LANES
            ]
        hidden_acc[...] = jnp.zeros_like(hidden_acc)
        out_acc[...] = jnp.zeros_like(out_acc)
        bias_acc[...] = jnp.zeros_like(bias_acc)

    field = field_ref[pl.ds(pl.multiple_of(index * cols, SUBS), cols), :].astype(jnp.bfloat16)
    back = jnp.dot(field[:, :F], w_out_ref[...], preferred_element_type=jnp.float32)
    preact_back = (back * slope_ref[...]).astype(jnp.bfloat16)
    preact_ref[...] = preact_back
    hidden_acc[...] += jnp.dot(
        latents_t_ref[...], preact_back, preferred_element_type=jnp.float32
    )
    out_acc[...] += jnp.dot(hidden_t_ref[...], field, preferred_element_type=jnp.float32)
    bias_acc[...] += jnp.sum(preact_back.astype(jnp.float32), axis=0, keepdims=True)

    @pl.when(index == total - 1)
    def _():
        tiles = width // LANES
        for row_tile in range(width // SUBS):
            for tile in range(tiles):
                sums_ref[pl.ds((row_tile * tiles + tile) * SUBS, SUBS), :] = hidden_acc[
                    pl.ds(row_tile * SUBS, SUBS), pl.ds(tile * LANES, LANES)
                ]
        base = width * tiles
        flipped = out_acc[...].T
        for tile in range(tiles):
            sums_ref[pl.ds(base + tile * F, F), :] = flipped[:F, tile * LANES : (tile + 1) * LANES]
        base = base + tiles * F
        sums_ref[pl.ds(base, sum_rows - base), :] = jnp.zeros((sum_rows - base, LANES), jnp.float32)
        for tile in range(tiles):
            sums_ref[pl.ds(base + tile, 1), :] = bias_acc[:, tile * LANES : (tile + 1) * LANES]
        half = sum_rows // 2
        mine = core_ref[0]
        keep_ref[...] = sums_ref[pl.ds(pl.multiple_of(mine * half, SUBS), half), :]
        send_ref[...] = sums_ref[pl.ds(pl.multiple_of((1 - mine) * half, SUBS), half), :]


def backward(core, grids, scale, place, w_out_t, slope, hidden_t, latents_t, sum_rows):
    cells, width = slope.shape
    blocks = len(grids)
    parts, _, cols = hidden_t.shape
    half = (sum_rows // 2, LANES)
    whole3 = lambda i: (0, 0, 0)
    whole2 = lambda i: (0, 0)
    return pl.pallas_call(
        functools.partial(backward_kernel, blocks=blocks),
        grid=(parts,),
        out_shape=(
            jax.ShapeDtypeStruct((cells, width), jnp.bfloat16),
            jax.ShapeDtypeStruct(half, jnp.float32),
            jax.ShapeDtypeStruct(half, jnp.float32),
        ),
        in_specs=[
            pl.BlockSpec(memory_space=pltpu.SMEM),
            pl.BlockSpec(scale.shape, whole3),
            pl.BlockSpec(place.shape, whole3),
            pl.BlockSpec(w_out_t.shape, whole2),
            pl.BlockSpec((cols, width), lambda i: (i, 0)),
            pl.BlockSpec((None, width, cols), lambda i: (i, 0, 0)),
            pl.BlockSpec((None, width, cols), lambda i: (i, 0, 0)),
        ]
        + [pl.BlockSpec(grids[0].shape, whole2)] * blocks,
        out_specs=(
            pl.BlockSpec((cols, width), lambda i: (i, 0)),
            pl.BlockSpec(half, whole2),
            pl.BlockSpec(half, whole2),
        ),
        scratch_shapes=[
            pltpu.VMEM((cells, LANES), jnp.float32),
            pltpu.VMEM((width, width), jnp.float32),
            pltpu.VMEM((width, LANES), jnp.float32),
            pltpu.VMEM((1, width), jnp.float32),
            pltpu.VMEM((sum_rows, LANES), jnp.float32),
        ],
        compiler_params=pltpu.CompilerParams(vmem_limit_bytes=32 * MIB),
        cost_estimate=pl.CostEstimate(
            flops=2 * cells * width * (width + 2 * LANES),
            bytes_accessed=cells * width * 10,
            transcendentals=0,
        ),
        name="backward",
    )(core, scale, place, w_out_t, slope, hidden_t, latents_t, *grids)


def add_kernel(index_ref, *refs, inputs, outputs, factor):
    size = refs[0].shape[0] // outputs
    for part in range(outputs):
        start = 0 if outputs == 1 else pl.multiple_of((index_ref[0] ^ part) * size, SUBS)
        total = refs[0][pl.ds(start, size), :]
        for piece in refs[1:inputs]:
            total = total + piece[pl.ds(start, size), :]
        if factor is not None:
            total = total * factor
        refs[inputs + part][...] = total


def add_pieces(index, pieces, outputs, factor=None):
    rows = pieces[0].shape[0]
    size = rows // outputs
    return pl.pallas_call(
        functools.partial(add_kernel, inputs=len(pieces), outputs=outputs, factor=factor),
        out_shape=[jax.ShapeDtypeStruct((size, LANES), jnp.float32)] * outputs,
        in_specs=[pl.BlockSpec(memory_space=pltpu.SMEM)]
        + [pl.BlockSpec(memory_space=pltpu.VMEM)] * len(pieces),
        out_specs=[pl.BlockSpec(memory_space=pltpu.VMEM)] * outputs,
        cost_estimate=pl.CostEstimate(
            flops=len(pieces) * rows * LANES,
            bytes_accessed=4 * (len(pieces) + 1) * rows * LANES,
            transcendentals=0,
        ),
        compiler_params=pltpu.CompilerParams(vmem_limit_bytes=6 * MIB),
        name="add_pieces",
    )(index, *pieces)


def finish_kernel(place_ref, *refs, lon_count, depth):
    hidden_ref, bias_ref, out_ref, flat_ref = refs[2 * lon_count :]
    core, lon, deep = place_ref[0], place_ref[1], place_ref[2]
    size = refs[0].shape[0] // depth
    for half in range(2):
        for part in range(lon_count):
            for piece in range(depth):
                start = (((core ^ half) * lon_count + (lon ^ part)) * depth + (deep ^ piece)) * size
                flat_ref[pl.ds(pl.multiple_of(start, SUBS), size), :] = refs[
                    half * lon_count + part
                ][pl.ds(piece * size, size), :]
    width = hidden_ref.shape[0]
    tiles = width // LANES
    for row_tile in range(width // SUBS):
        for tile in range(tiles):
            hidden_ref[pl.ds(row_tile * SUBS, SUBS), pl.ds(tile * LANES, LANES)] = flat_ref[
                pl.ds((row_tile * tiles + tile) * SUBS, SUBS), :
            ]
    base = width * tiles
    for tile in range(tiles):
        out_ref[:, pl.ds(tile * LANES, LANES)] = flat_ref[pl.ds(base + tile * F, F), :]
        bias_ref[:, pl.ds(tile * LANES, LANES)] = flat_ref[pl.ds(base + tiles * F + tile, 1), :]


def finish(place, pieces, width, depth):
    lon_count = len(pieces) // 2
    return pl.pallas_call(
        functools.partial(finish_kernel, lon_count=lon_count, depth=depth),
        out_shape=(
            jax.ShapeDtypeStruct((width, width), jnp.float32),
            jax.ShapeDtypeStruct((1, width), jnp.float32),
            jax.ShapeDtypeStruct((F, width), jnp.float32),
        ),
        in_specs=[pl.BlockSpec(memory_space=pltpu.SMEM)]
        + [pl.BlockSpec(memory_space=pltpu.VMEM)] * len(pieces),
        out_specs=(pl.BlockSpec(memory_space=pltpu.VMEM),) * 3,
        scratch_shapes=[pltpu.VMEM((len(pieces) * pieces[0].shape[0], LANES), jnp.float32)],
        compiler_params=pltpu.CompilerParams(vmem_limit_bytes=8 * MIB),
        name="finish",
    )(place, *pieces)


def swap(value, axis, bits):
    count = lax.axis_size(axis)
    return lax.ppermute(value, axis, [(i, i ^ bits) for i in range(count)])


def local(spectra, field_slot, field_weight, latents, w_hidden, b_hidden, w_out):
    slot_count, _, pair_count, _ = spectra.shape
    lat_rows, lon_cols, width = latents.shape
    lat_count = lax.axis_size("lat")
    lon_count = lax.axis_size("lon")
    rows_all = lat_rows * lat_count
    lat_index = lax.axis_index("lat").astype(jnp.int32)
    lon_index = lax.axis_index("lon").astype(jnp.int32)
    pair_pad = pad_to(pair_count, SUBS)
    cells = lat_rows * lon_cols
    parts = 4

    coeffs = coefficients(spectra, (lon_index * pair_count).reshape(1), rows_all, lat_rows)
    share = slot_count * lat_rows // lon_count
    coeffs = coeffs.reshape(lat_count * lon_count, share, 4 * pair_pad)
    coeffs = lax.all_to_all(coeffs, ("lat", "lon"), split_axis=0, concat_axis=0, tiled=True)

    trig = trig_table(pair_count, lon_count)

    lanes = lat_count * share

    def spread(values):
        values = jnp.broadcast_to(values, (lat_count, slot_count, lat_rows))
        values = values.reshape(lat_count, lon_count, share)
        values = jnp.transpose(values, (1, 0, 2)).reshape(lon_count, lanes)
        arrival = lon_index ^ jnp.arange(lon_count, dtype=jnp.int32)
        chosen = arrival[:, None] == jnp.arange(lon_count, dtype=jnp.int32)
        return jnp.sum(jnp.where(chosen[:, :, None], values[None], 0), axis=1)

    field_ids = spread(field_slot.reshape(lat_count, slot_count, 1))
    row_ids = spread(jnp.arange(lat_rows, dtype=jnp.int32).reshape(1, 1, lat_rows))
    chosen = field_ids[:, :, None] == jnp.arange(F, dtype=jnp.int32)
    weight = jnp.sum(jnp.where(chosen, field_weight, 0.0), axis=2)
    sine = jnp.sin(band_angles(lat_index * lat_rows + row_ids, rows_all))
    scale = (sine * weight)[:, None, :]
    target = row_ids * LANES + field_ids
    place = (
        target[:, :, None] == jnp.arange(lat_rows * LANES, dtype=jnp.int32)[None, None, :]
    ).astype(jnp.bfloat16)
    w_out_t = w_out.T

    core_index, deep_index = lat_index & 1, lat_index >> 1
    depth = lat_count // 2
    spots = jnp.stack([core_index, lon_index, deep_index])
    *grids, token = grid_field(lon_index.reshape(1), trig, coeffs, pair_count)
    slope, hidden_t, latents_t = forward(
        latents.reshape(cells, width), w_hidden, b_hidden, token, parts
    )
    grids = [grids[0]] + [swap(grids[part], "lon", part) for part in range(1, lon_count)]

    device_count = lat_count * lon_count
    used_rows = (width + F + 1) * width // LANES
    chunk = pad_to(pad_to(used_rows, device_count) // device_count, SUBS)
    preact_back, keep, send = backward(
        core_index.reshape(1), grids, scale, place, w_out_t, slope, hidden_t, latents_t,
        chunk * device_count,
    )
    pieces = add_pieces(
        lon_index.reshape(1), [keep, swap(send, "lat", 1)], lon_count
    )
    arrived = [swap(pieces[part], "lon", part) for part in range(1, lon_count)]
    latent_grad = lax.dot_general(
        preact_back, w_hidden, (((1,), (1,)), ((), ())), preferred_element_type=jnp.float32
    ).astype(jnp.bfloat16)
    arrived, latent_grad = lax.optimization_barrier((arrived, latent_grad))
    pieces = add_pieces(deep_index.reshape(1), [pieces[0]] + arrived, depth)
    arrived = [swap(pieces[part], "lat", 2 * part) for part in range(1, depth)]
    norm = 1.0 / math.sqrt(rows_all * NLON)
    total = add_pieces(deep_index.reshape(1), [pieces[0]] + arrived, 1, norm)[0]
    total = jnp.concatenate([total] + [swap(total, "lat", 2 * part) for part in range(1, depth)])
    totals = [total] + [swap(total, "lon", part) for part in range(1, lon_count)]
    totals = totals + [swap(piece, "lat", 1) for piece in totals]
    hidden_grad, bias_grad, out_grad = finish(spots, totals, width, depth)
    return (
        latent_grad.reshape(lat_rows, lon_cols, width),
        hidden_grad,
        bias_grad.reshape(width),
        out_grad.T,
    )


def solution(mesh):
    in_specs = (P("lat", None, "lon", None), P(), P(), P("lat", "lon", None), P(), P(), P())
    out_specs = (P("lat", "lon", None), P(), P(), P())
    return jax.shard_map(local, mesh=mesh, in_specs=in_specs, out_specs=out_specs, check_vma=False)
```

```python
import functools
import math

import jax
import jax.numpy as jnp
from jax import lax
from jax.experimental import pallas as pl
from jax.experimental.pallas import tpu as pltpu
from jax.sharding import PartitionSpec as P

NM = 720
NLON = 1440
F = 64
LANES = 128
SUBS = 8
STEPS = NM + 1
PAIRS = 4
MIB = 1024 * 1024
VMEM_LIMIT = 56 * MIB


def band_angles(row_ids, rows_all):
    return jnp.pi * (NM // 2 - rows_all // 2 + row_ids.astype(jnp.float32)) / NM


def pad_to(value, multiple):
    return (value + multiple - 1) // multiple * multiple


def coeff_kernel(
    first_ref, spectra_hbm, out_ref, spectra_ref, grow_ref, factor_ref, scale_ref, table_ref,
    stage_ref, copy_sem, *, pair_count, rows_all, lat_rows, slot_count,
):
    per_block = LANES // rows_all
    vregs = pad_to(pair_count, SUBS * per_block) // (SUBS * per_block)
    step_tile = rows_all
    stride = vregs * SUBS + 1
    pair_pad = pad_to(pair_count, SUBS)
    lat_count = rows_all // lat_rows
    first_pair = first_ref[0]

    fetch = pltpu.make_async_copy(spectra_hbm, spectra_ref, copy_sem)
    fetch.start()

    lane = lax.broadcasted_iota(jnp.int32, (SUBS, LANES), 1)
    sub = lax.broadcasted_iota(jnp.int32, (SUBS, LANES), 0)
    inner = lane & (rows_all - 1)
    which = lane // rows_all
    colatitude = band_angles(inner, rows_all)
    cosine = jnp.cos(colatitude)
    log_sine = jnp.log(jnp.sin(colatitude))

    def log_total(order_column):
        total = jnp.zeros((SUBS, LANES), jnp.float32)
        for tile in range(pad_to(NM, LANES) // LANES):
            term = (lane + tile * LANES).astype(jnp.float32)
            safe = jnp.maximum(term, 1.0)
            value = jnp.log((2.0 * safe + 1.0) / (2.0 * safe))
            total = total + jnp.where((term >= 1.0) & (term <= order_column), value, 0.0)
        return jnp.sum(total, axis=1, keepdims=True)

    def seed(order_of):
        total = jnp.zeros((SUBS, LANES), jnp.float32)
        for part in range(per_block):
            column = order_of(part).astype(jnp.float32)
            total = jnp.where(which == part, log_total(column), total)
        order = order_of(which).astype(jnp.float32)
        return jnp.exp(0.5 * total - 0.5 * math.log(4.0 * math.pi) + order * log_sine)

    pairs = vregs * SUBS * per_block
    steps_pad = pad_to(STEPS, LANES)
    step = lax.broadcasted_iota(jnp.int32, (pairs, steps_pad), 1)
    pair = first_pair + lax.broadcasted_iota(jnp.int32, (pairs, steps_pad), 0)
    switch = NM - pair
    in_first = step < switch
    order = jnp.where(in_first, pair, NM - 1 - pair).astype(jnp.float32)
    degree = jnp.where(in_first, pair + step, step - 1).astype(jnp.float32)
    grow = jnp.sqrt(
        jnp.maximum(4.0 * degree * degree - 1.0, 1.0)
        / jnp.maximum(degree * degree - order * order, 1.0)
    )
    since = jnp.where(in_first, step, step - switch)
    scale = jnp.where(since >= 2, grow / pltpu.roll(grow, 1, 1), 1.0)
    shift = 2
    while shift < STEPS:
        scale = jnp.where(since >= shift, scale * pltpu.roll(scale, shift, 1), scale)
        shift = 2 * shift
    factor = grow * pltpu.roll(scale, 1, 1) / scale
    for tile in range(steps_pad // LANES):
        factor_ref[tile] = factor[:, tile * LANES : (tile + 1) * LANES]
        for row in range(0, pairs, SUBS):
            piece = scale[row : row + SUBS, tile * LANES : (tile + 1) * LANES]
            for part in range(2):
                scale_ref[tile, pl.ds(2 * row + part, SUBS, stride=2), :] = piece

    firsts, seconds, switches = [], [], []
    for v in range(vregs):
        base = first_pair + (sub + v * SUBS) * per_block

        def order_first(part, base=base):
            return base + part

        def order_second(part, base=base):
            return NM - 1 - (base + part)

        firsts.append(seed(order_first))
        seconds.append(seed(order_second))
        switches.append(NM - (base + which))
        rows = pl.ds(v * SUBS, SUBS)
        for tile in range(steps_pad // LANES):
            if per_block == 1:
                grow_ref[tile, rows, :] = factor_ref[tile, rows, :]
            else:
                even = factor_ref[tile, pl.ds(2 * v * SUBS, SUBS, stride=2), :]
                odd = factor_ref[tile, pl.ds(2 * v * SUBS + 1, SUBS, stride=2), :]
                low = lane < rows_all
                grow_ref[2 * tile, rows, :] = jnp.where(low, even, pltpu.roll(odd, rows_all, 1))
                grow_ref[2 * tile + 1, rows, :] = jnp.where(
                    low, pltpu.roll(even, rows_all, 1), odd
                )

    def advance(tile, offset, state, grows, plain):
        previous, before = state
        index = which * rows_all + offset
        step = tile * step_tile + offset
        produced, kept = [], []
        for v in range(vregs):
            grow = jnp.take_along_axis(grows[v], index, axis=1)
            value = (grow * cosine) * previous[v] - before[v]
            older = previous[v]
            if not plain:
                restart = switches[v] == step
                value = jnp.where(restart, seconds[v], value)
                older = jnp.where(restart, 0.0, older)
            table_ref[pl.ds(step * stride + v * SUBS, SUBS), :] = value
            produced.append(value)
            kept.append(older)
        return (tuple(produced), tuple(kept))

    def run_tile(tile, state, count, unroll, plain=False):
        grows = [grow_ref[tile, pl.ds(v * SUBS, SUBS), :] for v in range(vregs)]

        def body(offset, carry):
            return advance(tile, offset, carry, grows, plain)

        return lax.fori_loop(0, count, body, state, unroll=unroll)

    zeros = tuple(jnp.zeros((SUBS, LANES), jnp.float32) for _ in range(vregs))
    state = (zeros, tuple(-value for value in firsts))
    whole_tiles = STEPS // step_tile
    plain_tiles = (NM // 2 + 1) // step_tile
    state = lax.fori_loop(
        0, plain_tiles, lambda tile, carry: run_tile(tile, carry, step_tile, 64, True), state
    )
    state = lax.fori_loop(
        plain_tiles, whole_tiles, lambda tile, carry: run_tile(tile, carry, step_tile, 64), state
    )
    if STEPS % step_tile:
        run_tile(whole_tiles, state, STEPS % step_tile, STEPS % step_tile % 16)

    for row in range(slot_count):
        for half in range(2):
            stage_ref[row, pl.ds((half + 1) * 2 * pair_pad - 2 * SUBS, 2 * SUBS), :] = jnp.zeros(
                (2 * SUBS, LANES), jnp.float32
            )
    fetch.wait()

    rows_half = slot_count * SUBS
    edges = (0, 256, 512, STEPS)
    dot = functools.partial(jnp.dot, preferred_element_type=jnp.float32)

    def split_parts(values):
        high = values.astype(jnp.bfloat16)
        low = (values - high.astype(jnp.float32)).astype(jnp.bfloat16)
        return high, low

    def product(left, right):
        left_high, left_low = split_parts(left)
        right_high, right_low = split_parts(right)
        rows = left.shape[0]
        both = dot(jnp.concatenate([left_high, left_low], axis=0), right_high)
        return both[:rows] + both[rows:] + dot(left_high, right_low)

    def group(start, kinds):
        values = spectra_ref[:, pl.ds(start, PAIRS), :, :].reshape(slot_count, SUBS, STEPS)
        scale = jnp.concatenate(
            [scale_ref[tile, pl.ds(2 * start, SUBS), :] for tile in range(scale_ref.shape[0])],
            axis=1,
        )
        values = values * scale[:, :STEPS]
        row_pair = lax.broadcasted_iota(jnp.int32, (1, SUBS, STEPS), 1) >> 1
        step = lax.broadcasted_iota(jnp.int32, (1, SUBS, STEPS), 2)
        in_first = step < NM - (first_pair + start + row_pair)
        first_block = start // per_block
        blocks = PAIRS // per_block
        table = jnp.concatenate(
            [table_ref[pl.ds(first_block + n, STEPS, stride=stride), :] for n in range(blocks)],
            axis=1,
        )
        sums = [None, None]
        for begin, end, kind in zip(edges[:-1], edges[1:], ("low",) + kinds):
            piece = values[:, :, begin:end]
            if kind == "both":
                first = in_first[:, :, begin:end]
                piece = jnp.concatenate(
                    [jnp.where(first, piece, 0.0), jnp.where(first, 0.0, piece)], axis=0
                )
            part = product(piece.reshape(-1, end - begin), table[begin:end])
            if kind == "both":
                halves = ((0, part[:rows_half]), (1, part[rows_half:]))
            else:
                halves = ((0 if kind == "low" else 1, part),)
            for half, value in halves:
                sums[half] = value if sums[half] is None else sums[half] + value
        both = jnp.concatenate(sums, axis=0).reshape(2 * slot_count, SUBS, blocks * LANES)
        row_id = lax.broadcasted_iota(jnp.int32, (1, SUBS, LANES), 1) >> 1
        lane_part = lax.broadcasted_iota(jnp.int32, (1, SUBS, LANES), 2)
        lane_part = jnp.where(lane_part < rows_all, 0, 1)
        total = None
        for block in range(blocks):
            part = both[:, :, block * LANES : (block + 1) * LANES]
            keep = row_id == block * per_block + lane_part
            total = jnp.where(keep, part, 0.0 if total is None else total)
        total = total.reshape(2 * rows_half, LANES)
        if per_block == 2:
            total = total + pltpu.roll(total, rows_all, 1)
        total = total.astype(jnp.bfloat16).astype(jnp.float32)
        for half in range(2):
            for row in range(slot_count):
                source = (half * slot_count + row) * SUBS
                stage_ref[row, pl.ds(half * 2 * pair_pad + 2 * start, SUBS), :] = total[
                    source : source + SUBS
                ]

    span = 7 * PAIRS

    def several(kinds):
        def body(index, carry):
            for part in range(0, span, PAIRS):
                group(index * span + part, kinds)
            return carry

        return body

    turns = pair_count // span
    border = NM - edges[2]
    low_turns = jnp.clip((border + 1 - first_pair) // span, 0, turns)
    high_turn = jnp.clip((border - first_pair + span - 1) // span, low_turns, turns)
    lax.fori_loop(0, low_turns, several(("low", "both")), 0)
    lax.fori_loop(low_turns, high_turn, several(("both", "both")), 0)
    lax.fori_loop(high_turn, turns, several(("both", "high")), 0)
    start = turns * span
    while start < pair_count:
        group(min(start, pair_count - PAIRS), ("both", "both"))
        start = start + PAIRS

    for row in range(slot_count):
        flipped = stage_ref[row].T
        out_ref[:, pl.ds(row * lat_rows, lat_rows), :] = flipped[:rows_all].reshape(
            lat_count, lat_rows, 4 * pair_pad
        )


def coefficients(spectra, first_pair, rows_all, lat_rows):
    slot_count, _, pair_count, steps = spectra.shape
    per_block = LANES // rows_all
    vregs = pad_to(pair_count, SUBS * per_block) // (SUBS * per_block)
    pairs = vregs * SUBS * per_block
    tile_total = pad_to(STEPS, LANES) // rows_all
    pair_pad = pad_to(pair_count, SUBS)
    lat_count = rows_all // lat_rows
    kernel = functools.partial(
        coeff_kernel, pair_count=pair_count, rows_all=rows_all, lat_rows=lat_rows,
        slot_count=slot_count,
    )
    return pl.pallas_call(
        kernel,
        out_shape=jax.ShapeDtypeStruct(
            (lat_count, slot_count * lat_rows, 4 * pair_pad), jnp.float32
        ),
        in_specs=[
            pl.BlockSpec(memory_space=pltpu.SMEM),
            pl.BlockSpec(memory_space=pl.ANY),
        ],
        out_specs=pl.BlockSpec(memory_space=pltpu.VMEM),
        scratch_shapes=[
            pltpu.VMEM((slot_count, pair_count, 2, steps), jnp.float32),
            pltpu.VMEM((tile_total, vregs * SUBS, LANES), jnp.float32),
            pltpu.VMEM((pad_to(STEPS, LANES) // LANES, pairs, LANES), jnp.float32),
            pltpu.VMEM((pad_to(STEPS, LANES) // LANES, 2 * pairs, LANES), jnp.float32),
            pltpu.VMEM((pad_to(STEPS, SUBS) * (vregs * SUBS + 1), LANES), jnp.float32),
            pltpu.VMEM((slot_count, 4 * pair_pad, LANES), jnp.float32),
            pltpu.SemaphoreType.DMA,
        ],
        compiler_params=pltpu.CompilerParams(vmem_limit_bytes=VMEM_LIMIT),
        name="coefficients",
    )(first_pair, jnp.transpose(spectra, (0, 2, 1, 3)))


def trig_kernel(out_ref, *, pair_count, pair_pad, quarter, fine_total):
    block = pl.program_id(0)
    width = 4 * pair_pad
    coarse_total = pad_to(quarter // fine_total, SUBS)

    def orders(rows):
        lane = lax.broadcasted_iota(jnp.int32, (rows, width), 1)
        upper = lane >= 2 * pair_pad
        pair = jnp.where(upper, lane - 2 * pair_pad, lane)
        is_sine = (pair & 1) == 1
        pair = block * pair_count + (pair >> 1)
        return jnp.where(upper, NM - 1 - pair, pair), is_sine

    def angles(rows, spacing):
        order, _ = orders(rows)
        column = lax.broadcasted_iota(jnp.int32, (rows, width), 0) * spacing
        phase = (order * column % NLON).astype(jnp.float32) * (2.0 * math.pi / NLON)
        return jnp.cos(phase), jnp.sin(phase)

    fine_cos, fine_sin = angles(fine_total, 1)
    coarse_cos, coarse_sin = angles(coarse_total, fine_total)
    _, is_sine = orders(fine_total)
    for tile in range(quarter // fine_total):
        left, right = coarse_cos[tile : tile + 1], coarse_sin[tile : tile + 1]
        cosine = left * fine_cos - right * fine_sin
        sine = right * fine_cos + left * fine_sin
        out_ref[pl.ds(tile * fine_total, fine_total), :] = jnp.where(
            is_sine, sine, cosine
        ).astype(jnp.bfloat16)


def trig_table(pair_count, lon_count):
    pair_pad = pad_to(pair_count, SUBS)
    quarter = NLON // 4
    fine_total = 40
    return pl.pallas_call(
        functools.partial(
            trig_kernel, pair_count=pair_count, pair_pad=pair_pad, quarter=quarter,
            fine_total=fine_total,
        ),
        grid=(lon_count,),
        out_shape=jax.ShapeDtypeStruct((lon_count, quarter, 4 * pair_pad), jnp.bfloat16),
        out_specs=pl.BlockSpec((None, quarter, 4 * pair_pad), lambda b: (b, 0, 0)),
        compiler_params=pltpu.CompilerParams(vmem_limit_bytes=12 * MIB),
        cost_estimate=pl.CostEstimate(
            flops=24 * lon_count * quarter * pair_pad,
            bytes_accessed=lon_count * quarter * 8 * pair_pad,
            transcendentals=0,
        ),
        name="trig_table",
    )()


def grid_kernel(lon_ref, trig_ref, coeff_ref, *refs, lon_count, pair_count):
    token_ref, flat_ref, right_ref = refs[lon_count:]
    token_ref[...] = jnp.zeros_like(token_ref)
    share = coeff_ref.shape[1]
    width = coeff_ref.shape[2]
    rows = coeff_ref.shape[0] // lon_count * share
    values = coeff_ref[...].reshape(rows // share, lon_count, share, width)
    line = lax.broadcasted_iota(jnp.int32, (width, rows), 0)
    upper = line >= width // 2
    pair = jnp.where(upper, line - width // 2, line)
    is_sine = (pair & 1) == 1
    for block in range(lon_count):
        flat = values[:, block].reshape(rows, width).T
        swapped = jnp.where(is_sine, -pltpu.roll(flat, 1, 0), pltpu.roll(flat, width - 1, 0))
        order = block * pair_count + (pair >> 1)
        order = jnp.where(upper, NM - 1 - order, order) & 3
        odd = (order & 1) == 1
        flip = jnp.where(odd, -flat, flat)
        turned = jnp.where(order == 1, swapped, jnp.where(order == 3, -swapped, flat))
        turned = jnp.where(order == 2, -flat, turned)
        back = jnp.where(odd, -turned, turned)
        for turn, part in enumerate((flat, turned, flip, back)):
            right_ref[pl.ds(block * width, width), pl.ds(turn * rows, rows)] = part.astype(
                jnp.bfloat16
            )
    total = None
    for block in range(lon_count):
        part = jnp.dot(
            trig_ref[block],
            right_ref[pl.ds(block * width, width), :],
            preferred_element_type=jnp.float32,
        )
        total = part if total is None else total + part
    quarter = total.shape[0]
    for turn in range(4):
        flat_ref[pl.ds(turn * quarter, quarter), :] = total[:, turn * rows : (turn + 1) * rows]
    cols = NLON // lon_count
    for part in range(lon_count):
        refs[part][...] = flat_ref[pl.ds((lon_ref[0] ^ part) * cols, cols), :]


def grid_field(lon, trig, coeffs, pair_count):
    lon_count, quarter, width = trig.shape
    rows = coeffs.shape[0] // lon_count * coeffs.shape[1]
    return pl.pallas_call(
        functools.partial(grid_kernel, lon_count=lon_count, pair_count=pair_count),
        out_shape=[jax.ShapeDtypeStruct((NLON // lon_count, rows), jnp.float32)] * lon_count
        + [jax.ShapeDtypeStruct((SUBS, LANES), jnp.float32)],
        in_specs=[pl.BlockSpec(memory_space=pltpu.SMEM)]
        + [pl.BlockSpec(memory_space=pltpu.VMEM)] * 2,
        out_specs=[pl.BlockSpec(memory_space=pltpu.VMEM)] * (lon_count + 1),
        scratch_shapes=[
            pltpu.VMEM((4 * quarter, rows), jnp.float32),
            pltpu.VMEM((lon_count * width, 4 * rows), jnp.bfloat16),
        ],
        compiler_params=pltpu.CompilerParams(vmem_limit_bytes=16 * MIB),
        cost_estimate=pl.CostEstimate(
            flops=2 * NLON * lon_count * width * rows,
            bytes_accessed=trig.size * 2 + 2 * coeffs.size * 4,
            transcendentals=0,
        ),
        name="grid_field",
    )(lon, trig, coeffs)


def gelu_parts(preact):
    scale = math.sqrt(2.0 / math.pi)
    square = preact * preact
    bend = jnp.tanh(scale * (preact + 0.044715 * (square * preact)))
    half = 0.5 * (1.0 + bend)
    slope = half + (0.5 * preact) * (1.0 - bend * bend) * (
        scale * (1.0 + (3.0 * 0.044715) * square)
    )
    return preact * half, slope


def forward_kernel(latents_ref, w_ref, b_ref, _, slope_ref, hidden_t_ref, latents_t_ref):
    latents = latents_ref[...]
    preact = jnp.dot(latents, w_ref[...], preferred_element_type=jnp.float32) + b_ref[...]
    hidden, slope = gelu_parts(preact)
    slope_ref[...] = slope
    hidden_t_ref[...] = hidden.astype(jnp.bfloat16).T
    latents_t_ref[...] = latents.T


def forward(latents, w_hidden, b_hidden, after, parts):
    cells, width = latents.shape
    cols = cells // parts
    return pl.pallas_call(
        forward_kernel,
        grid=(parts,),
        out_shape=(
            jax.ShapeDtypeStruct((cells, width), jnp.float32),
            jax.ShapeDtypeStruct((parts, width, cols), jnp.bfloat16),
            jax.ShapeDtypeStruct((parts, width, cols), jnp.bfloat16),
        ),
        in_specs=[
            pl.BlockSpec((cols, width), lambda i: (i, 0)),
            pl.BlockSpec((width, width), lambda i: (0, 0)),
            pl.BlockSpec((1, width), lambda i: (0, 0)),
            pl.BlockSpec((SUBS, LANES), lambda i: (0, 0)),
        ],
        out_specs=(
            pl.BlockSpec((cols, width), lambda i: (i, 0)),
            pl.BlockSpec((None, width, cols), lambda i: (i, 0, 0)),
            pl.BlockSpec((None, width, cols), lambda i: (i, 0, 0)),
        ),
        compiler_params=pltpu.CompilerParams(vmem_limit_bytes=32 * MIB),
        cost_estimate=pl.CostEstimate(
            flops=2 * cells * width * width,
            bytes_accessed=cells * width * 10,
            transcendentals=cells * width,
        ),
        name="forward",
    )(latents, w_hidden, b_hidden.reshape(1, width), after)


def backward_kernel(
    core_ref, scale_ref, place_ref, w_out_ref, slope_ref, hidden_t_ref, latents_t_ref, *refs,
    blocks,
):
    grid_refs = refs[:blocks]
    preact_ref, keep_ref, send_ref = refs[blocks : blocks + 3]
    field_ref, hidden_acc, out_acc, bias_acc, sums_ref = refs[blocks + 3 :]
    index = pl.program_id(0)
    total = pl.num_programs(0)
    lon_cols = grid_refs[0].shape[0]
    width = hidden_acc.shape[0]
    cols = slope_ref.shape[0]
    sum_rows = sums_ref.shape[0]

    @pl.when(index == 0)
    def _():
        field = None
        for block in range(blocks):
            scaled = (grid_refs[block][...] * scale_ref[block]).astype(jnp.bfloat16)
            part = jnp.dot(scaled, place_ref[block], preferred_element_type=jnp.float32)
            field = part if field is None else field + part
        for row in range(field.shape[1] // LANES):
            field_ref[pl.ds(row * lon_cols, lon_cols), :] = field[
                :, row * LANES : (row + 1) * LANES
            ]
        hidden_acc[...] = jnp.zeros_like(hidden_acc)
        out_acc[...] = jnp.zeros_like(out_acc)
        bias_acc[...] = jnp.zeros_like(bias_acc)

    field = field_ref[pl.ds(pl.multiple_of(index * cols, SUBS), cols), :].astype(jnp.bfloat16)
    back = jnp.dot(field[:, :F], w_out_ref[...], preferred_element_type=jnp.float32)
    preact_back = (back * slope_ref[...]).astype(jnp.bfloat16)
    preact_ref[...] = preact_back
    hidden_acc[...] += jnp.dot(
        latents_t_ref[...], preact_back, preferred_element_type=jnp.float32
    )
    out_acc[...] += jnp.dot(hidden_t_ref[...], field, preferred_element_type=jnp.float32)
    bias_acc[...] += jnp.sum(preact_back.astype(jnp.float32), axis=0, keepdims=True)

    @pl.when(index == total - 1)
    def _():
        tiles = width // LANES
        for row_tile in range(width // SUBS):
            for tile in range(tiles):
                sums_ref[pl.ds((row_tile * tiles + tile) * SUBS, SUBS), :] = hidden_acc[
                    pl.ds(row_tile * SUBS, SUBS), pl.ds(tile * LANES, LANES)
                ]
        base = width * tiles
        flipped = out_acc[...].T
        for tile in range(tiles):
            sums_ref[pl.ds(base + tile * F, F), :] = flipped[:F, tile * LANES : (tile + 1) * LANES]
        base = base + tiles * F
        sums_ref[pl.ds(base, sum_rows - base), :] = jnp.zeros((sum_rows - base, LANES), jnp.float32)
        for tile in range(tiles):
            sums_ref[pl.ds(base + tile, 1), :] = bias_acc[:, tile * LANES : (tile + 1) * LANES]
        half = sum_rows // 2
        mine = core_ref[0]
        keep_ref[...] = sums_ref[pl.ds(pl.multiple_of(mine * half, SUBS), half), :]
        send_ref[...] = sums_ref[pl.ds(pl.multiple_of((1 - mine) * half, SUBS), half), :]


def backward(core, grids, scale, place, w_out_t, slope, hidden_t, latents_t, sum_rows):
    cells, width = slope.shape
    blocks = len(grids)
    parts, _, cols = hidden_t.shape
    half = (sum_rows // 2, LANES)
    whole3 = lambda i: (0, 0, 0)
    whole2 = lambda i: (0, 0)
    return pl.pallas_call(
        functools.partial(backward_kernel, blocks=blocks),
        grid=(parts,),
        out_shape=(
            jax.ShapeDtypeStruct((cells, width), jnp.bfloat16),
            jax.ShapeDtypeStruct(half, jnp.float32),
            jax.ShapeDtypeStruct(half, jnp.float32),
        ),
        in_specs=[
            pl.BlockSpec(memory_space=pltpu.SMEM),
            pl.BlockSpec(scale.shape, whole3),
            pl.BlockSpec(place.shape, whole3),
            pl.BlockSpec(w_out_t.shape, whole2),
            pl.BlockSpec((cols, width), lambda i: (i, 0)),
            pl.BlockSpec((None, width, cols), lambda i: (i, 0, 0)),
            pl.BlockSpec((None, width, cols), lambda i: (i, 0, 0)),
        ]
        + [pl.BlockSpec(grids[0].shape, whole2)] * blocks,
        out_specs=(
            pl.BlockSpec((cols, width), lambda i: (i, 0)),
            pl.BlockSpec(half, whole2),
            pl.BlockSpec(half, whole2),
        ),
        scratch_shapes=[
            pltpu.VMEM((cells, LANES), jnp.float32),
            pltpu.VMEM((width, width), jnp.float32),
            pltpu.VMEM((width, LANES), jnp.float32),
            pltpu.VMEM((1, width), jnp.float32),
            pltpu.VMEM((sum_rows, LANES), jnp.float32),
        ],
        compiler_params=pltpu.CompilerParams(vmem_limit_bytes=32 * MIB),
        cost_estimate=pl.CostEstimate(
            flops=2 * cells * width * (width + 2 * LANES),
            bytes_accessed=cells * width * 10,
            transcendentals=0,
        ),
        name="backward",
    )(core, scale, place, w_out_t, slope, hidden_t, latents_t, *grids)


def add_kernel(index_ref, *refs, inputs, outputs, factor):
    size = refs[0].shape[0] // outputs
    for part in range(outputs):
        start = 0 if outputs == 1 else pl.multiple_of((index_ref[0] ^ part) * size, SUBS)
        total = refs[0][pl.ds(start, size), :]
        for piece in refs[1:inputs]:
            total = total + piece[pl.ds(start, size), :]
        if factor is not None:
            total = total * factor
        refs[inputs + part][...] = total


def add_pieces(index, pieces, outputs, factor=None):
    rows = pieces[0].shape[0]
    size = rows // outputs
    return pl.pallas_call(
        functools.partial(add_kernel, inputs=len(pieces), outputs=outputs, factor=factor),
        out_shape=[jax.ShapeDtypeStruct((size, LANES), jnp.float32)] * outputs,
        in_specs=[pl.BlockSpec(memory_space=pltpu.SMEM)]
        + [pl.BlockSpec(memory_space=pltpu.VMEM)] * len(pieces),
        out_specs=[pl.BlockSpec(memory_space=pltpu.VMEM)] * outputs,
        cost_estimate=pl.CostEstimate(
            flops=len(pieces) * rows * LANES,
            bytes_accessed=4 * (len(pieces) + 1) * rows * LANES,
            transcendentals=0,
        ),
        compiler_params=pltpu.CompilerParams(vmem_limit_bytes=6 * MIB),
        name="add_pieces",
    )(index, *pieces)


def finish_kernel(place_ref, *refs, lon_count, depth):
    hidden_ref, bias_ref, out_ref, flat_ref = refs[2 * lon_count :]
    core, lon, deep = place_ref[0], place_ref[1], place_ref[2]
    size = refs[0].shape[0] // depth
    for half in range(2):
        for part in range(lon_count):
            for piece in range(depth):
                start = (((core ^ half) * lon_count + (lon ^ part)) * depth + (deep ^ piece)) * size
                flat_ref[pl.ds(pl.multiple_of(start, SUBS), size), :] = refs[
                    half * lon_count + part
                ][pl.ds(piece * size, size), :]
    width = hidden_ref.shape[0]
    tiles = width // LANES
    for row_tile in range(width // SUBS):
        for tile in range(tiles):
            hidden_ref[pl.ds(row_tile * SUBS, SUBS), pl.ds(tile * LANES, LANES)] = flat_ref[
                pl.ds((row_tile * tiles + tile) * SUBS, SUBS), :
            ]
    base = width * tiles
    for tile in range(tiles):
        out_ref[:, pl.ds(tile * LANES, LANES)] = flat_ref[pl.ds(base + tile * F, F), :]
        bias_ref[:, pl.ds(tile * LANES, LANES)] = flat_ref[pl.ds(base + tiles * F + tile, 1), :]


def finish(place, pieces, width, depth):
    lon_count = len(pieces) // 2
    return pl.pallas_call(
        functools.partial(finish_kernel, lon_count=lon_count, depth=depth),
        out_shape=(
            jax.ShapeDtypeStruct((width, width), jnp.float32),
            jax.ShapeDtypeStruct((1, width), jnp.float32),
            jax.ShapeDtypeStruct((F, width), jnp.float32),
        ),
        in_specs=[pl.BlockSpec(memory_space=pltpu.SMEM)]
        + [pl.BlockSpec(memory_space=pltpu.VMEM)] * len(pieces),
        out_specs=(pl.BlockSpec(memory_space=pltpu.VMEM),) * 3,
        scratch_shapes=[pltpu.VMEM((len(pieces) * pieces[0].shape[0], LANES), jnp.float32)],
        compiler_params=pltpu.CompilerParams(vmem_limit_bytes=8 * MIB),
        name="finish",
    )(place, *pieces)


def swap(value, axis, bits):
    count = lax.axis_size(axis)
    return lax.ppermute(value, axis, [(i, i ^ bits) for i in range(count)])


def local(spectra, field_slot, field_weight, latents, w_hidden, b_hidden, w_out):
    slot_count, _, pair_count, _ = spectra.shape
    lat_rows, lon_cols, width = latents.shape
    lat_count = lax.axis_size("lat")
    lon_count = lax.axis_size("lon")
    rows_all = lat_rows * lat_count
    lat_index = lax.axis_index("lat").astype(jnp.int32)
    lon_index = lax.axis_index("lon").astype(jnp.int32)
    pair_pad = pad_to(pair_count, SUBS)
    cells = lat_rows * lon_cols
    parts = 4

    coeffs = coefficients(spectra, (lon_index * pair_count).reshape(1), rows_all, lat_rows)
    share = slot_count * lat_rows // lon_count
    coeffs = coeffs.reshape(lat_count * lon_count, share, 4 * pair_pad)
    coeffs = lax.all_to_all(coeffs, ("lat", "lon"), split_axis=0, concat_axis=0, tiled=True)

    trig = trig_table(pair_count, lon_count)

    lanes = lat_count * share

    def spread(values):
        values = jnp.broadcast_to(values, (lat_count, slot_count, lat_rows))
        values = values.reshape(lat_count, lon_count, share)
        values = jnp.transpose(values, (1, 0, 2)).reshape(lon_count, lanes)
        arrival = lon_index ^ jnp.arange(lon_count, dtype=jnp.int32)
        chosen = arrival[:, None] == jnp.arange(lon_count, dtype=jnp.int32)
        return jnp.sum(jnp.where(chosen[:, :, None], values[None], 0), axis=1)

    field_ids = spread(field_slot.reshape(lat_count, slot_count, 1))
    row_ids = spread(jnp.arange(lat_rows, dtype=jnp.int32).reshape(1, 1, lat_rows))
    chosen = field_ids[:, :, None] == jnp.arange(F, dtype=jnp.int32)
    weight = jnp.sum(jnp.where(chosen, field_weight, 0.0), axis=2)
    sine = jnp.sin(band_angles(lat_index * lat_rows + row_ids, rows_all))
    scale = (sine * weight)[:, None, :]
    target = row_ids * LANES + field_ids
    place = (
        target[:, :, None] == jnp.arange(lat_rows * LANES, dtype=jnp.int32)[None, None, :]
    ).astype(jnp.bfloat16)
    w_out_t = w_out.T

    core_index, deep_index = lat_index & 1, lat_index >> 1
    depth = lat_count // 2
    spots = jnp.stack([core_index, lon_index, deep_index])
    *grids, token = grid_field(lon_index.reshape(1), trig, coeffs, pair_count)
    slope, hidden_t, latents_t = forward(
        latents.reshape(cells, width), w_hidden, b_hidden, token, parts
    )
    grids = [grids[0]] + [swap(grids[part], "lon", part) for part in range(1, lon_count)]

    device_count = lat_count * lon_count
    used_rows = (width + F + 1) * width // LANES
    chunk = pad_to(pad_to(used_rows, device_count) // device_count, SUBS)
    preact_back, keep, send = backward(
        core_index.reshape(1), grids, scale, place, w_out_t, slope, hidden_t, latents_t,
        chunk * device_count,
    )
    pieces = add_pieces(
        lon_index.reshape(1), [keep, swap(send, "lat", 1)], lon_count
    )
    arrived = [swap(pieces[part], "lon", part) for part in range(1, lon_count)]
    latent_grad = lax.dot_general(
        preact_back, w_hidden, (((1,), (1,)), ((), ())), preferred_element_type=jnp.float32
    ).astype(jnp.bfloat16)
    arrived, latent_grad = lax.optimization_barrier((arrived, latent_grad))
    pieces = add_pieces(deep_index.reshape(1), [pieces[0]] + arrived, depth)
    arrived = [swap(pieces[part], "lat", 2 * part) for part in range(1, depth)]
    norm = 1.0 / math.sqrt(rows_all * NLON)
    total = add_pieces(deep_index.reshape(1), [pieces[0]] + arrived, 1, norm)[0]
    total = jnp.concatenate([total] + [swap(total, "lat", 2 * part) for part in range(1, depth)])
    totals = [total] + [swap(total, "lon", part) for part in range(1, lon_count)]
    totals = totals + [swap(piece, "lat", 1) for piece in totals]
    hidden_grad, bias_grad, out_grad = finish(spots, totals, width, depth)
    return (
        latent_grad.reshape(lat_rows, lon_cols, width),
        hidden_grad,
        bias_grad.reshape(width),
        out_grad.T,
    )


def solution(mesh):
    in_specs = (P("lat", None, "lon", None), P(), P(), P("lat", "lon", None), P(), P(), P())
    out_specs = (P("lat", "lon", None), P(), P(), P())
    return jax.shard_map(local, mesh=mesh, in_specs=in_specs, out_specs=out_specs, check_vma=False)
```
